32 devices in a mesh: dp: 4 (over y, x), tp: 8 (over z, core).
Axes of the slice: x: 2, y: 2, z: 4, core: 2. Of those that a mesh axis runs over, the one named last changes fastest.
Arguments:
- hidden: bfloat16 [768, 2880], P(('dp', 'tp')), parts along dimension 0, may hold values from -6 to 6
- attn_gain: float32 [2880], replicated, may hold values from 0.1 to 1.9
- w_query: bfloat16 [2880, 4096], P(None, 'tp'), may hold values from -0.109375 to 0.109375
- w_keyval: bfloat16 [2880, 1024], P(None, 'tp'), may hold values from -0.109375 to 0.109375
- w_out: bfloat16 [4096, 2880], P('tp'), may hold values from -0.09375 to 0.09375
- cache_keys: bfloat16 [32, 2048, 512], P(('dp', 'tp')), parts along dimension 0, may hold values from -70 to 70
- cache_values: bfloat16 [32, 2048, 512], P(('dp', 'tp')), parts along dimension 0, may hold values from -6 to 6
- cache_lens: int32 [32], P(('dp', 'tp')), parts along dimension 0, may hold values from 256 to 2048, as said below
- parents: int32 [32, 24], P(('dp', 'tp')), parts along dimension 0, may hold values from 0 to 23, as said below
- accepted: int32 [32], P(('dp', 'tp')), parts along dimension 0, may hold values from 0 to 23, as said below
- moe_gain: float32 [2880], replicated, may hold values from 0.1 to 1.9
- w_router: bfloat16 [2880, 32], replicated, may hold values from -0.109375 to 0.109375
- routes: int32 [768, 4], P('dp'), parts along dimension 0, may hold values from 0 to 31, all different within a row; in each aligned block of 192 rows (0 to 191, 192 to 383, ...) at most 48 rows name the same one
- w_gate: bfloat16 [11520, 2880], P('tp'), may hold values from -0.109375 to 0.109375
- w_up: bfloat16 [11520, 2880], P('tp'), may hold values from -0.109375 to 0.109375
- w_down: bfloat16 [11520, 2880], P('tp'), may hold values from -0.109375 to 0.109375
Outputs:
- layer_out: bfloat16 [768, 2880], P(('dp', 'tp')), parts along dimension 0
- accepted_kv: bfloat16 [32, 8, 1024], P(('dp', 'tp')), parts along dimension 0
The draws below stay inside these ranges and needn't reach their ends.
There are 4 independent parts, one for each index of `dp`. The reference program is written for one: setup_inputs(seed, part) draws one part's arguments, and reference() takes and returns one part's arrays. A program takes and returns all parts, laid end to end along the dimension named above; an argument that names none is the same for every part. Nothing has to cross between parts.
Inputs may be any that keep to these rules, and one draw needn't show every extreme that they name: `cache_lens`: 2048 for at least one request of every part. `parents`: node 0 names itself; every other node names a node of smaller index; no path from node 0 holds more than 8 nodes, and every tree has one of exactly 8. The path from node 0 to the accepted node holds at most 8 nodes, exactly 8 for at least one request of every part. `routes`: each token names 4 different experts; at most 48 tokens of a part name any one expert, a bound that some block reaches.
All inputs are finite; a program needn't handle non-finite values.
Results may differ from the reference program's by a relative error of at most 0.012.
The reference program's roundings to bfloat16 on the way count: a program that leaves them out, or rounds other values in their place, can miss the bound.
Values may be sent and summed in bfloat16 or wider, within the bound.
No kernel may reach another device: no remote copies, remote signals or barrier semaphores. Data moves between devices by JAX's collectives and lax.ppermute only.
A program may use at most 128 MiB of HBM per device.

```python
import math
import jax
import jax.numpy as jnp
import numpy as np
from jax import lax

D = 2880
HEADS = 64
KV_HEADS = 8
HEAD_DIM = 64
EXPERTS = 32
EXPERT_HID = 2880
TOP = 4
EXP_WIN = 4
DRAFT = 24
DEPTH = 8
CACHE = 2048
REQS = 8
TOKENS = 192
CAP = 48


def draw_cache_keys(key, part):
    shape = (REQS, CACHE, KV_HEADS * HEAD_DIM)
    base = jax.random.normal(key, shape, jnp.float32)
    return jnp.clip(base, -6.0, 6.0).astype(jnp.bfloat16)


def draw_cache_lens(key, part):
    lengths = jax.random.randint(key, (REQS,), CACHE // 8, CACHE + 1)
    longest = jax.random.randint(jax.random.fold_in(key, 3), (), 0, REQS)
    return jnp.where(jnp.arange(REQS) == longest, CACHE, lengths).astype(jnp.int32)


def draw_parents(key, part):
    parent_cols = [jnp.zeros((REQS,), jnp.int32)]
    depth_cols = [jnp.zeros((REQS,), jnp.int32)]
    for node in range(1, DRAFT):
        so_far = jnp.stack(depth_cols, axis=1)
        if node < DEPTH:
            picked = jnp.full((REQS,), node - 1, jnp.int32)
        else:
            scores = jax.random.randint(jax.random.fold_in(key, node), (REQS, node), 0, 4096) * node + jnp.arange(node)
            eligible = so_far < DEPTH - 1
            picked = jnp.argmax(jnp.where(eligible, scores, -1), axis=1).astype(jnp.int32)
        depth_new = jnp.take_along_axis(so_far, picked[:, None], axis=1)[:, 0] + 1
        parent_cols.append(picked)
        depth_cols.append(depth_new.astype(jnp.int32))
    return jnp.stack(parent_cols, axis=1).astype(jnp.int32)


def draw_accepted(key, part):
    leaves = jax.random.randint(key, (REQS,), 0, DRAFT)
    deepest = jax.random.randint(jax.random.fold_in(key, 5), (), 0, REQS)
    return jnp.where(jnp.arange(REQS) == deepest, DEPTH - 1, leaves).astype(jnp.int32)


def levels(key, extent, split, low, largest):
    level = 1.0
    for dim, parts in split:
        steps = jax.random.uniform(jax.random.fold_in(jax.random.fold_in(key, 6), dim), (parts,), jnp.float32, low / len(split), largest / len(split))
        level = level * jnp.repeat(jnp.exp(steps), extent[dim] // parts).reshape((-1,) + (1,) * (len(extent) - 1 - dim))
    return level


def assign_block(stream_key, own, number, rows, number_of, top, bound, slope):
    ranking = jax.random.permutation(stream_key, number_of)
    crowded, common = load_shares(number_of, rows * top, bound, slope, True), load_shares(number_of, rows * top, bound, slope, False)
    places = jnp.arange(number_of)

    def named(sizes, offset_by):
        used = int((sizes > 0).sum())
        fixed = max(1, used // 4)
        passed = fixed + (places - fixed + offset_by * (used - fixed)) % max(1, number_of - fixed)
        return jnp.zeros((number_of,), jnp.int32).at[ranking[jnp.where(places < fixed, places, passed)]].set(jnp.asarray(sizes, jnp.int32))

    sizes = jnp.where(number % 4 == 0, named(crowded, number // 4), named(common, number - number // 4 - 1))
    mixed = jax.random.permutation(jax.random.fold_in(own, 3), number_of)
    donor, receiver = mixed[0:number_of // 2 * 2:2], mixed[1:number_of // 2 * 2:2]
    room = jnp.minimum(sizes[donor] - 1, bound - sizes[receiver]) // 2
    room = jnp.where((donor == ranking[0]) | (receiver == ranking[0]) | (sizes[receiver] == 0), 0, jnp.maximum(room, 0))
    passed = jax.random.randint(jax.random.fold_in(own, 4), (number_of // 2,), 0, 1 << 20) % (room + 1)
    sizes = sizes.at[donor].add(-passed).at[receiver].add(passed)
    items = jnp.searchsorted(jnp.cumsum(sizes), jnp.arange(rows * top), side="right").astype(jnp.int32)
    table = items.reshape(top, rows).T
    table = table[jax.random.permutation(jax.random.fold_in(own, 1), rows)]
    offset_by = jax.random.randint(jax.random.fold_in(own, 2), (rows, 1), 0, top)
    return jnp.take_along_axis(table, (jnp.arange(top)[None, :] + offset_by) % top, axis=1)


def load_shares(count, total, most, slope, full):
    portions = [(1 << 20) // math.isqrt(grade ** slope) + 1 for grade in range(1, count + 1)]
    largest = most if full else min(most, max(-(-total // count), total * portions[0] // sum(portions)))
    least = 1 if total - largest >= count - 1 else 0
    holding, spare = [largest] + [least] * (count - 1), total - largest - least * (count - 1)
    while spare > 0:
        candidates = [i for i in range(1, count) if holding[i] < largest] or [i for i in range(1, count) if holding[i] < most]
        whole, budget = sum([portions[i] for i in candidates]), spare
        for i in candidates:
            more = min(most - holding[i], max(1, budget * portions[i] // whole), spare)
            holding[i] = holding[i] + more
            spare = spare - more
    return np.array(holding)


def gaussian(stream_key, extent, spread, limit, shards=(), kind=jnp.bfloat16):
    factor_of = levels(stream_key, extent, shards, -0.22, 0.18) if shards else 1.0
    entries = jax.random.normal(stream_key, extent, jnp.float32) * spread * factor_of
    return jnp.minimum(jnp.maximum(entries, -limit), limit).astype(kind)


def setup_inputs(seed: int = 0, part: int = 0) -> dict:
    keys = jax.random.split(jax.random.key(seed), 17)
    part_keys = jax.random.split(jax.random.fold_in(keys[16], part), 17)
    hidden = gaussian(part_keys[0], (TOKENS, D), 1.0, 6.0, ((0, 8),))
    attn_gain = jnp.clip(1.0 + 0.18 * jax.random.normal(keys[1], (D,), jnp.float32), 0.1, 1.9)
    w_query = gaussian(keys[2], (D, HEADS * HEAD_DIM), D ** -0.5, 0.109375, ((1, 8),))
    w_keyval = gaussian(keys[3], (D, 2 * KV_HEADS * HEAD_DIM), D ** -0.5, 0.109375, ((1, 8),))
    w_out = gaussian(keys[4], (HEADS * HEAD_DIM, D), (HEADS * HEAD_DIM) ** -0.5, 0.09375, ((0, 8),))
    cache_keys = draw_cache_keys(jax.random.fold_in(jax.random.fold_in(keys[16], part), 71), part)
    cache_values = gaussian(part_keys[6], (REQS, CACHE, KV_HEADS * HEAD_DIM), 1.0, 6.0, ((0, 8),))
    cache_lens = draw_cache_lens(jax.random.fold_in(jax.random.fold_in(keys[16], part), 71), part)
    parents = draw_parents(jax.random.fold_in(jax.random.fold_in(keys[16], part), 71), part)
    accepted = draw_accepted(jax.random.fold_in(jax.random.fold_in(keys[16], part), 71), part)
    moe_gain = jnp.clip(1.0 + 0.18 * jax.random.normal(keys[10], (D,), jnp.float32), 0.1, 1.9)
    w_router = gaussian(keys[11], (D, EXPERTS), D ** -0.5, 0.109375)
    routes_keys = jax.random.split(jax.random.fold_in(part_keys[12], 1), TOKENS // TOKENS)
    routes_turns = jax.random.permutation(jax.random.fold_in(part_keys[12], 3), TOKENS // TOKENS)
    routes = jax.vmap(lambda own, number: assign_block(jax.random.fold_in(part_keys[12], 2), own, number, TOKENS, EXPERTS, TOP, CAP, 2))(routes_keys, routes_turns).reshape((TOKENS, TOP))
    w_gate = gaussian(keys[13], (EXP_WIN * EXPERT_HID, D), D ** -0.5, 0.109375, ((0, 8),))
    w_up = gaussian(keys[14], (EXP_WIN * EXPERT_HID, D), D ** -0.5, 0.109375, ((0, 8),))
    w_down = gaussian(keys[15], (EXP_WIN * EXPERT_HID, D), EXPERT_HID ** -0.5, 0.109375, ((0, 8),))
    return {"hidden": hidden, "attn_gain": attn_gain, "w_query": w_query, "w_keyval": w_keyval, "w_out": w_out, "cache_keys": cache_keys, "cache_values": cache_values, "cache_lens": cache_lens, "parents": parents, "accepted": accepted, "moe_gain": moe_gain, "w_router": w_router, "routes": routes, "w_gate": w_gate, "w_up": w_up, "w_down": w_down}


THETA = 150000.0
SWIGLU_ALPHA = 1.702
EPSILON = 1e-05

def rms_norm(values, gain):
    floats = values.astype(jnp.float32)
    mean_sq = lax.optimization_barrier(jnp.mean(floats * floats, axis=-1, keepdims=True))
    return (floats * lax.rsqrt(mean_sq + EPSILON) * gain).astype(jnp.bfloat16)

def tree_paths(parent_row, depth_limit):
    count = parent_row.shape[0]
    identity = jnp.eye(count, dtype=jnp.bool_)
    ancestry = identity
    for level in range(depth_limit):
        ancestry = identity | jnp.take(ancestry, parent_row, axis=0)
    depths = lax.optimization_barrier(jnp.sum(ancestry.astype(jnp.int32), axis=1)) - 1
    return (ancestry, depths)

def rotate(values, positions):
    half = values.shape[-1] // 2
    steps_f = jnp.arange(half).astype(jnp.float32)
    inverse = jnp.exp(steps_f * (-2.0 * math.log(THETA) / values.shape[-1]))
    angles = positions[:, None] * inverse[None, :]
    cosine = jnp.cos(angles)[:, None, :]
    sine = jnp.sin(angles)[:, None, :]
    first = values[..., :half].astype(jnp.float32)
    second = values[..., half:].astype(jnp.float32)
    turned = jnp.concatenate([first * cosine - second * sine, second * cosine + first * sine], axis=-1)
    return turned.astype(jnp.bfloat16)

def rounded_float(values):
    return lax.optimization_barrier(values.astype(jnp.bfloat16)).astype(jnp.float32)

def attend_request(query, keyval, keys_cache, values_cache, length, parent_row, leaf, depth_limit):
    draft, heads, head_dim = query.shape
    kv_width = keyval.shape[1] // 2
    kv_heads = kv_width // head_dim
    ancestry, depths = tree_paths(parent_row, depth_limit)
    positions = (length + depths).astype(jnp.float32)
    query_rot = rotate(query, positions)
    new_keys = rotate(keyval[:, :kv_width].reshape(draft, kv_heads, head_dim), positions)
    new_values = keyval[:, kv_width:].reshape(draft, kv_heads, head_dim)
    grouped = query_rot.reshape(draft, kv_heads, heads // kv_heads, head_dim).astype(jnp.float32)
    scale = 1.0 / math.sqrt(head_dim)
    draft_scores = jnp.einsum('jgqd,kgd->gqjk', grouped, new_keys.astype(jnp.float32)) * scale
    draft_scores = jnp.where(ancestry[None, None], draft_scores, -jnp.inf)
    slots = keys_cache.shape[0]
    cache_k = keys_cache.reshape(slots, kv_heads, head_dim).astype(jnp.float32)
    cache_v = values_cache.reshape(slots, kv_heads, head_dim).astype(jnp.float32)
    cache_scores = jnp.einsum('jgqd,pgd->gqjp', grouped, cache_k) * scale
    live = jnp.arange(slots) < length
    cache_scores = jnp.where(live[None, None, None], cache_scores, -jnp.inf)
    top = jnp.maximum(lax.optimization_barrier(jnp.max(draft_scores, axis=-1)), lax.optimization_barrier(jnp.max(cache_scores, axis=-1)))
    draft_exp = jnp.exp(draft_scores - top[..., None])
    cache_exp = jnp.exp(cache_scores - top[..., None])
    total = lax.optimization_barrier(jnp.sum(draft_exp, axis=-1)) + lax.optimization_barrier(jnp.sum(cache_exp, axis=-1))
    weighted = jnp.einsum('gqjk,kgd->jgqd', rounded_float(draft_exp), new_values.astype(jnp.float32))
    weighted = weighted + jnp.einsum('gqjp,pgd->jgqd', rounded_float(cache_exp), cache_v)
    output = (weighted / jnp.transpose(total, (2, 0, 1))[..., None]).astype(jnp.bfloat16).reshape(draft, heads * head_dim)
    selector = ancestry[leaf][None, :] & (depths[None, :] == jnp.arange(depth_limit)[:, None])
    new_rows = jnp.concatenate([new_keys.reshape(draft, kv_width), new_values.reshape(draft, kv_width)], axis=1)
    accepted_rows = jnp.dot(selector.astype(jnp.bfloat16), new_rows, preferred_element_type=jnp.float32).astype(jnp.bfloat16)
    return (output, accepted_rows)

def gate_weights(inputs, router, routes):
    logits = jnp.dot(inputs, router, preferred_element_type=jnp.float32)
    onehot = routes[:, :, None] == jnp.arange(router.shape[1])[None, None, :]
    picked = lax.optimization_barrier(jnp.sum(jnp.where(onehot, logits[:, None, :], 0.0), axis=2))
    return jax.nn.softmax(picked, axis=1).astype(jnp.bfloat16)

def expert_term(inputs, weights, routes, expert, gate_rows, up_rows, down_rows, capacity):
    count = inputs.shape[0]
    match = routes == expert
    hits = jnp.any(match, axis=1)
    gate_of = lax.optimization_barrier(jnp.sum(jnp.where(match, weights.astype(jnp.float32), 0.0), axis=1))
    slot_ids = jnp.cumsum(hits.astype(jnp.int32)) - 1
    target = jnp.where(hits, slot_ids, capacity).astype(jnp.int32)
    index = jnp.full((capacity,), count, jnp.int32).at[target].set(jnp.arange(count).astype(jnp.int32), mode='drop')
    valid = index < count
    safe = jnp.minimum(index, count - 1)
    picked = inputs[safe]
    gate_val = lax.dot_general(picked, gate_rows, (((1,), (1,)), ((), ())), preferred_element_type=jnp.float32)
    up_val = lax.dot_general(picked, up_rows, (((1,), (1,)), ((), ())), preferred_element_type=jnp.float32)
    active = (gate_val * jax.nn.sigmoid(SWIGLU_ALPHA * gate_val) * (up_val + 1.0)).astype(jnp.bfloat16)
    result = jnp.dot(active, down_rows, preferred_element_type=jnp.float32)
    scale_rows = jnp.where(valid, gate_of[safe], 0.0)
    empty = jnp.zeros((count, inputs.shape[1]), jnp.float32)
    return empty.at[index].add(result * scale_rows[:, None], mode='drop')

def reference(hidden, attn_gain, w_query, w_keyval, w_out, cache_keys, cache_values, cache_lens, parents, accepted, moe_gain, w_router, routes, w_gate, w_up, w_down):
    normed = rms_norm(hidden, attn_gain)
    query = jnp.dot(normed, w_query, preferred_element_type=jnp.float32).astype(jnp.bfloat16)
    keyval = jnp.dot(normed, w_keyval, preferred_element_type=jnp.float32).astype(jnp.bfloat16)
    query = query.reshape(REQS, DRAFT, HEADS, HEAD_DIM)
    keyval = keyval.reshape(REQS, DRAFT, 2 * KV_HEADS * HEAD_DIM)

    def per_request(items):
        return attend_request(*items, DEPTH)
    attended, accepted_kv = lax.map(per_request, (query, keyval, cache_keys, cache_values, cache_lens, parents, accepted))
    attended = attended.reshape(TOKENS, HEADS * HEAD_DIM)
    middle = (hidden.astype(jnp.float32) + jnp.dot(attended, w_out, preferred_element_type=jnp.float32)).astype(jnp.bfloat16)
    moe_in = rms_norm(middle, moe_gain)
    weights = gate_weights(moe_in, w_router, routes)
    summed = jnp.zeros((TOKENS, D), jnp.float32)
    for expert in range(EXP_WIN):
        first = expert * EXPERT_HID
        last = first + EXPERT_HID
        summed = summed + expert_term(moe_in, weights, routes, expert, w_gate[first:last], w_up[first:last], w_down[first:last], CAP)
    layer_out = (middle.astype(jnp.float32) + summed).astype(jnp.bfloat16)
    return (layer_out, accepted_kv)
```

```python
import math

import jax
import jax.numpy as jnp
from jax import lax
from jax.experimental import pallas as pl
from jax.experimental.pallas import tpu as pltpu
from jax.sharding import PartitionSpec as P

HEADS = 64
HEAD_DIM = 64
EXPERT_HID = 2880
DEPTH = 8


THETA = 150000.0
SWIGLU_ALPHA = 1.702
EPSILON = 1e-05


def rms_norm(values, gain):
    floats = values.astype(jnp.float32)
    mean_sq = jnp.mean(floats * floats, axis=-1, keepdims=True)
    return (floats * lax.rsqrt(mean_sq + EPSILON) * gain).astype(jnp.bfloat16)


def tree_paths(parent_row, depth_limit):
    count = parent_row.shape[0]
    identity = jnp.eye(count, dtype=jnp.bool_)
    ancestry = identity
    for level in range(depth_limit):
        ancestry = identity | jnp.take(ancestry, parent_row, axis=0)
    depths = jnp.sum(ancestry.astype(jnp.int32), axis=1) - 1
    return (ancestry, depths)


def rotate(values, positions):
    half = values.shape[-1] // 2
    steps_f = jnp.arange(half).astype(jnp.float32)
    inverse = jnp.exp(steps_f * (-2.0 * math.log(THETA) / values.shape[-1]))
    angles = positions[:, None] * inverse[None, :]
    cosine = jnp.cos(angles)[:, None, :]
    sine = jnp.sin(angles)[:, None, :]
    first = values[..., :half].astype(jnp.float32)
    second = values[..., half:].astype(jnp.float32)
    turned = jnp.concatenate(
        [first * cosine - second * sine, second * cosine + first * sine], axis=-1
    )
    return turned.astype(jnp.bfloat16)


def prepare(query, keyval, length, parent_row, depth_limit):
    draft, heads, head_dim = query.shape
    kv_width = keyval.shape[1] // 2
    kv_heads = kv_width // head_dim
    ancestry, depths = tree_paths(parent_row, depth_limit)
    positions = (length + depths).astype(jnp.float32)
    query_rot = rotate(query, positions)
    new_keys = rotate(keyval[:, :kv_width].reshape(draft, kv_heads, head_dim), positions)
    new_values = keyval[:, kv_width:].reshape(draft, kv_heads, head_dim)
    grouped = query_rot.reshape(draft, kv_heads, heads // kv_heads, head_dim)
    draft_scores = jnp.einsum(
        "jgqd,kgd->gqjk", grouped, new_keys, preferred_element_type=jnp.float32
    ) * (1.0 / math.sqrt(head_dim))
    draft_scores = jnp.where(ancestry[None, None], draft_scores, -jnp.inf)
    return (grouped, new_keys, new_values, ancestry, depths, draft_scores)


def accept_rows(new_keys, new_values, ancestry, depths, leaf, depth_limit):
    draft = depths.shape[0]
    selector = ancestry[leaf][None, :] & (depths[None, :] == jnp.arange(depth_limit)[:, None])
    new_rows = jnp.concatenate([new_keys.reshape(draft, -1), new_values.reshape(draft, -1)], axis=1)
    return jnp.dot(
        selector.astype(jnp.bfloat16), new_rows, preferred_element_type=jnp.float32
    ).astype(jnp.bfloat16)


def finish(weighted, total, draft):
    return (
        (weighted / jnp.transpose(total, (2, 0, 1))[..., None])
        .astype(jnp.bfloat16)
        .reshape(draft, -1)
    )


def attend_padded(query, keyval, keys_cache, values_cache, length, parent_row, leaf, depth_limit):
    draft, heads, head_dim = query.shape
    grouped, new_keys, new_values, ancestry, depths, draft_scores = prepare(
        query, keyval, length, parent_row, depth_limit
    )
    slots = keys_cache.shape[0]
    kv_heads = new_keys.shape[1]
    cache_k = keys_cache.reshape(slots, kv_heads, head_dim)
    cache_v = values_cache.reshape(slots, kv_heads, head_dim)
    cache_scores = jnp.einsum(
        "jgqd,pgd->gqjp", grouped, cache_k, preferred_element_type=jnp.float32
    ) * (1.0 / math.sqrt(head_dim))
    live = jnp.arange(slots) < length
    cache_scores = jnp.where(live[None, None, None], cache_scores, -jnp.inf)
    top = jnp.maximum(jnp.max(draft_scores, axis=-1), jnp.max(cache_scores, axis=-1))
    draft_exp = jnp.exp(draft_scores - top[..., None])
    cache_exp = jnp.exp(cache_scores - top[..., None])
    total = jnp.sum(draft_exp, axis=-1) + jnp.sum(cache_exp, axis=-1)
    weighted = jnp.einsum(
        "gqjk,kgd->jgqd",
        draft_exp.astype(jnp.bfloat16),
        new_values,
        preferred_element_type=jnp.float32,
    )
    weighted = weighted + jnp.einsum(
        "gqjp,pgd->jgqd",
        cache_exp.astype(jnp.bfloat16),
        cache_v,
        preferred_element_type=jnp.float32,
    )
    return (
        finish(weighted, total, draft),
        accept_rows(new_keys, new_values, ancestry, depths, leaf, depth_limit),
    )


def gate_weights(inputs, router, routes):
    logits = jnp.dot(inputs, router, preferred_element_type=jnp.float32)
    onehot = routes[:, :, None] == jnp.arange(router.shape[1])[None, None, :]
    picked = jnp.sum(jnp.where(onehot, logits[:, None, :], 0.0), axis=2)
    return jax.nn.softmax(picked, axis=1).astype(jnp.bfloat16)


def expert_slots(inputs, weights, routes, expert, gate_rows, up_rows, down_rows, capacity):
    count = inputs.shape[0]
    match = routes == expert
    hits = jnp.any(match, axis=1)
    gate_of = jnp.sum(jnp.where(match, weights.astype(jnp.float32), 0.0), axis=1)
    slot_ids = jnp.cumsum(hits.astype(jnp.int32)) - 1
    target = jnp.where(hits, slot_ids, capacity)
    index = jnp.full((capacity,), count, jnp.int32).at[target].set(jnp.arange(count), mode="drop")
    valid = index < count
    safe = jnp.minimum(index, count - 1)
    picked = inputs[safe]
    gate_val = lax.dot_general(
        picked, gate_rows, (((1,), (1,)), ((), ())), preferred_element_type=jnp.float32
    )
    up_val = lax.dot_general(
        picked, up_rows, (((1,), (1,)), ((), ())), preferred_element_type=jnp.float32
    )
    active = (gate_val * jax.nn.sigmoid(SWIGLU_ALPHA * gate_val) * (up_val + 1.0)).astype(
        jnp.bfloat16
    )
    result = jnp.dot(active, down_rows, preferred_element_type=jnp.float32)
    scale_rows = jnp.where(valid, gate_of[safe], 0.0)
    return (result * scale_rows[:, None], index)


def local_general(
    hidden,
    attn_gain,
    w_query,
    w_keyval,
    w_out,
    cache_keys,
    cache_values,
    cache_lens,
    parents,
    accepted,
    moe_gain,
    w_router,
    routes,
    w_gate,
    w_up,
    w_down,
):
    devices = lax.axis_size("tp")
    index_me = lax.axis_index("tp")
    rows = hidden.shape[0]
    normed = rms_norm(hidden, attn_gain)
    local_query = w_query.shape[1]
    both_weights = jnp.concatenate([w_query, w_keyval], axis=1)
    projected = jnp.dot(
        lax.all_gather(normed, "tp", axis=0, tiled=True),
        both_weights,
        preferred_element_type=jnp.float32,
    ).astype(jnp.bfloat16)
    width = projected.shape[1]
    gathered_cols = lax.all_to_all(projected, "tp", split_axis=0, concat_axis=1, tiled=True)
    gathered_cols = gathered_cols.reshape(rows, devices, width)
    requests = cache_lens.shape[0]
    draft = parents.shape[1]
    query = gathered_cols[:, :, :local_query].reshape(requests, draft, HEADS, HEAD_DIM)
    keyval = gathered_cols[:, :, local_query:].reshape(
        requests, draft, devices * (width - local_query)
    )

    def per_request(items):
        return attend_padded(*items, DEPTH)

    attended, accepted_kv = lax.map(
        per_request, (query, keyval, cache_keys, cache_values, cache_lens, parents, accepted)
    )
    attended = attended.reshape(rows, HEADS * HEAD_DIM)
    head_cols = lax.all_to_all(attended, "tp", split_axis=1, concat_axis=0, tiled=True)
    attn_sum = lax.psum_scatter(
        jnp.dot(head_cols, w_out, preferred_element_type=jnp.float32),
        "tp",
        scatter_dimension=0,
        tiled=True,
    )
    middle = (hidden.astype(jnp.float32) + attn_sum).astype(jnp.bfloat16)
    moe_in = rms_norm(middle, moe_gain)
    all_inputs = lax.all_gather(moe_in, "tp", axis=0, tiled=True)
    all_weights = gate_weights(all_inputs, w_router, routes)
    units = w_down.shape[0]
    expert = index_me * units // EXPERT_HID
    count = all_inputs.shape[0]
    capacity = 2 * count * routes.shape[1] // w_router.shape[1]
    slot_rows, slot_index = expert_slots(
        all_inputs, all_weights, routes, expert, w_gate, w_up, w_down, capacity
    )
    term = (
        jnp.zeros((count, all_inputs.shape[1]), jnp.float32)
        .at[slot_index]
        .add(slot_rows, mode="drop")
    )
    mixed = lax.psum_scatter(
        term.astype(jnp.bfloat16), "tp", scatter_dimension=0, tiled=True
    ).astype(jnp.float32)
    layer_out = (middle.astype(jnp.float32) + mixed).astype(jnp.bfloat16)
    return (layer_out, accepted_kv)


NEGATIVE = -1e30
VMEM_LIMIT = 60 * 1024 * 1024
VM = pl.BlockSpec(memory_space=pltpu.VMEM)
SM = pl.BlockSpec(memory_space=pltpu.SMEM)


def run(kernel, outs, args, scalars=1, scratch=(), flops=0, moved=0):
    return pl.pallas_call(
        kernel,
        out_shape=tuple(jax.ShapeDtypeStruct(s, t) for s, t in outs),
        in_specs=[SM] * scalars + [VM] * (len(args) - scalars),
        out_specs=tuple(VM for _ in outs),
        scratch_shapes=list(scratch),
        compiler_params=pltpu.CompilerParams(vmem_limit_bytes=VMEM_LIMIT),
        cost_estimate=pl.CostEstimate(flops=flops, bytes_accessed=moved, transcendentals=0),
    )(*args)


def dot_nt(left, right):
    return lax.dot_general(
        left, right, (((1,), (1,)), ((), ())), preferred_element_type=jnp.float32
    )


def dot_tn(left, right):
    return lax.dot_general(
        left, right, (((0,), (0,)), ((), ())), preferred_element_type=jnp.float32
    )


def dot_nn(left, right):
    return jnp.dot(left, right, preferred_element_type=jnp.float32)


def iota(shape, dim):
    return lax.broadcasted_iota(jnp.int32, shape, dim)


def tree_kernel(lens, accepted, parents, cos_out, sin_out, bias_out, pick_out):
    wide = parents.shape[1]
    draft, lanes = cos_out.shape
    rows, cols = iota((wide, wide), 0), iota((wide, wide), 1)
    identity = (rows == cols).astype(jnp.bfloat16)
    step = jnp.maximum((parents[...] == rows).astype(jnp.bfloat16), identity)
    span = 1
    while span < DEPTH:
        step = (dot_nn(step, step) > 0.5).astype(jnp.bfloat16)
        span = span * 2
    ancestry = dot_tn(step, identity)
    depth_row = jnp.sum(step.astype(jnp.float32), axis=0, keepdims=True) - 1.0
    depth_col = jnp.sum(ancestry, axis=1, keepdims=True) - 1.0
    positions = depth_col[:draft] + lens[0].astype(jnp.float32)
    lane = iota((1, lanes), 1)
    powers = jnp.bitwise_and(lane, HEAD_DIM // 2 - 1).astype(jnp.float32)
    inverse = jnp.exp(powers * (-2.0 * math.log(THETA) / HEAD_DIM))
    angles = positions * inverse
    cos_out[...] = jnp.cos(angles)
    low = jnp.bitwise_and(lane, HEAD_DIM - 1) < HEAD_DIM // 2
    sine = jnp.sin(angles)
    sin_out[...] = jnp.where(low, -sine, sine)
    bias_out[...] = jnp.where(ancestry[:draft] > 0.5, 0.0, NEGATIVE)
    leaf_row = jnp.sum(jnp.where(rows == accepted[0], ancestry, 0.0), axis=0, keepdims=True)
    depths = iota(pick_out.shape, 0).astype(jnp.float32)
    pick_out[...] = jnp.where((depth_row == depths) & (leaf_row > 0.5), 1.0, 0.0)


def project_kernel(*refs):
    pieces, (gain, w_query, w_keyval), rest = refs[:8], refs[8:11], refs[11:]
    outs, normed = rest[:4], rest[4]
    count = pieces[0].shape[0]
    for k, piece in enumerate(pieces):
        floats = piece[...].astype(jnp.float32)
        mean_sq = jnp.mean(floats * floats, axis=-1, keepdims=True)
        normed[k * count : (k + 1) * count, :] = floats * lax.rsqrt(mean_sq + EPSILON) * gain[...]
    rows = normed[...].astype(jnp.bfloat16)
    query = dot_nn(rows, w_query[...]).astype(jnp.bfloat16)
    keyval = dot_nn(rows, w_keyval[...]).astype(jnp.bfloat16)
    split = w_query.shape[1]
    for i, out in enumerate(outs):
        out[:, :split] = query[2 * count * i : 2 * count * (i + 1)]
        out[:, split:] = keyval[2 * count * i : 2 * count * (i + 1)]


def attend_kernel(*refs):
    me, lens = refs[0][0], refs[1][0]
    straight, crossed = refs[2:6], refs[6:10]
    cos, sin, bias, pick, keys, values = refs[10:16]
    outs, accepted_out = refs[16:20], refs[20]
    blocks, queries, new_keys, new_values, attended = refs[21:]
    draft = cos.shape[0]
    lanes = 2 * HEAD_DIM
    for i in range(4):
        blocks[me ^ (2 * i)] = straight[i][:draft, :].astype(jnp.float32)
        blocks[me ^ (2 * i + 1)] = crossed[i][draft:, :].astype(jnp.float32)
    lane = iota((draft, lanes), 1)
    low = jnp.bitwise_and(lane, HEAD_DIM - 1) < HEAD_DIM // 2
    left = lane < HEAD_DIM
    cosine, sine, mask = cos[...], sin[...], bias[...]
    slots = keys.shape[0]
    live = jnp.where(iota((1, slots), 1) < lens, 0.0, NEGATIVE)

    def rope(tile):
        half = HEAD_DIM // 2
        partner = jnp.where(low, pltpu.roll(tile, lanes - half, 1), pltpu.roll(tile, half, 1))
        return (tile * cosine + partner * sine).astype(jnp.bfloat16).astype(jnp.float32)

    new_keys[...] = jnp.zeros_like(new_keys)
    new_values[...] = jnp.zeros_like(new_values)
    q_cols = blocks.shape[2] - lanes
    heads = q_cols // HEAD_DIM
    for pair in range(4):
        new_keys[:draft, :] = rope(blocks[pair, :, q_cols:])
        new_values[:draft, :] = blocks[4 + pair, :, q_cols:]
        fresh_k = new_keys[...].astype(jnp.bfloat16)
        fresh_v = new_values[...].astype(jnp.bfloat16)
        picked = pick[...].astype(jnp.bfloat16)
        span = slice(pair * lanes, (pair + 1) * lanes)
        accepted_out[:, span] = dot_nn(picked, fresh_k).astype(jnp.bfloat16)
        accepted_out[:, slice(4 * lanes + pair * lanes, 4 * lanes + (pair + 1) * lanes)] = dot_nn(
            picked, fresh_v
        ).astype(jnp.bfloat16)
        for p in range(2):
            for t in range(heads // 2):
                tile = rope(blocks[2 * pair + p, :, t * lanes : (t + 1) * lanes]) * 0.125
                turned = pltpu.roll(tile, HEAD_DIM, 1)
                first, second = (tile, turned) if p == 0 else (turned, tile)
                keep = left if p == 0 else ~left
                at = (p * heads + 2 * t) * draft
                queries[at : at + draft, :] = jnp.where(keep, first, 0.0)
                queries[at + draft : at + 2 * draft, :] = jnp.where(keep, second, 0.0)
        group = queries[...].astype(jnp.bfloat16)
        scores = dot_nt(group, keys[:, span]) + live
        fresh = dot_nt(group, fresh_k)
        fresh = (fresh.reshape(2 * heads, draft, lanes) + mask[None]).reshape(fresh.shape)
        top = jnp.maximum(
            jnp.max(scores, axis=1, keepdims=True), jnp.max(fresh, axis=1, keepdims=True)
        )
        weights = jnp.exp(scores - top)
        fresh = jnp.exp(fresh - top)
        total = jnp.sum(weights, axis=1, keepdims=True) + jnp.sum(fresh, axis=1, keepdims=True)
        mixed = dot_nn(weights.astype(jnp.bfloat16), values[:, span])
        mixed = (mixed + dot_nn(fresh.astype(jnp.bfloat16), fresh_v)) / total
        for p in range(2):
            for t in range(heads // 2):
                at = (p * heads + 2 * t) * draft
                first, second = mixed[at : at + draft], mixed[at + draft : at + 2 * draft]
                if p == 0:
                    tile = jnp.where(left, first, pltpu.roll(second, HEAD_DIM, 1))
                else:
                    tile = jnp.where(left, pltpu.roll(first, HEAD_DIM, 1), second)
                col = p * q_cols + t * lanes
                attended[pair, :, col : col + lanes] = tile
    for i, out in enumerate(outs):
        out[...] = attended[(me // 2) ^ i].astype(jnp.bfloat16)


def named_slots(routes, expert, first, count):
    tokens = routes.shape[1]
    hits = jnp.max((routes[...] == expert).astype(jnp.float32), axis=0, keepdims=True)
    upper = (iota((tokens, tokens), 0) <= iota((tokens, tokens), 1)).astype(jnp.bfloat16)
    wide = jnp.broadcast_to(hits, (16, tokens)).astype(jnp.bfloat16)
    order = dot_nn(wide, upper)[:1]
    place = iota((count, tokens), 0).astype(jnp.float32) + (first + 1).astype(jnp.float32)
    return jnp.where((order == place) & (hits > 0.5), 1.0, 0.0)


def residual_kernel(*refs):
    me, pieces, routes, out, rows = refs[0][0], refs[1:9], refs[9], refs[10], refs[11]
    count = pieces[0].shape[0]
    for k, piece in enumerate(pieces):
        rows[pl.ds(pl.multiple_of((me ^ k) * count, 8), count), :] = piece[...].astype(jnp.float32)
    half = out.shape[0]
    chosen = named_slots(routes, me // 2, (me % 2) * half, half).astype(jnp.bfloat16)
    out[...] = dot_nn(chosen, rows[...].astype(jnp.bfloat16))


def outproj_kernel(*refs):
    me, pieces = refs[0][0], refs[1:9]
    w_own, w_other, routes, residual = refs[9:13]
    own, sends = refs[13], refs[14:17]
    rows, chosen = refs[17:]
    count = pieces[0].shape[0]
    half = own.shape[0]
    core = me % 2
    for k, piece in enumerate(pieces):
        rows[pl.ds(pl.multiple_of((me ^ k) * count, 8), count), :] = piece[...].astype(jnp.float32)
    for i in range(4):
        chosen[i * half : (i + 1) * half, :] = named_slots(routes, (me // 2) ^ i, core * half, half)
    picked = dot_nn(chosen[...].astype(jnp.bfloat16), rows[...].astype(jnp.bfloat16))
    width = w_own.shape[1]
    low, high = picked[:, :width], picked[:, width:]
    first = jnp.where(core == 0, low, high).astype(jnp.bfloat16)
    second = jnp.where(core == 0, high, low).astype(jnp.bfloat16)
    summed = dot_nt(first, w_own[...]) + dot_nt(second, w_other[...])
    own[...] = summed[:half] + residual[...]
    for i, out in enumerate(sends):
        out[...] = summed[(i + 1) * half : (i + 2) * half].astype(jnp.bfloat16)


def token_kernel(*refs):
    me, pieces, (w_own, w_other, out, rows) = refs[0][0], refs[1:5], refs[5:]
    count = pieces[0].shape[0]
    core = me % 2
    for i, piece in enumerate(pieces):
        rows[i * count : (i + 1) * count, :] = piece[...].astype(jnp.float32)
    width = w_own.shape[1]
    low, high = rows[:, :width], rows[:, width:]
    first = jnp.where(core == 0, low, high).astype(jnp.bfloat16)
    second = jnp.where(core == 0, high, low).astype(jnp.bfloat16)
    out[...] = dot_nt(first, w_own[...]) + dot_nt(second, w_other[...])


def expert_kernel(me_ref, mine, theirs, gain, router, routes, w_gate, w_up, w_down, out, rows, active):
    me = me_ref[0]
    core, expert = me % 2, me // 2
    half = mine.shape[0]
    rows[pl.ds(pl.multiple_of(core * half, 8), half), :] = mine[...].astype(jnp.float32)
    rows[pl.ds(pl.multiple_of((1 - core) * half, 8), half), :] = theirs[...].astype(jnp.float32)
    floats = rows[...]
    mean_sq = jnp.mean(floats * floats, axis=-1, keepdims=True)
    inputs = (floats * lax.rsqrt(mean_sq + EPSILON) * gain[...]).astype(jnp.bfloat16)
    experts, tokens = router.shape[0], routes.shape[1]
    logits = dot_nt(inputs, router[...])
    chosen = named_slots(routes, expert, expert * 0, 2 * half).astype(jnp.bfloat16)
    named = jnp.zeros((experts, tokens), jnp.float32)
    for i in range(routes.shape[0]):
        named = jnp.maximum(
            named, (iota((experts, tokens), 0) == routes[i : i + 1, :]).astype(jnp.float32)
        )
    named = dot_nt(chosen, named.astype(jnp.bfloat16)) > 0.5
    logits = jnp.where(named, logits, NEGATIVE)
    odds = jnp.exp(logits - jnp.max(logits, axis=1, keepdims=True))
    here = named & (iota(logits.shape, 1) == expert)
    share = jnp.sum(jnp.where(here, odds, 0.0), axis=1, keepdims=True)
    share = (share / jnp.sum(odds, axis=1, keepdims=True)).astype(jnp.bfloat16).astype(jnp.float32)
    gate_val = dot_nt(inputs, w_gate[...])
    up_val = dot_nt(inputs, w_up[...])
    act = gate_val * jax.nn.sigmoid(SWIGLU_ALPHA * gate_val) * (up_val + 1.0)
    active[...] = act.astype(jnp.bfloat16)
    out[...] = (dot_nn(active[...], w_down[...]) * share).astype(jnp.bfloat16)


def combine_kernel(*refs):
    me, mine, theirs, routes, sums, hidden = refs[0][0], *refs[1:6]
    own, sends, rows = refs[6], refs[7:10], refs[10]
    count = hidden.shape[0]
    total = (mine[...].astype(jnp.float32) + theirs[...].astype(jnp.float32)).astype(jnp.bfloat16)
    expert = me // 2
    chosen = named_slots(routes, expert, expert * 0, total.shape[0]).astype(jnp.bfloat16)
    rows[...] = dot_tn(chosen, total)

    def of(i):
        start = pl.multiple_of((me ^ (2 * i)) * count, 8)
        return rows[pl.ds(start, count), :] + sums[i * count : (i + 1) * count, :]

    own[...] = of(0) + hidden[...].astype(jnp.float32)
    for i, out in enumerate(sends):
        out[...] = of(i + 1).astype(jnp.bfloat16)


def local_paired(
    hidden,
    attn_gain,
    w_query,
    w_keyval,
    w_out,
    cache_keys,
    cache_values,
    cache_lens,
    parents,
    accepted,
    moe_gain,
    w_router,
    routes,
    w_gate,
    w_up,
    w_down,
):
    devices = lax.axis_size("tp")
    me = lax.axis_index("tp").astype(jnp.int32).reshape(1)
    bf16, f32 = jnp.bfloat16, jnp.float32

    def swap(values, offset):
        return lax.ppermute(values, "tp", [(i, i ^ offset) for i in range(devices)])

    rows, width = hidden.shape
    tokens = routes.shape[0]
    draft = parents.shape[1]
    capacity = 2 * tokens * routes.shape[1] // w_router.shape[1]
    half = capacity // 2
    routes_t = routes.T
    router_t = w_router.T
    w_out_t = w_out.T
    gain_row = attn_gain.reshape(1, width)
    moe_row = moe_gain.reshape(1, width)

    line = {s: swap(hidden, s) for s in (6, 4, 2)}
    line[0] = hidden
    across = {s: swap(line[s], 1) for s in (0, 2, 4, 6)}
    pieces = [piece for s in (0, 2, 4, 6) for piece in (line[s], across[s])]
    w_other_t = swap(w_out, 1).T

    lanes = 128
    tree = run(
        tree_kernel,
        [((draft, lanes), f32), ((draft, lanes), f32), ((draft, lanes), f32), ((DEPTH, lanes), f32)],
        [cache_lens, accepted, jnp.pad(parents, ((0, 0), (0, lanes - draft)))],
        scalars=2,
    )

    queries, keyvals = w_query.shape[1], w_keyval.shape[1]
    columns = queries + keyvals
    projected = run(
        project_kernel,
        [((2 * rows, columns), bf16)] * 4,
        [*pieces, gain_row, w_query, w_keyval],
        scalars=0,
        scratch=[pltpu.VMEM((tokens, width), f32)],
        flops=2 * tokens * width * columns,
        moved=width * columns * 2,
    )
    straight = [projected[0]] + [swap(projected[i], 2 * i) for i in (1, 2, 3)]
    crossed = [swap(block, 1) for block in straight]
    residual = run(
        residual_kernel,
        [((half, width), f32)],
        [me, *pieces, routes_t],
        scratch=[pltpu.VMEM((tokens, width), f32)],
        flops=2 * half * tokens * width,
        moved=tokens * width * 4,
    )[0]
    slots, kv_cols = cache_keys.shape[1:]
    attended = run(
        attend_kernel,
        [((rows, 2 * queries), bf16)] * 4 + [((DEPTH, 2 * kv_cols), bf16)],
        [me, cache_lens, *straight, *crossed, *tree, cache_keys[0], cache_values[0]],
        scalars=2,
        scratch=[
            pltpu.VMEM((devices, rows, columns), f32),
            pltpu.VMEM((rows * queries * 2 // HEAD_DIM, lanes), f32),
            pltpu.VMEM((lanes, lanes), f32),
            pltpu.VMEM((lanes, lanes), f32),
            pltpu.VMEM((devices // 2, rows, 2 * queries), f32),
        ],
        flops=4 * rows * HEADS * slots * HEAD_DIM,
        moved=4 * slots * kv_cols,
    )
    accepted_kv = attended[4][None]
    straight = [attended[0]] + [swap(attended[i], 2 * i) for i in (1, 2, 3)]
    crossed = [swap(block, 1) for block in straight]
    pieces = [piece for pair in zip(straight, crossed) for piece in pair]
    out_flops = 2 * 4 * half * 2 * queries * width
    dispatched = run(
        outproj_kernel,
        [((half, width), f32)] + [((half, width), bf16)] * 3,
        [me, *pieces, w_out_t, w_other_t, routes_t, residual],
        scratch=[pltpu.VMEM((tokens, 2 * queries), f32), pltpu.VMEM((4 * half, tokens), f32)],
        flops=out_flops,
        moved=4 * queries * width,
    )
    arrived = [swap(dispatched[i], 2 * i) for i in (1, 2, 3)]
    sums = run(
        token_kernel,
        [((4 * rows, width), f32)],
        [me, *straight, w_out_t, w_other_t],
        scratch=[pltpu.VMEM((4 * rows, 2 * queries), f32)],
        flops=out_flops,
        moved=4 * queries * width,
    )[0]
    middle = dispatched[0]
    for block in arrived:
        middle = middle + block.astype(f32)
    middle = middle.astype(bf16)
    expert_rows = run(
        expert_kernel,
        [((capacity, width), bf16)],
        [me, middle, swap(middle, 1), moe_row, router_t, routes_t, w_gate, w_up, w_down],
        scratch=[pltpu.VMEM((capacity, width), f32), pltpu.VMEM((capacity, w_down.shape[0]), bf16)],
        flops=6 * capacity * width * w_down.shape[0],
        moved=6 * width * w_down.shape[0],
    )[0]
    combined = run(
        combine_kernel,
        [((rows, width), f32)] + [((rows, width), bf16)] * 3,
        [me, expert_rows, swap(expert_rows, 1), routes_t, sums, hidden],
        scratch=[pltpu.VMEM((tokens, width), f32)],
        flops=2 * capacity * tokens * width,
        moved=tokens * width * 4,
    )
    layer_out = combined[0]
    for i in (1, 2, 3):
        layer_out = layer_out + swap(combined[i], 2 * i).astype(f32)
    return (layer_out.astype(bf16), accepted_kv)


def local(hidden, attn_gain, w_query, w_keyval, *rest):
    devices = lax.axis_size("tp")
    parents, units = rest[4], rest[11].shape[0]
    paired = (
        devices == 8
        and parents.shape[0] == 1
        and units * 2 == EXPERT_HID
        and w_query.shape[1] * devices == HEADS * HEAD_DIM
        and w_keyval.shape[1] == 2 * HEAD_DIM
    )
    return (local_paired if paired else local_general)(hidden, attn_gain, w_query, w_keyval, *rest)


def solution(mesh):
    return jax.shard_map(
        local,
        mesh=mesh,
        in_specs=(
            P(("dp", "tp"), None),
            P(),
            P(None, "tp"),
            P(None, "tp"),
            P("tp", None),
            P(("dp", "tp"), None, None),
            P(("dp", "tp"), None, None),
            P(("dp", "tp")),
            P(("dp", "tp"), None),
            P(("dp", "tp")),
            P(),
            P(),
            P("dp", None),
            P("tp", None),
            P("tp", None),
            P("tp", None),
        ),
        out_specs=(P(("dp", "tp"), None), P(("dp", "tp"), None, None)),
        check_vma=False,
    )
```

```python
import math

import jax
import jax.numpy as jnp
from jax import lax
from jax.experimental import pallas as pl
from jax.experimental.pallas import tpu as pltpu
from jax.sharding import PartitionSpec as P

HEADS = 64
HEAD_DIM = 64
EXPERT_HID = 2880
DEPTH = 8


THETA = 150000.0
SWIGLU_ALPHA = 1.702
EPSILON = 1e-05


def rms_norm(values, gain):
    floats = values.astype(jnp.float32)
    mean_sq = jnp.mean(floats * floats, axis=-1, keepdims=True)
    return (floats * lax.rsqrt(mean_sq + EPSILON) * gain).astype(jnp.bfloat16)


def tree_paths(parent_row, depth_limit):
    count = parent_row.shape[0]
    identity = jnp.eye(count, dtype=jnp.bool_)
    ancestry = identity
    for level in range(depth_limit):
        ancestry = identity | jnp.take(ancestry, parent_row, axis=0)
    depths = jnp.sum(ancestry.astype(jnp.int32), axis=1) - 1
    return (ancestry, depths)


def rotate(values, positions):
    half = values.shape[-1] // 2
    steps_f = jnp.arange(half).astype(jnp.float32)
    inverse = jnp.exp(steps_f * (-2.0 * math.log(THETA) / values.shape[-1]))
    angles = positions[:, None] * inverse[None, :]
    cosine = jnp.cos(angles)[:, None, :]
    sine = jnp.sin(angles)[:, None, :]
    first = values[..., :half].astype(jnp.float32)
    second = values[..., half:].astype(jnp.float32)
    turned = jnp.concatenate(
        [first * cosine - second * sine, second * cosine + first * sine], axis=-1
    )
    return turned.astype(jnp.bfloat16)


def prepare(query, keyval, length, parent_row, depth_limit):
    draft, heads, head_dim = query.shape
    kv_width = keyval.shape[1] // 2
    kv_heads = kv_width // head_dim
    ancestry, depths = tree_paths(parent_row, depth_limit)
    positions = (length + depths).astype(jnp.float32)
    query_rot = rotate(query, positions)
    new_keys = rotate(keyval[:, :kv_width].reshape(draft, kv_heads, head_dim), positions)
    new_values = keyval[:, kv_width:].reshape(draft, kv_heads, head_dim)
    grouped = query_rot.reshape(draft, kv_heads, heads // kv_heads, head_dim)
    draft_scores = jnp.einsum(
        "jgqd,kgd->gqjk", grouped, new_keys, preferred_element_type=jnp.float32
    ) * (1.0 / math.sqrt(head_dim))
    draft_scores = jnp.where(ancestry[None, None], draft_scores, -jnp.inf)
    return (grouped, new_keys, new_values, ancestry, depths, draft_scores)


def accept_rows(new_keys, new_values, ancestry, depths, leaf, depth_limit):
    draft = depths.shape[0]
    selector = ancestry[leaf][None, :] & (depths[None, :] == jnp.arange(depth_limit)[:, None])
    new_rows = jnp.concatenate([new_keys.reshape(draft, -1), new_values.reshape(draft, -1)], axis=1)
    return jnp.dot(
        selector.astype(jnp.bfloat16), new_rows, preferred_element_type=jnp.float32
    ).astype(jnp.bfloat16)


def finish(weighted, total, draft):
    return (
        (weighted / jnp.transpose(total, (2, 0, 1))[..., None])
        .astype(jnp.bfloat16)
        .reshape(draft, -1)
    )


def attend_padded(query, keyval, keys_cache, values_cache, length, parent_row, leaf, depth_limit):
    draft, heads, head_dim = query.shape
    grouped, new_keys, new_values, ancestry, depths, draft_scores = prepare(
        query, keyval, length, parent_row, depth_limit
    )
    slots = keys_cache.shape[0]
    kv_heads = new_keys.shape[1]
    cache_k = keys_cache.reshape(slots, kv_heads, head_dim)
    cache_v = values_cache.reshape(slots, kv_heads, head_dim)
    cache_scores = jnp.einsum(
        "jgqd,pgd->gqjp", grouped, cache_k, preferred_element_type=jnp.float32
    ) * (1.0 / math.sqrt(head_dim))
    live = jnp.arange(slots) < length
    cache_scores = jnp.where(live[None, None, None], cache_scores, -jnp.inf)
    top = jnp.maximum(jnp.max(draft_scores, axis=-1), jnp.max(cache_scores, axis=-1))
    draft_exp = jnp.exp(draft_scores - top[..., None])
    cache_exp = jnp.exp(cache_scores - top[..., None])
    total = jnp.sum(draft_exp, axis=-1) + jnp.sum(cache_exp, axis=-1)
    weighted = jnp.einsum(
        "gqjk,kgd->jgqd",
        draft_exp.astype(jnp.bfloat16),
        new_values,
        preferred_element_type=jnp.float32,
    )
    weighted = weighted + jnp.einsum(
        "gqjp,pgd->jgqd",
        cache_exp.astype(jnp.bfloat16),
        cache_v,
        preferred_element_type=jnp.float32,
    )
    return (
        finish(weighted, total, draft),
        accept_rows(new_keys, new_values, ancestry, depths, leaf, depth_limit),
    )


def gate_weights(inputs, router, routes):
    logits = jnp.dot(inputs, router, preferred_element_type=jnp.float32)
    onehot = routes[:, :, None] == jnp.arange(router.shape[1])[None, None, :]
    picked = jnp.sum(jnp.where(onehot, logits[:, None, :], 0.0), axis=2)
    return jax.nn.softmax(picked, axis=1).astype(jnp.bfloat16)


def expert_slots(inputs, weights, routes, expert, gate_rows, up_rows, down_rows, capacity):
    count = inputs.shape[0]
    match = routes == expert
    hits = jnp.any(match, axis=1)
    gate_of = jnp.sum(jnp.where(match, weights.astype(jnp.float32), 0.0), axis=1)
    slot_ids = jnp.cumsum(hits.astype(jnp.int32)) - 1
    target = jnp.where(hits, slot_ids, capacity)
    index = jnp.full((capacity,), count, jnp.int32).at[target].set(jnp.arange(count), mode="drop")
    valid = index < count
    safe = jnp.minimum(index, count - 1)
    picked = inputs[safe]
    gate_val = lax.dot_general(
        picked, gate_rows, (((1,), (1,)), ((), ())), preferred_element_type=jnp.float32
    )
    up_val = lax.dot_general(
        picked, up_rows, (((1,), (1,)), ((), ())), preferred_element_type=jnp.float32
    )
    active = (gate_val * jax.nn.sigmoid(SWIGLU_ALPHA * gate_val) * (up_val + 1.0)).astype(
        jnp.bfloat16
    )
    result = jnp.dot(active, down_rows, preferred_element_type=jnp.float32)
    scale_rows = jnp.where(valid, gate_of[safe], 0.0)
    return (result * scale_rows[:, None], index)


def local_general(
    hidden,
    attn_gain,
    w_query,
    w_keyval,
    w_out,
    cache_keys,
    cache_values,
    cache_lens,
    parents,
    accepted,
    moe_gain,
    w_router,
    routes,
    w_gate,
    w_up,
    w_down,
):
    devices = lax.axis_size("tp")
    index_me = lax.axis_index("tp")
    rows = hidden.shape[0]
    normed = rms_norm(hidden, attn_gain)
    local_query = w_query.shape[1]
    both_weights = jnp.concatenate([w_query, w_keyval], axis=1)
    projected = jnp.dot(
        lax.all_gather(normed, "tp", axis=0, tiled=True),
        both_weights,
        preferred_element_type=jnp.float32,
    ).astype(jnp.bfloat16)
    width = projected.shape[1]
    gathered_cols = lax.all_to_all(projected, "tp", split_axis=0, concat_axis=1, tiled=True)
    gathered_cols = gathered_cols.reshape(rows, devices, width)
    requests = cache_lens.shape[0]
    draft = parents.shape[1]
    query = gathered_cols[:, :, :local_query].reshape(requests, draft, HEADS, HEAD_DIM)
    keyval = gathered_cols[:, :, local_query:].reshape(
        requests, draft, devices * (width - local_query)
    )

    def per_request(items):
        return attend_padded(*items, DEPTH)

    attended, accepted_kv = lax.map(
        per_request, (query, keyval, cache_keys, cache_values, cache_lens, parents, accepted)
    )
    attended = attended.reshape(rows, HEADS * HEAD_DIM)
    head_cols = lax.all_to_all(attended, "tp", split_axis=1, concat_axis=0, tiled=True)
    attn_sum = lax.psum_scatter(
        jnp.dot(head_cols, w_out, preferred_element_type=jnp.float32),
        "tp",
        scatter_dimension=0,
        tiled=True,
    )
    middle = (hidden.astype(jnp.float32) + attn_sum).astype(jnp.bfloat16)
    moe_in = rms_norm(middle, moe_gain)
    all_inputs = lax.all_gather(moe_in, "tp", axis=0, tiled=True)
    all_weights = gate_weights(all_inputs, w_router, routes)
    units = w_down.shape[0]
    expert = index_me * units // EXPERT_HID
    count = all_inputs.shape[0]
    capacity = 2 * count * routes.shape[1] // w_router.shape[1]
    slot_rows, slot_index = expert_slots(
        all_inputs, all_weights, routes, expert, w_gate, w_up, w_down, capacity
    )
    term = (
        jnp.zeros((count, all_inputs.shape[1]), jnp.float32)
        .at[slot_index]
        .add(slot_rows, mode="drop")
    )
    mixed = lax.psum_scatter(
        term.astype(jnp.bfloat16), "tp", scatter_dimension=0, tiled=True
    ).astype(jnp.float32)
    layer_out = (middle.astype(jnp.float32) + mixed).astype(jnp.bfloat16)
    return (layer_out, accepted_kv)


NEGATIVE = -1e30
MIB = 1024 * 1024
VMEM_LIMIT = 24 * MIB
VM = pl.BlockSpec(memory_space=pltpu.VMEM)
SM = pl.BlockSpec(memory_space=pltpu.SMEM)


def run(kernel, outs, args, scalars=1, scratch=(), flops=0, moved=0, limit=VMEM_LIMIT):
    return pl.pallas_call(
        kernel,
        out_shape=tuple(jax.ShapeDtypeStruct(s, t) for s, t in outs),
        in_specs=[SM] * scalars + [VM] * (len(args) - scalars),
        out_specs=tuple(VM for _ in outs),
        scratch_shapes=list(scratch),
        compiler_params=pltpu.CompilerParams(vmem_limit_bytes=limit),
        cost_estimate=pl.CostEstimate(flops=flops, bytes_accessed=moved, transcendentals=0),
    )(*args)


def near(values):
    return pltpu.with_memory_space_constraint(values, pltpu.VMEM)


def far(values):
    return pltpu.with_memory_space_constraint(values, pltpu.HBM)


def load(*arrays):
    def kernel(*refs):
        count = len(arrays)
        sources, targets, sems = refs[:count], refs[count : 2 * count], refs[2 * count]
        copies = [
            pltpu.make_async_copy(source, target, sems.at[i])
            for i, (source, target) in enumerate(zip(sources, targets))
        ]
        for copy in copies:
            copy.start()
        for copy in copies:
            copy.wait()

    moved = sum(a.size * a.dtype.itemsize for a in arrays)
    return pl.pallas_call(
        kernel,
        out_shape=tuple(pltpu.VMEM(a.shape, a.dtype) for a in arrays),
        in_specs=[pl.BlockSpec(memory_space=pl.ANY)] * len(arrays),
        out_specs=tuple(VM for _ in arrays),
        scratch_shapes=[pltpu.SemaphoreType.DMA((len(arrays),))],
        compiler_params=pltpu.CompilerParams(vmem_limit_bytes=MIB),
        cost_estimate=pl.CostEstimate(flops=0, bytes_accessed=2 * moved, transcendentals=0),
    )(*[far(a) for a in arrays])


def dot_nt(left, right):
    return lax.dot_general(
        left, right, (((1,), (1,)), ((), ())), preferred_element_type=jnp.float32
    )


def dot_tn(left, right):
    return lax.dot_general(
        left, right, (((0,), (0,)), ((), ())), preferred_element_type=jnp.float32
    )


def dot_nn(left, right):
    return jnp.dot(left, right, preferred_element_type=jnp.float32)


def iota(shape, dim):
    return lax.broadcasted_iota(jnp.int32, shape, dim)


def tree_kernel(lens, accepted, parents, cos_out, sin_out, bias_out, pick_out):
    wide = parents.shape[1]
    draft, lanes = cos_out.shape
    rows, cols = iota((wide, wide), 0), iota((wide, wide), 1)
    identity = (rows == cols).astype(jnp.bfloat16)
    step = jnp.maximum((parents[...] == rows).astype(jnp.bfloat16), identity)
    span = 1
    while span < DEPTH:
        step = (dot_nn(step, step) > 0.5).astype(jnp.bfloat16)
        span = span * 2
    ancestry = dot_tn(step, identity)
    depth_row = jnp.sum(step.astype(jnp.float32), axis=0, keepdims=True) - 1.0
    depth_col = jnp.sum(ancestry, axis=1, keepdims=True) - 1.0
    positions = depth_col[:draft] + lens[0].astype(jnp.float32)
    lane = iota((1, lanes), 1)
    powers = jnp.bitwise_and(lane, HEAD_DIM // 2 - 1).astype(jnp.float32)
    inverse = jnp.exp(powers * (-2.0 * math.log(THETA) / HEAD_DIM))
    angles = positions * inverse
    cos_out[...] = jnp.cos(angles)
    low = jnp.bitwise_and(lane, HEAD_DIM - 1) < HEAD_DIM // 2
    sine = jnp.sin(angles)
    sin_out[...] = jnp.where(low, -sine, sine)
    bias_out[...] = jnp.where(ancestry[:draft] > 0.5, 0.0, NEGATIVE)
    leaf_row = jnp.sum(jnp.where(rows == accepted[0], ancestry, 0.0), axis=0, keepdims=True)
    depths = iota(pick_out.shape, 0).astype(jnp.float32)
    pick_out[...] = jnp.where((depth_row == depths) & (leaf_row > 0.5), 1.0, 0.0)


def project_kernel(*refs):
    pieces, (gain, w_query, w_keyval), rest = refs[:8], refs[8:11], refs[11:]
    outs, normed = rest[:4], rest[4]
    count = pieces[0].shape[0]
    for k, piece in enumerate(pieces):
        floats = piece[...].astype(jnp.float32)
        mean_sq = jnp.mean(floats * floats, axis=-1, keepdims=True)
        normed[k * count : (k + 1) * count, :] = floats * lax.rsqrt(mean_sq + EPSILON) * gain[...]
    rows = normed[...].astype(jnp.bfloat16)
    query = dot_nn(rows, w_query[...]).astype(jnp.bfloat16)
    keyval = dot_nn(rows, w_keyval[...]).astype(jnp.bfloat16)
    split = w_query.shape[1]
    for i, out in enumerate(outs):
        out[:, :split] = query[2 * count * i : 2 * count * (i + 1)]
        out[:, split:] = keyval[2 * count * i : 2 * count * (i + 1)]


def attend_kernel(*refs):
    me, lens = refs[0][0], refs[1][0]
    straight, crossed = refs[2:6], refs[6:10]
    cos, sin, bias, pick, keys, values = refs[10:16]
    outs, accepted_out = refs[16:20], refs[20]
    blocks, queries, new_keys, new_values, attended = refs[21:]
    draft = cos.shape[0]
    lanes = 2 * HEAD_DIM
    for i in range(4):
        blocks[me ^ (2 * i)] = straight[i][:draft, :].astype(jnp.float32)
        blocks[me ^ (2 * i + 1)] = crossed[i][draft:, :].astype(jnp.float32)
    lane = iota((draft, lanes), 1)
    low = jnp.bitwise_and(lane, HEAD_DIM - 1) < HEAD_DIM // 2
    left = lane < HEAD_DIM
    cosine, sine, mask = cos[...], sin[...], bias[...]
    slots = keys.shape[0]
    live = jnp.where(iota((1, slots), 1) < lens, 0.0, NEGATIVE)

    def rope(tile):
        half = HEAD_DIM // 2
        partner = jnp.where(low, pltpu.roll(tile, lanes - half, 1), pltpu.roll(tile, half, 1))
        return (tile * cosine + partner * sine).astype(jnp.bfloat16).astype(jnp.float32)

    new_keys[...] = jnp.zeros_like(new_keys)
    new_values[...] = jnp.zeros_like(new_values)
    q_cols = blocks.shape[2] - lanes
    heads = q_cols // HEAD_DIM
    for pair in range(4):
        new_keys[:draft, :] = rope(blocks[pair, :, q_cols:])
        new_values[:draft, :] = blocks[4 + pair, :, q_cols:]
        fresh_k = new_keys[...].astype(jnp.bfloat16)
        fresh_v = new_values[...].astype(jnp.bfloat16)
        picked = pick[...].astype(jnp.bfloat16)
        span = slice(pair * lanes, (pair + 1) * lanes)
        accepted_out[:, span] = dot_nn(picked, fresh_k).astype(jnp.bfloat16)
        accepted_out[:, slice(4 * lanes + pair * lanes, 4 * lanes + (pair + 1) * lanes)] = dot_nn(
            picked, fresh_v
        ).astype(jnp.bfloat16)
        for p in range(2):
            for t in range(heads // 2):
                tile = rope(blocks[2 * pair + p, :, t * lanes : (t + 1) * lanes]) * 0.125
                turned = pltpu.roll(tile, HEAD_DIM, 1)
                first, second = (tile, turned) if p == 0 else (turned, tile)
                keep = left if p == 0 else ~left
                at = (p * heads + 2 * t) * draft
                queries[at : at + draft, :] = jnp.where(keep, first, 0.0)
                queries[at + draft : at + 2 * draft, :] = jnp.where(keep, second, 0.0)
        group = queries[...].astype(jnp.bfloat16)
        scores = dot_nt(group, keys[:, span]) + live
        fresh = dot_nt(group, fresh_k)
        fresh = (fresh.reshape(2 * heads, draft, lanes) + mask[None]).reshape(fresh.shape)
        top = jnp.maximum(
            jnp.max(scores, axis=1, keepdims=True), jnp.max(fresh, axis=1, keepdims=True)
        )
        weights = jnp.exp(scores - top)
        fresh = jnp.exp(fresh - top)
        total = jnp.sum(weights, axis=1, keepdims=True) + jnp.sum(fresh, axis=1, keepdims=True)
        mixed = dot_nn(weights.astype(jnp.bfloat16), values[:, span])
        mixed = (mixed + dot_nn(fresh.astype(jnp.bfloat16), fresh_v)) / total
        for p in range(2):
            for t in range(heads // 2):
                at = (p * heads + 2 * t) * draft
                first, second = mixed[at : at + draft], mixed[at + draft : at + 2 * draft]
                if p == 0:
                    tile = jnp.where(left, first, pltpu.roll(second, HEAD_DIM, 1))
                else:
                    tile = jnp.where(left, pltpu.roll(first, HEAD_DIM, 1), second)
                col = p * q_cols + t * lanes
                attended[pair, :, col : col + lanes] = tile
    for i, out in enumerate(outs):
        out[...] = attended[(me // 2) ^ i].astype(jnp.bfloat16)


def named_slots(routes, expert, first, count):
    tokens = routes.shape[1]
    hits = jnp.max((routes[...] == expert).astype(jnp.float32), axis=0, keepdims=True)
    upper = (iota((tokens, tokens), 0) <= iota((tokens, tokens), 1)).astype(jnp.bfloat16)
    wide = jnp.broadcast_to(hits, (16, tokens)).astype(jnp.bfloat16)
    order = dot_nn(wide, upper)[:1]
    place = iota((count, tokens), 0).astype(jnp.float32) + (first + 1).astype(jnp.float32)
    return jnp.where((order == place) & (hits > 0.5), 1.0, 0.0)


def residual_kernel(*refs):
    me, pieces, routes, out, rows = refs[0][0], refs[1:9], refs[9], refs[10], refs[11]
    count = pieces[0].shape[0]
    for k, piece in enumerate(pieces):
        rows[pl.ds(pl.multiple_of((me ^ k) * count, 8), count), :] = piece[...].astype(jnp.float32)
    half = out.shape[0]
    chosen = named_slots(routes, me // 2, (me % 2) * half, half).astype(jnp.bfloat16)
    out[...] = dot_nn(chosen, rows[...].astype(jnp.bfloat16))


def outproj_kernel(*refs):
    me, pieces = refs[0][0], refs[1:9]
    w_own, w_other, routes, residual = refs[9:13]
    own, sends = refs[13], refs[14:17]
    rows, chosen = refs[17:]
    count = pieces[0].shape[0]
    half = own.shape[0]
    core = me % 2
    for k, piece in enumerate(pieces):
        rows[pl.ds(pl.multiple_of((me ^ k) * count, 8), count), :] = piece[...].astype(jnp.float32)
    for i in range(4):
        chosen[i * half : (i + 1) * half, :] = named_slots(routes, (me // 2) ^ i, core * half, half)
    picked = dot_nn(chosen[...].astype(jnp.bfloat16), rows[...].astype(jnp.bfloat16))
    width = w_own.shape[1]
    low, high = picked[:, :width], picked[:, width:]
    first = jnp.where(core == 0, low, high).astype(jnp.bfloat16)
    second = jnp.where(core == 0, high, low).astype(jnp.bfloat16)
    summed = dot_nt(first, w_own[...]) + dot_nt(second, w_other[...])
    own[...] = summed[:half] + residual[...]
    for i, out in enumerate(sends):
        out[...] = summed[(i + 1) * half : (i + 2) * half].astype(jnp.bfloat16)


def token_kernel(*refs):
    me, pieces, (w_own, w_other, out, rows) = refs[0][0], refs[1:5], refs[5:]
    count = pieces[0].shape[0]
    core = me % 2
    for i, piece in enumerate(pieces):
        rows[i * count : (i + 1) * count, :] = piece[...].astype(jnp.float32)
    width = w_own.shape[1]
    low, high = rows[:, :width], rows[:, width:]
    first = jnp.where(core == 0, low, high).astype(jnp.bfloat16)
    second = jnp.where(core == 0, high, low).astype(jnp.bfloat16)
    out[...] = dot_nt(first, w_own[...]) + dot_nt(second, w_other[...])


def expert_kernel(me_ref, mine, theirs, gain, router, routes, w_gate, w_up, w_down, out, rows, active):
    me = me_ref[0]
    core, expert = me % 2, me // 2
    half = mine.shape[0]
    rows[pl.ds(pl.multiple_of(core * half, 8), half), :] = mine[...].astype(jnp.float32)
    rows[pl.ds(pl.multiple_of((1 - core) * half, 8), half), :] = theirs[...].astype(jnp.float32)
    floats = rows[...]
    mean_sq = jnp.mean(floats * floats, axis=-1, keepdims=True)
    inputs = (floats * lax.rsqrt(mean_sq + EPSILON) * gain[...]).astype(jnp.bfloat16)
    experts, tokens = router.shape[0], routes.shape[1]
    logits = dot_nt(inputs, router[...])
    chosen = named_slots(routes, expert, expert * 0, 2 * half).astype(jnp.bfloat16)
    named = jnp.zeros((experts, tokens), jnp.float32)
    for i in range(routes.shape[0]):
        named = jnp.maximum(
            named, (iota((experts, tokens), 0) == routes[i : i + 1, :]).astype(jnp.float32)
        )
    named = dot_nt(chosen, named.astype(jnp.bfloat16)) > 0.5
    logits = jnp.where(named, logits, NEGATIVE)
    odds = jnp.exp(logits - jnp.max(logits, axis=1, keepdims=True))
    here = named & (iota(logits.shape, 1) == expert)
    share = jnp.sum(jnp.where(here, odds, 0.0), axis=1, keepdims=True)
    share = (share / jnp.sum(odds, axis=1, keepdims=True)).astype(jnp.bfloat16).astype(jnp.float32)
    gate_val = dot_nt(inputs, w_gate[...])
    up_val = dot_nt(inputs, w_up[...])
    act = gate_val * jax.nn.sigmoid(SWIGLU_ALPHA * gate_val) * (up_val + 1.0)
    active[...] = act.astype(jnp.bfloat16)
    out[...] = (dot_nn(active[...], w_down[...]) * share).astype(jnp.bfloat16)


def combine_kernel(*refs):
    me, mine, theirs, routes, sums, hidden = refs[0][0], *refs[1:6]
    own, sends, rows = refs[6], refs[7:10], refs[10]
    count = hidden.shape[0]
    total = (mine[...].astype(jnp.float32) + theirs[...].astype(jnp.float32)).astype(jnp.bfloat16)
    expert = me // 2
    chosen = named_slots(routes, expert, expert * 0, total.shape[0]).astype(jnp.bfloat16)
    rows[...] = dot_tn(chosen, total)

    def of(i):
        start = pl.multiple_of((me ^ (2 * i)) * count, 8)
        return rows[pl.ds(start, count), :] + sums[i * count : (i + 1) * count, :]

    own[...] = of(0) + hidden[...].astype(jnp.float32)
    for i, out in enumerate(sends):
        out[...] = of(i + 1).astype(jnp.bfloat16)


def local_paired(
    hidden,
    attn_gain,
    w_query,
    w_keyval,
    w_out,
    cache_keys,
    cache_values,
    cache_lens,
    parents,
    accepted,
    moe_gain,
    w_router,
    routes,
    w_gate,
    w_up,
    w_down,
):
    devices = lax.axis_size("tp")
    me = lax.axis_index("tp").astype(jnp.int32).reshape(1)
    bf16, f32 = jnp.bfloat16, jnp.float32

    def swap(values, offset):
        return lax.ppermute(values, "tp", [(i, i ^ offset) for i in range(devices)])

    rows, width = hidden.shape
    tokens = routes.shape[0]
    draft = parents.shape[1]
    capacity = 2 * tokens * routes.shape[1] // w_router.shape[1]
    half = capacity // 2
    routes_t = routes.T
    router_t = w_router.T
    w_out_t = w_out.T
    gain_row = attn_gain.reshape(1, width)
    moe_row = moe_gain.reshape(1, width)

    line = {s: swap(hidden, s) for s in (6, 4, 2)}
    lanes = 128
    parents = jnp.pad(parents, ((0, 0), (0, lanes - draft)))
    early = (gain_row, moe_row, parents, load(w_query, w_keyval))
    line, early = lax.optimization_barrier((line, early))
    gain_row, moe_row, parents, (near_query, near_keyval) = early
    line[0] = hidden
    across = {s: swap(line[s], 1) for s in (0, 2, 4, 6)}
    pieces = [piece for s in (0, 2, 4, 6) for piece in (line[s], across[s])]

    queries, keyvals = w_query.shape[1], w_keyval.shape[1]
    columns = queries + keyvals
    projected = run(
        project_kernel,
        [((2 * rows, columns), bf16)] * 4,
        [*pieces, gain_row, near(near_query), near(near_keyval)],
        scalars=0,
        scratch=[pltpu.VMEM((tokens, width), f32)],
        flops=2 * tokens * width * columns,
        moved=width * columns * 2,
    )
    (keys, values, w_pair, lens, me_then), projected = lax.optimization_barrier(
        ((cache_keys[0], cache_values[0], w_out, cache_lens, me), projected)
    )
    straight = [projected[0]] + [swap(projected[i], 2 * i) for i in (1, 2, 3)]
    tree = run(
        tree_kernel,
        [((draft, lanes), f32), ((draft, lanes), f32), ((draft, lanes), f32), ((DEPTH, lanes), f32)],
        [lens, accepted, parents],
        scalars=2,
    )
    residual = run(
        residual_kernel,
        [((half, width), f32)],
        [me_then, *pieces, routes_t],
        scratch=[pltpu.VMEM((tokens, width), f32)],
        flops=2 * half * tokens * width,
        moved=tokens * width * 4,
    )[0]
    cached = load(keys, values)
    straight, tree, residual, cached = lax.optimization_barrier((straight, tree, residual, cached))
    crossed = [swap(block, 1) for block in straight]
    w_other_t = swap(w_pair, 1).T
    slots, kv_cols = cache_keys.shape[1:]
    attended = run(
        attend_kernel,
        [((rows, 2 * queries), bf16)] * 4 + [((DEPTH, 2 * kv_cols), bf16)],
        [me, cache_lens, *straight, *crossed, *tree, near(cached[0]), near(cached[1])],
        scalars=2,
        scratch=[
            pltpu.VMEM((devices, rows, columns), f32),
            pltpu.VMEM((rows * queries * 2 // HEAD_DIM, lanes), f32),
            pltpu.VMEM((lanes, lanes), f32),
            pltpu.VMEM((lanes, lanes), f32),
            pltpu.VMEM((devices // 2, rows, 2 * queries), f32),
        ],
        flops=4 * rows * HEADS * slots * HEAD_DIM,
        moved=4 * slots * kv_cols,
    )
    accepted_kv = attended[4][None]
    w_out_t, attended = lax.optimization_barrier((w_out_t, attended))
    straight = [attended[0]] + [swap(attended[i], 2 * i) for i in (1, 2, 3)]
    straight, (near_out,) = lax.optimization_barrier((straight, load(w_out_t)))
    crossed = [swap(block, 1) for block in straight]
    pieces = [piece for pair in zip(straight, crossed) for piece in pair]
    out_flops = 2 * 4 * half * 2 * queries * width
    dispatched = run(
        outproj_kernel,
        [((half, width), f32)] + [((half, width), bf16)] * 3,
        [me, *pieces, near(near_out), near(w_other_t), routes_t, residual],
        scratch=[pltpu.VMEM((tokens, 2 * queries), f32), pltpu.VMEM((4 * half, tokens), f32)],
        flops=out_flops,
        moved=4 * queries * width,
    )
    arrived = [swap(dispatched[i], 2 * i) for i in (1, 2, 3)]
    me_after = lax.optimization_barrier((me, dispatched[1]))[0]
    sums = run(
        token_kernel,
        [((4 * rows, width), f32)],
        [me_after, *straight, near(near_out), near(w_other_t)],
        scratch=[pltpu.VMEM((4 * rows, 2 * queries), f32)],
        limit=6 * MIB,
        flops=out_flops,
        moved=4 * queries * width,
    )[0]
    experts, _ = lax.optimization_barrier(((w_gate, w_up, w_down), dispatched[1]))
    near_gate, near_up, near_down = load(*experts)
    near_weights = (near_gate, near_up, near_down)
    middle, arrived, sums, near_weights = lax.optimization_barrier(
        (dispatched[0], arrived, sums, near_weights)
    )
    for block in arrived:
        middle = middle + block.astype(f32)
    middle = middle.astype(bf16)
    expert_rows = run(
        expert_kernel,
        [((capacity, width), bf16)],
        [
            me,
            middle,
            swap(middle, 1),
            moe_row,
            router_t,
            routes_t,
            *map(near, near_weights),
        ],
        scratch=[pltpu.VMEM((capacity, width), f32), pltpu.VMEM((capacity, w_down.shape[0]), bf16)],
        limit=6 * MIB,
        flops=6 * capacity * width * w_down.shape[0],
        moved=6 * width * w_down.shape[0],
    )[0]
    combined = run(
        combine_kernel,
        [((rows, width), f32)] + [((rows, width), bf16)] * 3,
        [me, expert_rows, swap(expert_rows, 1), routes_t, sums, hidden],
        scratch=[pltpu.VMEM((tokens, width), f32)],
        flops=2 * capacity * tokens * width,
        moved=tokens * width * 4,
    )
    layer_out = combined[0]
    for i in (1, 2, 3):
        layer_out = layer_out + swap(combined[i], 2 * i).astype(f32)
    return (layer_out.astype(bf16), accepted_kv)


def local(hidden, attn_gain, w_query, w_keyval, *rest):
    devices = lax.axis_size("tp")
    parents, units = rest[4], rest[11].shape[0]
    paired = (
        devices == 8
        and parents.shape[0] == 1
        and units * 2 == EXPERT_HID
        and w_query.shape[1] * devices == HEADS * HEAD_DIM
        and w_keyval.shape[1] == 2 * HEAD_DIM
    )
    return (local_paired if paired else local_general)(hidden, attn_gain, w_query, w_keyval, *rest)


def solution(mesh):
    return jax.shard_map(
        local,
        mesh=mesh,
        in_specs=(
            P(("dp", "tp"), None),
            P(),
            P(None, "tp"),
            P(None, "tp"),
            P("tp", None),
            P(("dp", "tp"), None, None),
            P(("dp", "tp"), None, None),
            P(("dp", "tp")),
            P(("dp", "tp"), None),
            P(("dp", "tp")),
            P(),
            P(),
            P("dp", None),
            P("tp", None),
            P("tp", None),
            P("tp", None),
        ),
        out_specs=(P(("dp", "tp"), None), P(("dp", "tp"), None, None)),
        check_vma=False,
    )
```

```python
import math

import jax
import jax.numpy as jnp
from jax import lax
from jax.experimental import pallas as pl
from jax.experimental.pallas import tpu as pltpu
from jax.sharding import PartitionSpec as P

HEADS = 64
HEAD_DIM = 64
EXPERT_HID = 2880
DEPTH = 8


THETA = 150000.0
SWIGLU_ALPHA = 1.702
EPSILON = 1e-05


def rms_norm(values, gain):
    floats = values.astype(jnp.float32)
    mean_sq = jnp.mean(floats * floats, axis=-1, keepdims=True)
    return (floats * lax.rsqrt(mean_sq + EPSILON) * gain).astype(jnp.bfloat16)


def tree_paths(parent_row, depth_limit):
    count = parent_row.shape[0]
    identity = jnp.eye(count, dtype=jnp.bool_)
    ancestry = identity
    for level in range(depth_limit):
        ancestry = identity | jnp.take(ancestry, parent_row, axis=0)
    depths = jnp.sum(ancestry.astype(jnp.int32), axis=1) - 1
    return (ancestry, depths)


def rotate(values, positions):
    half = values.shape[-1] // 2
    steps_f = jnp.arange(half).astype(jnp.float32)
    inverse = jnp.exp(steps_f * (-2.0 * math.log(THETA) / values.shape[-1]))
    angles = positions[:, None] * inverse[None, :]
    cosine = jnp.cos(angles)[:, None, :]
    sine = jnp.sin(angles)[:, None, :]
    first = values[..., :half].astype(jnp.float32)
    second = values[..., half:].astype(jnp.float32)
    turned = jnp.concatenate(
        [first * cosine - second * sine, second * cosine + first * sine], axis=-1
    )
    return turned.astype(jnp.bfloat16)


def prepare(query, keyval, length, parent_row, depth_limit):
    draft, heads, head_dim = query.shape
    kv_width = keyval.shape[1] // 2
    kv_heads = kv_width // head_dim
    ancestry, depths = tree_paths(parent_row, depth_limit)
    positions = (length + depths).astype(jnp.float32)
    query_rot = rotate(query, positions)
    new_keys = rotate(keyval[:, :kv_width].reshape(draft, kv_heads, head_dim), positions)
    new_values = keyval[:, kv_width:].reshape(draft, kv_heads, head_dim)
    grouped = query_rot.reshape(draft, kv_heads, heads // kv_heads, head_dim)
    draft_scores = jnp.einsum(
        "jgqd,kgd->gqjk", grouped, new_keys, preferred_element_type=jnp.float32
    ) * (1.0 / math.sqrt(head_dim))
    draft_scores = jnp.where(ancestry[None, None], draft_scores, -jnp.inf)
    return (grouped, new_keys, new_values, ancestry, depths, draft_scores)


def accept_rows(new_keys, new_values, ancestry, depths, leaf, depth_limit):
    draft = depths.shape[0]
    selector = ancestry[leaf][None, :] & (depths[None, :] == jnp.arange(depth_limit)[:, None])
    new_rows = jnp.concatenate([new_keys.reshape(draft, -1), new_values.reshape(draft, -1)], axis=1)
    return jnp.dot(
        selector.astype(jnp.bfloat16), new_rows, preferred_element_type=jnp.float32
    ).astype(jnp.bfloat16)


def finish(weighted, total, draft):
    return (
        (weighted / jnp.transpose(total, (2, 0, 1))[..., None])
        .astype(jnp.bfloat16)
        .reshape(draft, -1)
    )


def attend_padded(query, keyval, keys_cache, values_cache, length, parent_row, leaf, depth_limit):
    draft, heads, head_dim = query.shape
    grouped, new_keys, new_values, ancestry, depths, draft_scores = prepare(
        query, keyval, length, parent_row, depth_limit
    )
    slots = keys_cache.shape[0]
    kv_heads = new_keys.shape[1]
    cache_k = keys_cache.reshape(slots, kv_heads, head_dim)
    cache_v = values_cache.reshape(slots, kv_heads, head_dim)
    cache_scores = jnp.einsum(
        "jgqd,pgd->gqjp", grouped, cache_k, preferred_element_type=jnp.float32
    ) * (1.0 / math.sqrt(head_dim))
    live = jnp.arange(slots) < length
    cache_scores = jnp.where(live[None, None, None], cache_scores, -jnp.inf)
    top = jnp.maximum(jnp.max(draft_scores, axis=-1), jnp.max(cache_scores, axis=-1))
    draft_exp = jnp.exp(draft_scores - top[..., None])
    cache_exp = jnp.exp(cache_scores - top[..., None])
    total = jnp.sum(draft_exp, axis=-1) + jnp.sum(cache_exp, axis=-1)
    weighted = jnp.einsum(
        "gqjk,kgd->jgqd",
        draft_exp.astype(jnp.bfloat16),
        new_values,
        preferred_element_type=jnp.float32,
    )
    weighted = weighted + jnp.einsum(
        "gqjp,pgd->jgqd",
        cache_exp.astype(jnp.bfloat16),
        cache_v,
        preferred_element_type=jnp.float32,
    )
    return (
        finish(weighted, total, draft),
        accept_rows(new_keys, new_values, ancestry, depths, leaf, depth_limit),
    )


def gate_weights(inputs, router, routes):
    logits = jnp.dot(inputs, router, preferred_element_type=jnp.float32)
    onehot = routes[:, :, None] == jnp.arange(router.shape[1])[None, None, :]
    picked = jnp.sum(jnp.where(onehot, logits[:, None, :], 0.0), axis=2)
    return jax.nn.softmax(picked, axis=1).astype(jnp.bfloat16)


def expert_slots(inputs, weights, routes, expert, gate_rows, up_rows, down_rows, capacity):
    count = inputs.shape[0]
    match = routes == expert
    hits = jnp.any(match, axis=1)
    gate_of = jnp.sum(jnp.where(match, weights.astype(jnp.float32), 0.0), axis=1)
    slot_ids = jnp.cumsum(hits.astype(jnp.int32)) - 1
    target = jnp.where(hits, slot_ids, capacity)
    index = jnp.full((capacity,), count, jnp.int32).at[target].set(jnp.arange(count), mode="drop")
    valid = index < count
    safe = jnp.minimum(index, count - 1)
    picked = inputs[safe]
    gate_val = lax.dot_general(
        picked, gate_rows, (((1,), (1,)), ((), ())), preferred_element_type=jnp.float32
    )
    up_val = lax.dot_general(
        picked, up_rows, (((1,), (1,)), ((), ())), preferred_element_type=jnp.float32
    )
    active = (gate_val * jax.nn.sigmoid(SWIGLU_ALPHA * gate_val) * (up_val + 1.0)).astype(
        jnp.bfloat16
    )
    result = jnp.dot(active, down_rows, preferred_element_type=jnp.float32)
    scale_rows = jnp.where(valid, gate_of[safe], 0.0)
    return (result * scale_rows[:, None], index)


def local_general(
    hidden,
    attn_gain,
    w_query,
    w_keyval,
    w_out,
    cache_keys,
    cache_values,
    cache_lens,
    parents,
    accepted,
    moe_gain,
    w_router,
    routes,
    w_gate,
    w_up,
    w_down,
):
    devices = lax.axis_size("tp")
    index_me = lax.axis_index("tp")
    rows = hidden.shape[0]
    normed = rms_norm(hidden, attn_gain)
    local_query = w_query.shape[1]
    both_weights = jnp.concatenate([w_query, w_keyval], axis=1)
    projected = jnp.dot(
        lax.all_gather(normed, "tp", axis=0, tiled=True),
        both_weights,
        preferred_element_type=jnp.float32,
    ).astype(jnp.bfloat16)
    width = projected.shape[1]
    gathered_cols = lax.all_to_all(projected, "tp", split_axis=0, concat_axis=1, tiled=True)
    gathered_cols = gathered_cols.reshape(rows, devices, width)
    requests = cache_lens.shape[0]
    draft = parents.shape[1]
    query = gathered_cols[:, :, :local_query].reshape(requests, draft, HEADS, HEAD_DIM)
    keyval = gathered_cols[:, :, local_query:].reshape(
        requests, draft, devices * (width - local_query)
    )

    def per_request(items):
        return attend_padded(*items, DEPTH)

    attended, accepted_kv = lax.map(
        per_request, (query, keyval, cache_keys, cache_values, cache_lens, parents, accepted)
    )
    attended = attended.reshape(rows, HEADS * HEAD_DIM)
    head_cols = lax.all_to_all(attended, "tp", split_axis=1, concat_axis=0, tiled=True)
    attn_sum = lax.psum_scatter(
        jnp.dot(head_cols, w_out, preferred_element_type=jnp.float32),
        "tp",
        scatter_dimension=0,
        tiled=True,
    )
    middle = (hidden.astype(jnp.float32) + attn_sum).astype(jnp.bfloat16)
    moe_in = rms_norm(middle, moe_gain)
    all_inputs = lax.all_gather(moe_in, "tp", axis=0, tiled=True)
    all_weights = gate_weights(all_inputs, w_router, routes)
    units = w_down.shape[0]
    expert = index_me * units // EXPERT_HID
    count = all_inputs.shape[0]
    capacity = 2 * count * routes.shape[1] // w_router.shape[1]
    slot_rows, slot_index = expert_slots(
        all_inputs, all_weights, routes, expert, w_gate, w_up, w_down, capacity
    )
    term = (
        jnp.zeros((count, all_inputs.shape[1]), jnp.float32)
        .at[slot_index]
        .add(slot_rows, mode="drop")
    )
    mixed = lax.psum_scatter(
        term.astype(jnp.bfloat16), "tp", scatter_dimension=0, tiled=True
    ).astype(jnp.float32)
    layer_out = (middle.astype(jnp.float32) + mixed).astype(jnp.bfloat16)
    return (layer_out, accepted_kv)


NEGATIVE = -1e30
MIB = 1024 * 1024
VMEM_LIMIT = 24 * MIB
VM = pl.BlockSpec(memory_space=pltpu.VMEM)
SM = pl.BlockSpec(memory_space=pltpu.SMEM)


def run(kernel, outs, args, scalars=1, scratch=(), flops=0, moved=0, limit=VMEM_LIMIT):
    return pl.pallas_call(
        kernel,
        out_shape=tuple(jax.ShapeDtypeStruct(s, t) for s, t in outs),
        in_specs=[SM] * scalars + [VM] * (len(args) - scalars),
        out_specs=tuple(VM for _ in outs),
        scratch_shapes=list(scratch),
        compiler_params=pltpu.CompilerParams(vmem_limit_bytes=limit),
        cost_estimate=pl.CostEstimate(flops=flops, bytes_accessed=moved, transcendentals=0),
    )(*args)


def near(values):
    return pltpu.with_memory_space_constraint(values, pltpu.VMEM)


def far(values):
    return pltpu.with_memory_space_constraint(values, pltpu.HBM)


def load(*arrays):
    def kernel(*refs):
        count = len(arrays)
        sources, targets, sems = refs[:count], refs[count : 2 * count], refs[2 * count]
        copies = [
            pltpu.make_async_copy(source, target, sems.at[i])
            for i, (source, target) in enumerate(zip(sources, targets))
        ]
        for copy in copies:
            copy.start()
        for copy in copies:
            copy.wait()

    moved = sum(a.size * a.dtype.itemsize for a in arrays)
    return pl.pallas_call(
        kernel,
        out_shape=tuple(pltpu.VMEM(a.shape, a.dtype) for a in arrays),
        in_specs=[pl.BlockSpec(memory_space=pl.ANY)] * len(arrays),
        out_specs=tuple(VM for _ in arrays),
        scratch_shapes=[pltpu.SemaphoreType.DMA((len(arrays),))],
        compiler_params=pltpu.CompilerParams(vmem_limit_bytes=MIB),
        cost_estimate=pl.CostEstimate(flops=0, bytes_accessed=2 * moved, transcendentals=0),
    )(*[far(a) for a in arrays])


def dot_nt(left, right):
    return lax.dot_general(
        left, right, (((1,), (1,)), ((), ())), preferred_element_type=jnp.float32
    )


def dot_tn(left, right):
    return lax.dot_general(
        left, right, (((0,), (0,)), ((), ())), preferred_element_type=jnp.float32
    )


def dot_nn(left, right):
    return jnp.dot(left, right, preferred_element_type=jnp.float32)


def iota(shape, dim):
    return lax.broadcasted_iota(jnp.int32, shape, dim)


def tree_kernel(lens, accepted, parents, cos_out, sin_out, bias_out, pick_out):
    wide = parents.shape[1]
    draft, lanes = cos_out.shape
    rows, cols = iota((wide, wide), 0), iota((wide, wide), 1)
    identity = (rows == cols).astype(jnp.bfloat16)
    step = jnp.maximum((parents[...] == rows).astype(jnp.bfloat16), identity)
    span = 1
    while span < DEPTH:
        step = (dot_nn(step, step) > 0.5).astype(jnp.bfloat16)
        span = span * 2
    ancestry = dot_tn(step, identity)
    depth_row = jnp.sum(step.astype(jnp.float32), axis=0, keepdims=True) - 1.0
    depth_col = jnp.sum(ancestry, axis=1, keepdims=True) - 1.0
    positions = depth_col[:draft] + lens[0].astype(jnp.float32)
    lane = iota((1, lanes), 1)
    powers = jnp.bitwise_and(lane, HEAD_DIM // 2 - 1).astype(jnp.float32)
    inverse = jnp.exp(powers * (-2.0 * math.log(THETA) / HEAD_DIM))
    angles = positions * inverse
    cos_out[...] = jnp.cos(angles)
    low = jnp.bitwise_and(lane, HEAD_DIM - 1) < HEAD_DIM // 2
    sine = jnp.sin(angles)
    sin_out[...] = jnp.where(low, -sine, sine)
    bias_out[...] = jnp.where(ancestry[:draft] > 0.5, 0.0, NEGATIVE)
    leaf_row = jnp.sum(jnp.where(rows == accepted[0], ancestry, 0.0), axis=0, keepdims=True)
    depths = iota(pick_out.shape, 0).astype(jnp.float32)
    pick_out[...] = jnp.where((depth_row == depths) & (leaf_row > 0.5), 1.0, 0.0)


def project_kernel(*refs):
    pieces, (gain, *weights), rest = refs[:4], refs[4:9], refs[9:]
    outs, normed = rest[:4], rest[4]
    count = pieces[0].shape[0]
    for k, piece in enumerate(pieces):
        floats = piece[...].astype(jnp.float32)
        mean_sq = jnp.mean(floats * floats, axis=-1, keepdims=True)
        normed[k * count : (k + 1) * count, :] = floats * lax.rsqrt(mean_sq + EPSILON) * gain[...]
    rows = normed[...].astype(jnp.bfloat16)
    at = 0
    for weight in weights:
        result = dot_nn(rows, weight[...])
        width = weight.shape[1]
        for i, out in enumerate(outs):
            out[:, at : at + width] = result[count * i : count * (i + 1)].astype(jnp.bfloat16)
        at += width


def attend_kernel(*refs):
    me, lens = refs[0][0], refs[1][0]
    arrived = refs[2:6]
    cos, sin, bias, pick, keys, values = refs[6:12]
    outs, accepted_out = refs[12:16], refs[16]
    blocks, queries, new_keys, new_values, attended = refs[17:]
    draft = cos.shape[0]
    lanes = 2 * HEAD_DIM
    for i in range(4):
        columns = blocks.shape[2]
        blocks[me ^ (2 * i)] = arrived[i][:, :columns].astype(jnp.float32)
        blocks[me ^ (2 * i + 1)] = arrived[i][:, columns:].astype(jnp.float32)
    lane = iota((draft, lanes), 1)
    low = jnp.bitwise_and(lane, HEAD_DIM - 1) < HEAD_DIM // 2
    left = lane < HEAD_DIM
    cosine, sine, mask = cos[...], sin[...], bias[...]
    slots = keys.shape[0]
    live = jnp.where(iota((1, slots), 1) < lens, 0.0, NEGATIVE)

    def rope(tile):
        half = HEAD_DIM // 2
        partner = jnp.where(low, pltpu.roll(tile, lanes - half, 1), pltpu.roll(tile, half, 1))
        return (tile * cosine + partner * sine).astype(jnp.bfloat16).astype(jnp.float32)

    new_keys[...] = jnp.zeros_like(new_keys)
    new_values[...] = jnp.zeros_like(new_values)
    q_cols = blocks.shape[2] - lanes
    heads = q_cols // HEAD_DIM
    for pair in range(4):
        new_keys[:draft, :] = rope(blocks[pair, :, q_cols:])
        new_values[:draft, :] = blocks[4 + pair, :, q_cols:]
        fresh_k = new_keys[...].astype(jnp.bfloat16)
        fresh_v = new_values[...].astype(jnp.bfloat16)
        picked = pick[...].astype(jnp.bfloat16)
        span = slice(pair * lanes, (pair + 1) * lanes)
        accepted_out[:, span] = dot_nn(picked, fresh_k).astype(jnp.bfloat16)
        accepted_out[:, slice(4 * lanes + pair * lanes, 4 * lanes + (pair + 1) * lanes)] = dot_nn(
            picked, fresh_v
        ).astype(jnp.bfloat16)
        for p in range(2):
            for t in range(heads // 2):
                tile = rope(blocks[2 * pair + p, :, t * lanes : (t + 1) * lanes]) * 0.125
                turned = pltpu.roll(tile, HEAD_DIM, 1)
                first, second = (tile, turned) if p == 0 else (turned, tile)
                keep = left if p == 0 else ~left
                at = (p * heads + 2 * t) * draft
                queries[at : at + draft, :] = jnp.where(keep, first, 0.0)
                queries[at + draft : at + 2 * draft, :] = jnp.where(keep, second, 0.0)
        group = queries[...].astype(jnp.bfloat16)
        scores = dot_nt(group, keys[:, span]) + live
        fresh = dot_nt(group, fresh_k)
        fresh = (fresh.reshape(2 * heads, draft, lanes) + mask[None]).reshape(fresh.shape)
        top = jnp.maximum(
            jnp.max(scores, axis=1, keepdims=True), jnp.max(fresh, axis=1, keepdims=True)
        )
        weights = jnp.exp(scores - top)
        fresh = jnp.exp(fresh - top)
        total = jnp.sum(weights, axis=1, keepdims=True) + jnp.sum(fresh, axis=1, keepdims=True)
        mixed = dot_nn(weights.astype(jnp.bfloat16), values[:, span])
        mixed = (mixed + dot_nn(fresh.astype(jnp.bfloat16), fresh_v)) / total
        for p in range(2):
            for t in range(heads // 2):
                at = (p * heads + 2 * t) * draft
                first, second = mixed[at : at + draft], mixed[at + draft : at + 2 * draft]
                if p == 0:
                    tile = jnp.where(left, first, pltpu.roll(second, HEAD_DIM, 1))
                else:
                    tile = jnp.where(left, pltpu.roll(first, HEAD_DIM, 1), second)
                col = p * q_cols + t * lanes
                attended[pair, :, col : col + lanes] = tile
    for i, out in enumerate(outs):
        out[...] = attended[(me // 2) ^ i].astype(jnp.bfloat16)


def named_slots(routes, expert, first, count):
    tokens = routes.shape[1]
    hits = jnp.max((routes[...] == expert).astype(jnp.float32), axis=0, keepdims=True)
    upper = (iota((tokens, tokens), 0) <= iota((tokens, tokens), 1)).astype(jnp.bfloat16)
    wide = jnp.broadcast_to(hits, (16, tokens)).astype(jnp.bfloat16)
    order = dot_nn(wide, upper)[:1]
    place = iota((count, tokens), 0).astype(jnp.float32) + (first + 1).astype(jnp.float32)
    return jnp.where((order == place) & (hits > 0.5), 1.0, 0.0)


def residual_kernel(*refs):
    me, pieces, routes, out, rows = refs[0][0], refs[1:9], refs[9], refs[10], refs[11]
    count = pieces[0].shape[0]
    for k, piece in enumerate(pieces):
        rows[pl.ds(pl.multiple_of((me ^ k) * count, 8), count), :] = piece[...].astype(jnp.float32)
    half = out.shape[0]
    chosen = named_slots(routes, me // 2, (me % 2) * half, half).astype(jnp.bfloat16)
    out[...] = dot_nn(chosen, rows[...].astype(jnp.bfloat16))


def outproj_kernel(*refs):
    me, pieces = refs[0][0], refs[1:9]
    w_own, w_other, routes = refs[9:12]
    own, sends = refs[12], refs[13:16]
    rows, chosen = refs[16:]
    count = pieces[0].shape[0]
    half = own.shape[0]
    core = me % 2
    for k, piece in enumerate(pieces):
        rows[pl.ds(pl.multiple_of((me ^ k) * count, 8), count), :] = piece[...].astype(jnp.float32)
    for i in range(4):
        chosen[i * half : (i + 1) * half, :] = named_slots(routes, (me // 2) ^ i, core * half, half)
    picked = dot_nn(chosen[...].astype(jnp.bfloat16), rows[...].astype(jnp.bfloat16))
    width = w_own.shape[1]
    low, high = picked[:, :width], picked[:, width:]
    first = jnp.where(core == 0, low, high).astype(jnp.bfloat16)
    second = jnp.where(core == 0, high, low).astype(jnp.bfloat16)
    summed = dot_nt(first, w_own[...]) + dot_nt(second, w_other[...])
    own[...] = summed[:half]
    for i, out in enumerate(sends):
        out[...] = summed[(i + 1) * half : (i + 2) * half].astype(jnp.bfloat16)


def token_kernel(*refs):
    me, pieces, (w_own, w_other, out, rows) = refs[0][0], refs[1:5], refs[5:]
    count = pieces[0].shape[0]
    core = me % 2
    for i, piece in enumerate(pieces):
        rows[i * count : (i + 1) * count, :] = piece[...].astype(jnp.float32)
    width = w_own.shape[1]
    low, high = rows[:, :width], rows[:, width:]
    first = jnp.where(core == 0, low, high).astype(jnp.bfloat16)
    second = jnp.where(core == 0, high, low).astype(jnp.bfloat16)
    out[...] = dot_nt(first, w_own[...]) + dot_nt(second, w_other[...])


def expert_kernel(me_ref, mine, theirs, gain, router, routes, w_gate, w_up, w_down, out, rows, active):
    me = me_ref[0]
    core, expert = me % 2, me // 2
    half = mine.shape[0]
    rows[pl.ds(pl.multiple_of(core * half, 8), half), :] = mine[...].astype(jnp.float32)
    rows[pl.ds(pl.multiple_of((1 - core) * half, 8), half), :] = theirs[...].astype(jnp.float32)
    floats = rows[...]
    mean_sq = jnp.mean(floats * floats, axis=-1, keepdims=True)
    inputs = (floats * lax.rsqrt(mean_sq + EPSILON) * gain[...]).astype(jnp.bfloat16)
    experts, tokens = router.shape[0], routes.shape[1]
    logits = dot_nt(inputs, router[...])
    chosen = named_slots(routes, expert, expert * 0, 2 * half).astype(jnp.bfloat16)
    named = jnp.zeros((experts, tokens), jnp.float32)
    for i in range(routes.shape[0]):
        named = jnp.maximum(
            named, (iota((experts, tokens), 0) == routes[i : i + 1, :]).astype(jnp.float32)
        )
    named = dot_nt(chosen, named.astype(jnp.bfloat16)) > 0.5
    logits = jnp.where(named, logits, NEGATIVE)
    odds = jnp.exp(logits - jnp.max(logits, axis=1, keepdims=True))
    here = named & (iota(logits.shape, 1) == expert)
    share = jnp.sum(jnp.where(here, odds, 0.0), axis=1, keepdims=True)
    share = (share / jnp.sum(odds, axis=1, keepdims=True)).astype(jnp.bfloat16).astype(jnp.float32)
    gate_val = dot_nt(inputs, w_gate[...])
    up_val = dot_nt(inputs, w_up[...])
    act = gate_val * jax.nn.sigmoid(SWIGLU_ALPHA * gate_val) * (up_val + 1.0)
    active[...] = act.astype(jnp.bfloat16)
    out[...] = (dot_nn(active[...], w_down[...]) * share).astype(jnp.bfloat16)


def combine_kernel(*refs):
    me, mine, theirs, routes, sums, hidden = refs[0][0], *refs[1:6]
    own, sends, rows = refs[6], refs[7:10], refs[10]
    count = hidden.shape[0]
    total = (mine[...].astype(jnp.float32) + theirs[...].astype(jnp.float32)).astype(jnp.bfloat16)
    expert = me // 2
    chosen = named_slots(routes, expert, expert * 0, total.shape[0]).astype(jnp.bfloat16)
    rows[...] = dot_tn(chosen, total)

    def of(i):
        start = pl.multiple_of((me ^ (2 * i)) * count, 8)
        return rows[pl.ds(start, count), :] + sums[i * count : (i + 1) * count, :]

    own[...] = of(0) + hidden[...].astype(jnp.float32)
    for i, out in enumerate(sends):
        out[...] = of(i + 1).astype(jnp.bfloat16)


def local_paired(
    hidden,
    attn_gain,
    w_query,
    w_keyval,
    w_out,
    cache_keys,
    cache_values,
    cache_lens,
    parents,
    accepted,
    moe_gain,
    w_router,
    routes,
    w_gate,
    w_up,
    w_down,
):
    devices = lax.axis_size("tp")
    me = lax.axis_index("tp").astype(jnp.int32).reshape(1)
    bf16, f32 = jnp.bfloat16, jnp.float32

    def swap(values, offset):
        return lax.ppermute(values, "tp", [(i, i ^ offset) for i in range(devices)])

    rows, width = hidden.shape
    tokens = routes.shape[0]
    draft = parents.shape[1]
    capacity = 2 * tokens * routes.shape[1] // w_router.shape[1]
    half = capacity // 2
    routes_t = routes.T
    router_t = w_router.T
    gain_row = attn_gain.reshape(1, width)
    moe_row = moe_gain.reshape(1, width)

    line = {s: swap(hidden, s) for s in (6, 4, 2)}
    other_query, other_keyval = swap(w_query, 1), swap(w_keyval, 1)
    lanes = 128
    parents = jnp.pad(parents, ((0, 0), (0, lanes - draft)))
    early = (gain_row, moe_row, parents, load(w_query, w_keyval))
    line, early = lax.optimization_barrier((line, early))
    gain_row, moe_row, parents, (near_query, near_keyval) = early
    line[0] = hidden

    queries, keyvals = w_query.shape[1], w_keyval.shape[1]
    columns = queries + keyvals
    projected = run(
        project_kernel,
        [((rows, 2 * columns), bf16)] * 4,
        [
            *(line[s] for s in (0, 2, 4, 6)),
            gain_row,
            near(near_query),
            near(near_keyval),
            near(other_query),
            near(other_keyval),
        ],
        scalars=0,
        scratch=[pltpu.VMEM((4 * rows, width), f32)],
        limit=10 * MIB,
        flops=2 * tokens * width * columns,
        moved=width * columns * 2,
    )
    later = (line, w_out, cache_keys[0], cache_values[0], cache_lens)
    later, projected = lax.optimization_barrier((later, projected))
    line, w_pair, keys, values, lens = later
    arrived = [projected[0]] + [swap(projected[i], 2 * i) for i in (1, 2, 3)]
    tree = run(
        tree_kernel,
        [((draft, lanes), f32), ((draft, lanes), f32), ((draft, lanes), f32), ((DEPTH, lanes), f32)],
        [lens, accepted, parents],
        scalars=2,
        limit=4 * MIB,
    )
    cached = load(keys, values)
    arrived, tree, cached = lax.optimization_barrier((arrived, tree, cached))
    across = {s: swap(line[s], 1) for s in (0, 2, 4, 6)}
    pieces = [piece for s in (0, 2, 4, 6) for piece in (line[s], across[s])]
    w_other = swap(w_pair, 1)
    slots, kv_cols = cache_keys.shape[1:]
    attended = run(
        attend_kernel,
        [((rows, 2 * queries), bf16)] * 4 + [((DEPTH, 2 * kv_cols), bf16)],
        [me, cache_lens, *arrived, *tree, near(cached[0]), near(cached[1])],
        scalars=2,
        scratch=[
            pltpu.VMEM((devices, rows, columns), f32),
            pltpu.VMEM((rows * queries * 2 // HEAD_DIM, lanes), f32),
            pltpu.VMEM((lanes, lanes), f32),
            pltpu.VMEM((lanes, lanes), f32),
            pltpu.VMEM((devices // 2, rows, 2 * queries), f32),
        ],
        limit=14 * MIB,
        flops=4 * rows * HEADS * slots * HEAD_DIM,
        moved=4 * slots * kv_cols,
    )
    accepted_kv = attended[4][None]
    (w_own, w_other), attended = lax.optimization_barrier(((w_out, w_other), attended))
    straight = [attended[0]] + [swap(attended[i], 2 * i) for i in (1, 2, 3)]
    near_out = load(w_own.T, w_other.T)
    straight, near_out = lax.optimization_barrier((straight, near_out))
    crossed = [swap(block, 1) for block in straight]
    blocks = [block for pair in zip(straight, crossed) for block in pair]
    out_flops = 2 * 4 * half * 2 * queries * width
    dispatched = run(
        outproj_kernel,
        [((half, width), f32)] + [((half, width), bf16)] * 3,
        [me, *blocks, *map(near, near_out), routes_t],
        scratch=[pltpu.VMEM((tokens, 2 * queries), f32), pltpu.VMEM((4 * half, tokens), f32)],
        limit=10 * MIB,
        flops=out_flops,
        moved=4 * queries * width,
    )
    arrived = [swap(dispatched[i], 2 * i) for i in (1, 2, 3)]
    (me_then, experts), _ = lax.optimization_barrier(
        ((me, (w_gate, w_up, w_down)), dispatched[1])
    )
    sums = run(
        token_kernel,
        [((4 * rows, width), f32)],
        [me_then, *straight, *map(near, near_out)],
        scratch=[pltpu.VMEM((4 * rows, 2 * queries), f32)],
        limit=6 * MIB,
        flops=out_flops,
        moved=4 * queries * width,
    )[0]
    residual = run(
        residual_kernel,
        [((half, width), f32)],
        [me_then, *pieces, routes_t],
        scratch=[pltpu.VMEM((tokens, width), f32)],
        limit=6 * MIB,
        flops=2 * half * tokens * width,
        moved=tokens * width * 4,
    )[0]
    near_weights = load(*experts)
    middle, arrived, sums, residual, near_weights = lax.optimization_barrier(
        (dispatched[0], arrived, sums, residual, near_weights)
    )
    middle = middle + residual
    for block in arrived:
        middle = middle + block.astype(f32)
    middle = middle.astype(bf16)
    expert_rows = run(
        expert_kernel,
        [((capacity, width), bf16)],
        [
            me,
            middle,
            swap(middle, 1),
            moe_row,
            router_t,
            routes_t,
            *map(near, near_weights),
        ],
        scratch=[pltpu.VMEM((capacity, width), f32), pltpu.VMEM((capacity, w_down.shape[0]), bf16)],
        limit=6 * MIB,
        flops=6 * capacity * width * w_down.shape[0],
        moved=6 * width * w_down.shape[0],
    )[0]
    combined = run(
        combine_kernel,
        [((rows, width), f32)] + [((rows, width), bf16)] * 3,
        [me, expert_rows, swap(expert_rows, 1), routes_t, sums, hidden],
        scratch=[pltpu.VMEM((tokens, width), f32)],
        flops=2 * capacity * tokens * width,
        moved=tokens * width * 4,
    )
    layer_out = combined[0]
    for i in (1, 2, 3):
        layer_out = layer_out + swap(combined[i], 2 * i).astype(f32)
    return (layer_out.astype(bf16), accepted_kv)


def local(hidden, attn_gain, w_query, w_keyval, *rest):
    devices = lax.axis_size("tp")
    parents, units = rest[4], rest[11].shape[0]
    paired = (
        devices == 8
        and parents.shape[0] == 1
        and units * 2 == EXPERT_HID
        and w_query.shape[1] * devices == HEADS * HEAD_DIM
        and w_keyval.shape[1] == 2 * HEAD_DIM
    )
    return (local_paired if paired else local_general)(hidden, attn_gain, w_query, w_keyval, *rest)


def solution(mesh):
    return jax.shard_map(
        local,
        mesh=mesh,
        in_specs=(
            P(("dp", "tp"), None),
            P(),
            P(None, "tp"),
            P(None, "tp"),
            P("tp", None),
            P(("dp", "tp"), None, None),
            P(("dp", "tp"), None, None),
            P(("dp", "tp")),
            P(("dp", "tp"), None),
            P(("dp", "tp")),
            P(),
            P(),
            P("dp", None),
            P("tp", None),
            P("tp", None),
            P("tp", None),
        ),
        out_specs=(P(("dp", "tp"), None), P(("dp", "tp"), None, None)),
        check_vma=False,
    )
```

```python
import functools
import math

import jax
import jax.numpy as jnp
from jax import lax
from jax.experimental import pallas as pl
from jax.experimental.pallas import tpu as pltpu
from jax.sharding import PartitionSpec as P

HEADS = 64
HEAD_DIM = 64
EXPERT_HID = 2880
DEPTH = 8


THETA = 150000.0
SWIGLU_ALPHA = 1.702
EPSILON = 1e-05


def rms_norm(values, gain):
    floats = values.astype(jnp.float32)
    mean_sq = jnp.mean(floats * floats, axis=-1, keepdims=True)
    return (floats * lax.rsqrt(mean_sq + EPSILON) * gain).astype(jnp.bfloat16)


def tree_paths(parent_row, depth_limit):
    count = parent_row.shape[0]
    identity = jnp.eye(count, dtype=jnp.bool_)
    ancestry = identity
    for level in range(depth_limit):
        ancestry = identity | jnp.take(ancestry, parent_row, axis=0)
    depths = jnp.sum(ancestry.astype(jnp.int32), axis=1) - 1
    return (ancestry, depths)


def rotate(values, positions):
    half = values.shape[-1] // 2
    steps_f = jnp.arange(half).astype(jnp.float32)
    inverse = jnp.exp(steps_f * (-2.0 * math.log(THETA) / values.shape[-1]))
    angles = positions[:, None] * inverse[None, :]
    cosine = jnp.cos(angles)[:, None, :]
    sine = jnp.sin(angles)[:, None, :]
    first = values[..., :half].astype(jnp.float32)
    second = values[..., half:].astype(jnp.float32)
    turned = jnp.concatenate(
        [first * cosine - second * sine, second * cosine + first * sine], axis=-1
    )
    return turned.astype(jnp.bfloat16)


def prepare(query, keyval, length, parent_row, depth_limit):
    draft, heads, head_dim = query.shape
    kv_width = keyval.shape[1] // 2
    kv_heads = kv_width // head_dim
    ancestry, depths = tree_paths(parent_row, depth_limit)
    positions = (length + depths).astype(jnp.float32)
    query_rot = rotate(query, positions)
    new_keys = rotate(keyval[:, :kv_width].reshape(draft, kv_heads, head_dim), positions)
    new_values = keyval[:, kv_width:].reshape(draft, kv_heads, head_dim)
    grouped = query_rot.reshape(draft, kv_heads, heads // kv_heads, head_dim)
    draft_scores = jnp.einsum(
        "jgqd,kgd->gqjk", grouped, new_keys, preferred_element_type=jnp.float32
    ) * (1.0 / math.sqrt(head_dim))
    draft_scores = jnp.where(ancestry[None, None], draft_scores, -jnp.inf)
    return (grouped, new_keys, new_values, ancestry, depths, draft_scores)


def accept_rows(new_keys, new_values, ancestry, depths, leaf, depth_limit):
    draft = depths.shape[0]
    selector = ancestry[leaf][None, :] & (depths[None, :] == jnp.arange(depth_limit)[:, None])
    new_rows = jnp.concatenate([new_keys.reshape(draft, -1), new_values.reshape(draft, -1)], axis=1)
    return jnp.dot(
        selector.astype(jnp.bfloat16), new_rows, preferred_element_type=jnp.float32
    ).astype(jnp.bfloat16)


def finish(weighted, total, draft):
    return (
        (weighted / jnp.transpose(total, (2, 0, 1))[..., None])
        .astype(jnp.bfloat16)
        .reshape(draft, -1)
    )


def attend_padded(query, keyval, keys_cache, values_cache, length, parent_row, leaf, depth_limit):
    draft, heads, head_dim = query.shape
    grouped, new_keys, new_values, ancestry, depths, draft_scores = prepare(
        query, keyval, length, parent_row, depth_limit
    )
    slots = keys_cache.shape[0]
    kv_heads = new_keys.shape[1]
    cache_k = keys_cache.reshape(slots, kv_heads, head_dim)
    cache_v = values_cache.reshape(slots, kv_heads, head_dim)
    cache_scores = jnp.einsum(
        "jgqd,pgd->gqjp", grouped, cache_k, preferred_element_type=jnp.float32
    ) * (1.0 / math.sqrt(head_dim))
    live = jnp.arange(slots) < length
    cache_scores = jnp.where(live[None, None, None], cache_scores, -jnp.inf)
    top = jnp.maximum(jnp.max(draft_scores, axis=-1), jnp.max(cache_scores, axis=-1))
    draft_exp = jnp.exp(draft_scores - top[..., None])
    cache_exp = jnp.exp(cache_scores - top[..., None])
    total = jnp.sum(draft_exp, axis=-1) + jnp.sum(cache_exp, axis=-1)
    weighted = jnp.einsum(
        "gqjk,kgd->jgqd",
        draft_exp.astype(jnp.bfloat16),
        new_values,
        preferred_element_type=jnp.float32,
    )
    weighted = weighted + jnp.einsum(
        "gqjp,pgd->jgqd",
        cache_exp.astype(jnp.bfloat16),
        cache_v,
        preferred_element_type=jnp.float32,
    )
    return (
        finish(weighted, total, draft),
        accept_rows(new_keys, new_values, ancestry, depths, leaf, depth_limit),
    )


def gate_weights(inputs, router, routes):
    logits = jnp.dot(inputs, router, preferred_element_type=jnp.float32)
    onehot = routes[:, :, None] == jnp.arange(router.shape[1])[None, None, :]
    picked = jnp.sum(jnp.where(onehot, logits[:, None, :], 0.0), axis=2)
    return jax.nn.softmax(picked, axis=1).astype(jnp.bfloat16)


def expert_slots(inputs, weights, routes, expert, gate_rows, up_rows, down_rows, capacity):
    count = inputs.shape[0]
    match = routes == expert
    hits = jnp.any(match, axis=1)
    gate_of = jnp.sum(jnp.where(match, weights.astype(jnp.float32), 0.0), axis=1)
    slot_ids = jnp.cumsum(hits.astype(jnp.int32)) - 1
    target = jnp.where(hits, slot_ids, capacity)
    index = jnp.full((capacity,), count, jnp.int32).at[target].set(jnp.arange(count), mode="drop")
    valid = index < count
    safe = jnp.minimum(index, count - 1)
    picked = inputs[safe]
    gate_val = lax.dot_general(
        picked, gate_rows, (((1,), (1,)), ((), ())), preferred_element_type=jnp.float32
    )
    up_val = lax.dot_general(
        picked, up_rows, (((1,), (1,)), ((), ())), preferred_element_type=jnp.float32
    )
    active = (gate_val * jax.nn.sigmoid(SWIGLU_ALPHA * gate_val) * (up_val + 1.0)).astype(
        jnp.bfloat16
    )
    result = jnp.dot(active, down_rows, preferred_element_type=jnp.float32)
    scale_rows = jnp.where(valid, gate_of[safe], 0.0)
    return (result * scale_rows[:, None], index)


def local_general(
    hidden,
    attn_gain,
    w_query,
    w_keyval,
    w_out,
    cache_keys,
    cache_values,
    cache_lens,
    parents,
    accepted,
    moe_gain,
    w_router,
    routes,
    w_gate,
    w_up,
    w_down,
):
    devices = lax.axis_size("tp")
    index_me = lax.axis_index("tp")
    rows = hidden.shape[0]
    normed = rms_norm(hidden, attn_gain)
    local_query = w_query.shape[1]
    both_weights = jnp.concatenate([w_query, w_keyval], axis=1)
    projected = jnp.dot(
        lax.all_gather(normed, "tp", axis=0, tiled=True),
        both_weights,
        preferred_element_type=jnp.float32,
    ).astype(jnp.bfloat16)
    width = projected.shape[1]
    gathered_cols = lax.all_to_all(projected, "tp", split_axis=0, concat_axis=1, tiled=True)
    gathered_cols = gathered_cols.reshape(rows, devices, width)
    requests = cache_lens.shape[0]
    draft = parents.shape[1]
    query = gathered_cols[:, :, :local_query].reshape(requests, draft, HEADS, HEAD_DIM)
    keyval = gathered_cols[:, :, local_query:].reshape(
        requests, draft, devices * (width - local_query)
    )

    def per_request(items):
        return attend_padded(*items, DEPTH)

    attended, accepted_kv = lax.map(
        per_request, (query, keyval, cache_keys, cache_values, cache_lens, parents, accepted)
    )
    attended = attended.reshape(rows, HEADS * HEAD_DIM)
    head_cols = lax.all_to_all(attended, "tp", split_axis=1, concat_axis=0, tiled=True)
    attn_sum = lax.psum_scatter(
        jnp.dot(head_cols, w_out, preferred_element_type=jnp.float32),
        "tp",
        scatter_dimension=0,
        tiled=True,
    )
    middle = (hidden.astype(jnp.float32) + attn_sum).astype(jnp.bfloat16)
    moe_in = rms_norm(middle, moe_gain)
    all_inputs = lax.all_gather(moe_in, "tp", axis=0, tiled=True)
    all_weights = gate_weights(all_inputs, w_router, routes)
    units = w_down.shape[0]
    expert = index_me * units // EXPERT_HID
    count = all_inputs.shape[0]
    capacity = 2 * count * routes.shape[1] // w_router.shape[1]
    slot_rows, slot_index = expert_slots(
        all_inputs, all_weights, routes, expert, w_gate, w_up, w_down, capacity
    )
    term = (
        jnp.zeros((count, all_inputs.shape[1]), jnp.float32)
        .at[slot_index]
        .add(slot_rows, mode="drop")
    )
    mixed = lax.psum_scatter(
        term.astype(jnp.bfloat16), "tp", scatter_dimension=0, tiled=True
    ).astype(jnp.float32)
    layer_out = (middle.astype(jnp.float32) + mixed).astype(jnp.bfloat16)
    return (layer_out, accepted_kv)


NEGATIVE = -1e30
MIB = 1024 * 1024
VMEM_LIMIT = 24 * MIB
SCORE_STEP = 1024
VM = pl.BlockSpec(memory_space=pltpu.VMEM)
SM = pl.BlockSpec(memory_space=pltpu.SMEM)


def run(kernel, outs, args, scalars=1, scratch=(), flops=0, moved=0, limit=VMEM_LIMIT):
    return pl.pallas_call(
        kernel,
        out_shape=tuple(jax.ShapeDtypeStruct(s, t) for s, t in outs),
        in_specs=[SM] * scalars + [VM] * (len(args) - scalars),
        out_specs=tuple(VM for _ in outs),
        scratch_shapes=list(scratch),
        compiler_params=pltpu.CompilerParams(vmem_limit_bytes=limit),
        cost_estimate=pl.CostEstimate(flops=flops, bytes_accessed=moved, transcendentals=0),
    )(*args)


def near(values):
    return pltpu.with_memory_space_constraint(values, pltpu.VMEM)


def far(values):
    return pltpu.with_memory_space_constraint(values, pltpu.HBM)


def load(*arrays):
    def kernel(*refs):
        count = len(arrays)
        sources, targets, sems = refs[:count], refs[count : 2 * count], refs[2 * count]
        copies = [
            pltpu.make_async_copy(source, target, sems.at[i])
            for i, (source, target) in enumerate(zip(sources, targets))
        ]
        for copy in copies:
            copy.start()
        for copy in copies:
            copy.wait()

    moved = sum(a.size * a.dtype.itemsize for a in arrays)
    return pl.pallas_call(
        kernel,
        out_shape=tuple(pltpu.VMEM(a.shape, a.dtype) for a in arrays),
        in_specs=[pl.BlockSpec(memory_space=pl.ANY)] * len(arrays),
        out_specs=tuple(VM for _ in arrays),
        scratch_shapes=[pltpu.SemaphoreType.DMA((len(arrays),))],
        compiler_params=pltpu.CompilerParams(vmem_limit_bytes=MIB),
        cost_estimate=pl.CostEstimate(flops=0, bytes_accessed=2 * moved, transcendentals=0),
    )(*[far(a) for a in arrays])


def dot_nt(left, right):
    return lax.dot_general(
        left, right, (((1,), (1,)), ((), ())), preferred_element_type=jnp.float32
    )


def dot_tn(left, right):
    return lax.dot_general(
        left, right, (((0,), (0,)), ((), ())), preferred_element_type=jnp.float32
    )


def dot_nn(left, right):
    return jnp.dot(left, right, preferred_element_type=jnp.float32)


def iota(shape, dim):
    return lax.broadcasted_iota(jnp.int32, shape, dim)


def tree_kernel(lens, accepted, parents, cos_out, sin_out, bias_out, pick_out):
    wide = parents.shape[1]
    draft, lanes = cos_out.shape
    rows, cols = iota((wide, wide), 0), iota((wide, wide), 1)
    identity = (rows == cols).astype(jnp.bfloat16)
    step = jnp.maximum((parents[...] == rows).astype(jnp.bfloat16), identity)
    span = 1
    while span < DEPTH:
        step = (dot_nn(step, step) > 0.5).astype(jnp.bfloat16)
        span = span * 2
    ancestry = dot_tn(step, identity)
    depth_row = jnp.sum(step.astype(jnp.float32), axis=0, keepdims=True) - 1.0
    depth_col = jnp.sum(ancestry, axis=1, keepdims=True) - 1.0
    positions = depth_col[:draft] + lens[0].astype(jnp.float32)
    lane = iota((1, lanes), 1)
    powers = jnp.bitwise_and(lane, HEAD_DIM // 2 - 1).astype(jnp.float32)
    inverse = jnp.exp(powers * (-2.0 * math.log(THETA) / HEAD_DIM))
    angles = positions * inverse
    cos_out[...] = jnp.cos(angles)
    low = jnp.bitwise_and(lane, HEAD_DIM - 1) < HEAD_DIM // 2
    sine = jnp.sin(angles)
    sin_out[...] = jnp.where(low, -sine, sine)
    bias_out[...] = jnp.where(ancestry[:draft] > 0.5, 0.0, NEGATIVE)
    leaf_row = jnp.sum(jnp.where(rows == accepted[0], ancestry, 0.0), axis=0, keepdims=True)
    depths = iota(pick_out.shape, 0).astype(jnp.float32)
    pick_out[...] = jnp.where((depth_row == depths) & (leaf_row > 0.5), 1.0, 0.0)


def project_kernel(*refs):
    pieces, (gain, *weights), rest = refs[:4], refs[4:9], refs[9:]
    outs, normed = rest[:4], rest[4]
    count = pieces[0].shape[0]
    scale = gain[...].reshape(1, gain.shape[0])
    for k, piece in enumerate(pieces):
        floats = piece[...].astype(jnp.float32)
        mean_sq = jnp.mean(floats * floats, axis=-1, keepdims=True)
        normed[k * count : (k + 1) * count, :] = floats * lax.rsqrt(mean_sq + EPSILON) * scale
    rows = normed[...].astype(jnp.bfloat16)
    at = 0
    for weight in weights:
        result = dot_nn(rows, weight[...])
        width = weight.shape[1]
        for i, out in enumerate(outs):
            out[:, at : at + width] = result[count * i : count * (i + 1)].astype(jnp.bfloat16)
        at += width


def attend_kernel(*refs):
    me, lens = refs[0][0], refs[1][0]
    arrived = refs[2:6]
    cos, sin, bias, pick, keys, values = refs[6:12]
    outs, accepted_out = refs[12:16], refs[16]
    blocks, queries, new_keys, new_values, attended, held = refs[17:]
    draft = cos.shape[0]
    lanes = 2 * HEAD_DIM
    for i in range(4):
        columns = blocks.shape[2]
        blocks[me ^ (2 * i)] = arrived[i][:, :columns].astype(jnp.float32)
        blocks[me ^ (2 * i + 1)] = arrived[i][:, columns:].astype(jnp.float32)
    lane = iota((draft, lanes), 1)
    low = jnp.bitwise_and(lane, HEAD_DIM - 1) < HEAD_DIM // 2
    left = lane < HEAD_DIM
    cosine, sine, mask = cos[...], sin[...], bias[...]
    slots = keys.shape[0]
    step = SCORE_STEP
    live = jnp.where(iota((1, slots), 1) < lens, 0.0, NEGATIVE)

    def rope(tile):
        half = HEAD_DIM // 2
        partner = jnp.where(low, pltpu.roll(tile, lanes - half, 1), pltpu.roll(tile, half, 1))
        return (tile * cosine + partner * sine).astype(jnp.bfloat16).astype(jnp.float32)

    new_keys[...] = jnp.zeros_like(new_keys)
    new_values[...] = jnp.zeros_like(new_values)
    q_cols = blocks.shape[2] - lanes
    heads = q_cols // HEAD_DIM
    count = heads * draft
    groups = queries.shape[0] // count
    pairs, both = groups // 2, 2 * count

    def fill(pair):
        new_keys[pair, :draft, :] = rope(blocks[pair, :, q_cols:])
        new_values[pair, :draft, :] = blocks[groups // 2 + pair, :, q_cols:]
        for p in range(2):
            for t in range(heads // 2):
                tile = rope(blocks[2 * pair + p, :, t * lanes : (t + 1) * lanes]) * 0.125
                turned = pltpu.roll(tile, HEAD_DIM, 1)
                first, second = (tile, turned) if p == 0 else (turned, tile)
                keep = left if p == 0 else ~left
                at = (2 * pair + p) * count + 2 * t * draft
                queries[at : at + draft, :] = jnp.where(keep, first, 0.0)
                queries[at + draft : at + 2 * draft, :] = jnp.where(keep, second, 0.0)

    def columns_of(pair):
        return slice(pair * lanes, (pair + 1) * lanes)

    def asked(pair):
        return queries[pair * both : (pair + 1) * both, :].astype(jnp.bfloat16)

    def tiles(block):
        return [block[:, i : i + lanes] for i in range(0, block.shape[1], lanes)]

    def score(pair, at):
        chunk = dot_nt(asked(pair), keys[at : at + step, columns_of(pair)])
        chunk = chunk + live[:, at : at + step]
        held[pair % 2, :, at : at + step] = chunk
        return functools.reduce(jnp.maximum, tiles(chunk))

    def tree_score(pair):
        fresh = dot_nt(asked(pair), new_keys[pair].astype(jnp.bfloat16))
        return (fresh.reshape(2 * heads, draft, lanes) + mask[None]).reshape(fresh.shape)

    chunks = range(0, slots, step)
    for pair in range(pairs):
        fill(pair)
    fresh = tree_score(0)
    peak = functools.reduce(jnp.maximum, [fresh] + [score(0, at) for at in chunks])
    for pair in range(pairs):
        top = jnp.max(peak, axis=1, keepdims=True)
        weights = jnp.exp(fresh - top)
        total = weights
        mixed = dot_nn(weights.astype(jnp.bfloat16), new_values[pair].astype(jnp.bfloat16))
        if pair + 1 < pairs:
            fresh = peak = tree_score(pair + 1)
        for at in chunks:
            if pair + 1 < pairs:
                peak = jnp.maximum(peak, score(pair + 1, at))
            weights = jnp.exp(held[pair % 2, :, at : at + step] - top)
            total = total + functools.reduce(jnp.add, tiles(weights))
            part = dot_nn(weights.astype(jnp.bfloat16), values[at : at + step, columns_of(pair)])
            mixed = mixed + part
        mixed = mixed / jnp.sum(total, axis=1, keepdims=True)
        for p in range(2):
            for t in range(heads // 2):
                at = (p * heads + 2 * t) * draft
                first, second = mixed[at : at + draft], mixed[at + draft : at + 2 * draft]
                if p == 0:
                    tile = jnp.where(left, first, pltpu.roll(second, HEAD_DIM, 1))
                else:
                    tile = jnp.where(left, pltpu.roll(first, HEAD_DIM, 1), second)
                col = p * q_cols + t * lanes
                attended[pair, :, col : col + lanes] = tile
    picked = pick[...].astype(jnp.bfloat16)
    for pair in range(groups // 2):
        for half, fresh in enumerate((new_keys, new_values)):
            at = (half * (groups // 2) + pair) * lanes
            rows = dot_nn(picked, fresh[pair].astype(jnp.bfloat16))
            accepted_out[:, at : at + lanes] = rows.astype(jnp.bfloat16)
    for i, out in enumerate(outs):
        out[...] = attended[(me // 2) ^ i].astype(jnp.bfloat16)


def named_slots(routes, expert, first, count):
    tokens = routes.shape[1]
    hits = jnp.max((routes[...] == expert).astype(jnp.float32), axis=0, keepdims=True)
    upper = (iota((tokens, tokens), 0) <= iota((tokens, tokens), 1)).astype(jnp.bfloat16)
    wide = jnp.broadcast_to(hits, (16, tokens)).astype(jnp.bfloat16)
    order = dot_nn(wide, upper)[:1]
    place = iota((count, tokens), 0).astype(jnp.float32) + (first + 1).astype(jnp.float32)
    return jnp.where((order == place) & (hits > 0.5), 1.0, 0.0)


def residual_kernel(*refs):
    me, pieces, routes, out, rows = refs[0][0], refs[1:5], refs[5], refs[6], refs[7]
    count = pieces[0].shape[0]
    expert = me // 2
    rows[...] = jnp.zeros_like(rows)
    for i, piece in enumerate(pieces):
        at = pl.multiple_of((me ^ (2 * i)) * count, 8)
        rows[pl.ds(at, count), :] = piece[...].astype(jnp.float32)
    chosen = named_slots(routes, expert, expert * 0, out.shape[0]).astype(jnp.bfloat16)
    out[...] = dot_nn(chosen, rows[...].astype(jnp.bfloat16)).astype(jnp.bfloat16)


def outproj_kernel(*refs):
    me, pieces = refs[0][0], refs[1:9]
    w_own, w_other, routes = refs[9:12]
    own, sends = refs[12], refs[13:16]
    rows, chosen = refs[16:]
    count = pieces[0].shape[0]
    half = own.shape[0]
    core = me % 2
    for k, piece in enumerate(pieces):
        rows[pl.ds(pl.multiple_of((me ^ k) * count, 8), count), :] = piece[...].astype(jnp.float32)
    for i in range(4):
        chosen[i * half : (i + 1) * half, :] = named_slots(routes, (me // 2) ^ i, core * half, half)
    picked = dot_nn(chosen[...].astype(jnp.bfloat16), rows[...].astype(jnp.bfloat16))
    width = w_own.shape[1]
    low, high = picked[:, :width], picked[:, width:]
    first = jnp.where(core == 0, low, high).astype(jnp.bfloat16)
    second = jnp.where(core == 0, high, low).astype(jnp.bfloat16)
    summed = dot_nt(first, w_own[...]) + dot_nt(second, w_other[...])
    own[...] = summed[:half]
    for i, out in enumerate(sends):
        out[...] = summed[(i + 1) * half : (i + 2) * half].astype(jnp.bfloat16)


def token_kernel(*refs):
    me, pieces, (w_own, w_other, out, rows) = refs[0][0], refs[1:5], refs[5:]
    count = pieces[0].shape[0]
    core = me % 2
    for i, piece in enumerate(pieces):
        rows[i * count : (i + 1) * count, :] = piece[...].astype(jnp.float32)
    width = w_own.shape[1]
    low, high = rows[:, :width], rows[:, width:]
    first = jnp.where(core == 0, low, high).astype(jnp.bfloat16)
    second = jnp.where(core == 0, high, low).astype(jnp.bfloat16)
    out[...] = dot_nt(first, w_own[...]) + dot_nt(second, w_other[...])


def expert_kernel(me_ref, mine, theirs, kept, other, gain, *refs):
    router, routes, w_gate, w_up, w_down, out, rows, active = refs
    me = me_ref[0]
    core, expert = me % 2, me // 2
    half = mine.shape[0]
    rows[pl.ds(pl.multiple_of(core * half, 8), half), :] = mine[...].astype(jnp.float32)
    rows[pl.ds(pl.multiple_of((1 - core) * half, 8), half), :] = theirs[...].astype(jnp.float32)
    floats = rows[...] + kept[...].astype(jnp.float32) + other[...].astype(jnp.float32)
    floats = floats.astype(jnp.bfloat16).astype(jnp.float32)
    mean_sq = jnp.mean(floats * floats, axis=-1, keepdims=True)
    scale = gain[...].reshape(1, gain.shape[0])
    inputs = (floats * lax.rsqrt(mean_sq + EPSILON) * scale).astype(jnp.bfloat16)
    experts, tokens = router.shape[0], routes.shape[1]
    logits = dot_nt(inputs, router[...])
    chosen = named_slots(routes, expert, expert * 0, 2 * half).astype(jnp.bfloat16)
    named = jnp.zeros((experts, tokens), jnp.float32)
    for i in range(routes.shape[0]):
        named = jnp.maximum(
            named, (iota((experts, tokens), 0) == routes[i : i + 1, :]).astype(jnp.float32)
        )
    named = dot_nt(chosen, named.astype(jnp.bfloat16)) > 0.5
    logits = jnp.where(named, logits, NEGATIVE)
    odds = jnp.exp(logits - jnp.max(logits, axis=1, keepdims=True))
    here = named & (iota(logits.shape, 1) == expert)
    share = jnp.sum(jnp.where(here, odds, 0.0), axis=1, keepdims=True)
    share = (share / jnp.sum(odds, axis=1, keepdims=True)).astype(jnp.bfloat16).astype(jnp.float32)
    gate_val = dot_nt(inputs, w_gate[...])
    up_val = dot_nt(inputs, w_up[...])
    act = gate_val * jax.nn.sigmoid(SWIGLU_ALPHA * gate_val) * (up_val + 1.0)
    active[...] = act.astype(jnp.bfloat16)
    out[...] = (dot_nn(active[...], w_down[...]) * share).astype(jnp.bfloat16)


def combine_kernel(*refs):
    me, mine, theirs, routes, sums, hidden = refs[0][0], *refs[1:6]
    own, sends, rows = refs[6], refs[7:10], refs[10]
    count = hidden.shape[0]
    total = (mine[...].astype(jnp.float32) + theirs[...].astype(jnp.float32)).astype(jnp.bfloat16)
    expert = me // 2
    chosen = named_slots(routes, expert, expert * 0, total.shape[0]).astype(jnp.bfloat16)
    rows[...] = dot_tn(chosen, total)

    def of(i):
        start = pl.multiple_of((me ^ (2 * i)) * count, 8)
        return rows[pl.ds(start, count), :] + sums[i * count : (i + 1) * count, :]

    own[...] = of(0) + hidden[...].astype(jnp.float32)
    for i, out in enumerate(sends):
        out[...] = of(i + 1).astype(jnp.bfloat16)


def local_paired(
    hidden,
    attn_gain,
    w_query,
    w_keyval,
    w_out,
    cache_keys,
    cache_values,
    cache_lens,
    parents,
    accepted,
    moe_gain,
    w_router,
    routes,
    w_gate,
    w_up,
    w_down,
):
    devices = lax.axis_size("tp")
    me = lax.axis_index("tp").astype(jnp.int32).reshape(1)
    bf16, f32 = jnp.bfloat16, jnp.float32

    def spread(blocks):
        return [blocks[0], *(swap(blocks[i], 2 * i) for i in (2, 3, 1))]

    def swap(values, offset):
        return lax.ppermute(values, "tp", [(i, i ^ offset) for i in range(devices)])

    rows, width = hidden.shape
    tokens = routes.shape[0]
    draft = parents.shape[1]
    capacity = 2 * tokens * routes.shape[1] // w_router.shape[1]
    half = capacity // 2
    routes_t = routes.T
    router_t = w_router.T

    line = [hidden, *(swap(hidden, s) for s in (2, 6, 4))]
    lanes = 128
    parents = jnp.pad(parents, ((0, 0), (0, lanes - draft)))
    other_query, other_keyval = swap(w_query, 1), swap(w_keyval, 1)
    early = (parents, load(w_query, w_keyval))
    line, early = lax.optimization_barrier((line, early))
    line = [line[i] for i in (0, 1, 3, 2)]
    parents, (near_query, near_keyval) = early
    queries, keyvals = w_query.shape[1], w_keyval.shape[1]
    columns = queries + keyvals
    projected = run(
        project_kernel,
        [((rows, 2 * columns), bf16)] * 4,
        [
            *line,
            attn_gain,
            near(near_query),
            near(near_keyval),
            near(other_query),
            near(other_keyval),
        ],
        scalars=0,
        scratch=[pltpu.VMEM((4 * rows, width), f32)],
        limit=10 * MIB,
        flops=2 * tokens * width * columns,
        moved=width * columns * 2,
    )
    later = (line, w_out, cache_keys[0], cache_values[0], cache_lens)
    later, projected = lax.optimization_barrier((later, projected))
    line, w_pair, keys, values, lens = later
    arrived = spread(projected)
    tree = run(
        tree_kernel,
        [((draft, lanes), f32), ((draft, lanes), f32), ((draft, lanes), f32), ((DEPTH, lanes), f32)],
        [lens, accepted, parents],
        scalars=2,
        limit=4 * MIB,
    )
    w_other = swap(w_pair, 1)
    cached = load(keys, values)
    arrived, tree, cached = lax.optimization_barrier((arrived, tree, cached))
    arrived = [arrived[i] for i in (0, 3, 1, 2)]
    slots, kv_cols = cache_keys.shape[1:]
    attended = run(
        attend_kernel,
        [((rows, 2 * queries), bf16)] * 4 + [((DEPTH, 2 * kv_cols), bf16)],
        [me, cache_lens, *arrived, *tree, near(cached[0]), near(cached[1])],
        scalars=2,
        scratch=[
            pltpu.VMEM((devices, rows, columns), f32),
            pltpu.VMEM((rows * HEADS, lanes), f32),
            pltpu.VMEM((devices // 2, lanes, lanes), f32),
            pltpu.VMEM((devices // 2, lanes, lanes), f32),
            pltpu.VMEM((devices // 2, rows, 2 * queries), f32),
            pltpu.VMEM((2, rows * queries * 2 // HEAD_DIM, slots), f32),
        ],
        limit=16 * MIB,
        flops=4 * rows * HEADS * slots * HEAD_DIM,
        moved=4 * slots * kv_cols,
    )
    accepted_kv = attended[4][None]
    later = (w_out, w_other, me)
    (w_own, w_other, me_now), attended = lax.optimization_barrier((later, attended))
    straight = spread(attended)
    near_out = load(w_own.T, w_other.T)
    residual = run(
        residual_kernel,
        [((capacity, width), bf16)],
        [me_now, *line, routes_t],
        scratch=[pltpu.VMEM((tokens, width), f32)],
        limit=6 * MIB,
        flops=2 * half * tokens * width,
        moved=tokens * width * 4,
    )[0]
    own_crossed = swap(straight[0], 1)
    shadow = (near_out, residual, own_crossed)
    straight, (near_out, residual, own_crossed) = lax.optimization_barrier((straight, shadow))
    straight = [straight[i] for i in (0, 3, 1, 2)]
    crossed = [own_crossed, *(swap(block, 1) for block in straight[1:])]
    blocks = [block for pair in zip(straight, crossed) for block in pair]
    out_flops = 2 * 4 * half * 2 * queries * width
    dispatched = run(
        outproj_kernel,
        [((half, width), f32)] + [((half, width), bf16)] * 3,
        [me, *blocks, *map(near, near_out), routes_t],
        scratch=[pltpu.VMEM((tokens, 2 * queries), f32), pltpu.VMEM((4 * half, tokens), f32)],
        limit=10 * MIB,
        flops=out_flops,
        moved=4 * queries * width,
    )
    arrived = spread(dispatched)[1:]
    (me_then, residual, experts), _ = lax.optimization_barrier(
        ((me, residual, (w_gate, w_up, w_down)), dispatched[1])
    )
    residuals = (residual, swap(residual, 1))
    sums = run(
        token_kernel,
        [((4 * rows, width), f32)],
        [me_then, *straight, *map(near, near_out)],
        scratch=[pltpu.VMEM((4 * rows, 2 * queries), f32)],
        limit=6 * MIB,
        flops=out_flops,
        moved=4 * queries * width,
    )[0]
    near_weights = load(*experts)
    middle, arrived, sums, residuals, near_weights = lax.optimization_barrier(
        (dispatched[0], arrived, sums, residuals, near_weights)
    )
    for block in arrived:
        middle = middle + block.astype(f32)
    middle = middle.astype(bf16)
    expert_rows = run(
        expert_kernel,
        [((capacity, width), bf16)],
        [
            me,
            middle,
            swap(middle, 1),
            *residuals,
            moe_gain,
            router_t,
            routes_t,
            *map(near, near_weights),
        ],
        scratch=[pltpu.VMEM((capacity, width), f32), pltpu.VMEM((capacity, w_down.shape[0]), bf16)],
        limit=6 * MIB,
        flops=6 * capacity * width * w_down.shape[0],
        moved=6 * width * w_down.shape[0],
    )[0]
    combined = run(
        combine_kernel,
        [((rows, width), f32)] + [((rows, width), bf16)] * 3,
        [me, expert_rows, swap(expert_rows, 1), routes_t, sums, hidden],
        scratch=[pltpu.VMEM((tokens, width), f32)],
        flops=2 * capacity * tokens * width,
        moved=tokens * width * 4,
    )
    layer_out, *arrived = spread(combined)
    for block in arrived:
        layer_out = layer_out + block.astype(f32)
    return (layer_out.astype(bf16), accepted_kv)


def local(hidden, attn_gain, w_query, w_keyval, *rest):
    devices = lax.axis_size("tp")
    parents, units = rest[4], rest[11].shape[0]
    paired = (
        devices == 8
        and parents.shape[0] == 1
        and units * 2 == EXPERT_HID
        and w_query.shape[1] * devices == HEADS * HEAD_DIM
        and w_keyval.shape[1] == 2 * HEAD_DIM
    )
    return (local_paired if paired else local_general)(hidden, attn_gain, w_query, w_keyval, *rest)


def solution(mesh):
    return jax.shard_map(
        local,
        mesh=mesh,
        in_specs=(
            P(("dp", "tp"), None),
            P(),
            P(None, "tp"),
            P(None, "tp"),
            P("tp", None),
            P(("dp", "tp"), None, None),
            P(("dp", "tp"), None, None),
            P(("dp", "tp")),
            P(("dp", "tp"), None),
            P(("dp", "tp")),
            P(),
            P(),
            P("dp", None),
            P("tp", None),
            P("tp", None),
            P("tp", None),
        ),
        out_specs=(P(("dp", "tp"), None), P(("dp", "tp"), None, None)),
        check_vma=False,
    )
```

```python
import functools
import math

import jax
import jax.numpy as jnp
from jax import lax
from jax.experimental import pallas as pl
from jax.experimental.pallas import tpu as pltpu
from jax.sharding import PartitionSpec as P

HEADS = 64
HEAD_DIM = 64
EXPERT_HID = 2880
DEPTH = 8


THETA = 150000.0
SWIGLU_ALPHA = 1.702
EPSILON = 1e-05


def rms_norm(values, gain):
    floats = values.astype(jnp.float32)
    mean_sq = jnp.mean(floats * floats, axis=-1, keepdims=True)
    return (floats * lax.rsqrt(mean_sq + EPSILON) * gain).astype(jnp.bfloat16)


def tree_paths(parent_row, depth_limit):
    count = parent_row.shape[0]
    identity = jnp.eye(count, dtype=jnp.bool_)
    ancestry = identity
    for level in range(depth_limit):
        ancestry = identity | jnp.take(ancestry, parent_row, axis=0)
    depths = jnp.sum(ancestry.astype(jnp.int32), axis=1) - 1
    return (ancestry, depths)


def rotate(values, positions):
    half = values.shape[-1] // 2
    steps_f = jnp.arange(half).astype(jnp.float32)
    inverse = jnp.exp(steps_f * (-2.0 * math.log(THETA) / values.shape[-1]))
    angles = positions[:, None] * inverse[None, :]
    cosine = jnp.cos(angles)[:, None, :]
    sine = jnp.sin(angles)[:, None, :]
    first = values[..., :half].astype(jnp.float32)
    second = values[..., half:].astype(jnp.float32)
    turned = jnp.concatenate(
        [first * cosine - second * sine, second * cosine + first * sine], axis=-1
    )
    return turned.astype(jnp.bfloat16)


def prepare(query, keyval, length, parent_row, depth_limit):
    draft, heads, head_dim = query.shape
    kv_width = keyval.shape[1] // 2
    kv_heads = kv_width // head_dim
    ancestry, depths = tree_paths(parent_row, depth_limit)
    positions = (length + depths).astype(jnp.float32)
    query_rot = rotate(query, positions)
    new_keys = rotate(keyval[:, :kv_width].reshape(draft, kv_heads, head_dim), positions)
    new_values = keyval[:, kv_width:].reshape(draft, kv_heads, head_dim)
    grouped = query_rot.reshape(draft, kv_heads, heads // kv_heads, head_dim)
    draft_scores = jnp.einsum(
        "jgqd,kgd->gqjk", grouped, new_keys, preferred_element_type=jnp.float32
    ) * (1.0 / math.sqrt(head_dim))
    draft_scores = jnp.where(ancestry[None, None], draft_scores, -jnp.inf)
    return (grouped, new_keys, new_values, ancestry, depths, draft_scores)


def accept_rows(new_keys, new_values, ancestry, depths, leaf, depth_limit):
    draft = depths.shape[0]
    selector = ancestry[leaf][None, :] & (depths[None, :] == jnp.arange(depth_limit)[:, None])
    new_rows = jnp.concatenate([new_keys.reshape(draft, -1), new_values.reshape(draft, -1)], axis=1)
    return jnp.dot(
        selector.astype(jnp.bfloat16), new_rows, preferred_element_type=jnp.float32
    ).astype(jnp.bfloat16)


def finish(weighted, total, draft):
    return (
        (weighted / jnp.transpose(total, (2, 0, 1))[..., None])
        .astype(jnp.bfloat16)
        .reshape(draft, -1)
    )


def attend_padded(query, keyval, keys_cache, values_cache, length, parent_row, leaf, depth_limit):
    draft, heads, head_dim = query.shape
    grouped, new_keys, new_values, ancestry, depths, draft_scores = prepare(
        query, keyval, length, parent_row, depth_limit
    )
    slots = keys_cache.shape[0]
    kv_heads = new_keys.shape[1]
    cache_k = keys_cache.reshape(slots, kv_heads, head_dim)
    cache_v = values_cache.reshape(slots, kv_heads, head_dim)
    cache_scores = jnp.einsum(
        "jgqd,pgd->gqjp", grouped, cache_k, preferred_element_type=jnp.float32
    ) * (1.0 / math.sqrt(head_dim))
    live = jnp.arange(slots) < length
    cache_scores = jnp.where(live[None, None, None], cache_scores, -jnp.inf)
    top = jnp.maximum(jnp.max(draft_scores, axis=-1), jnp.max(cache_scores, axis=-1))
    draft_exp = jnp.exp(draft_scores - top[..., None])
    cache_exp = jnp.exp(cache_scores - top[..., None])
    total = jnp.sum(draft_exp, axis=-1) + jnp.sum(cache_exp, axis=-1)
    weighted = jnp.einsum(
        "gqjk,kgd->jgqd",
        draft_exp.astype(jnp.bfloat16),
        new_values,
        preferred_element_type=jnp.float32,
    )
    weighted = weighted + jnp.einsum(
        "gqjp,pgd->jgqd",
        cache_exp.astype(jnp.bfloat16),
        cache_v,
        preferred_element_type=jnp.float32,
    )
    return (
        finish(weighted, total, draft),
        accept_rows(new_keys, new_values, ancestry, depths, leaf, depth_limit),
    )


def gate_weights(inputs, router, routes):
    logits = jnp.dot(inputs, router, preferred_element_type=jnp.float32)
    onehot = routes[:, :, None] == jnp.arange(router.shape[1])[None, None, :]
    picked = jnp.sum(jnp.where(onehot, logits[:, None, :], 0.0), axis=2)
    return jax.nn.softmax(picked, axis=1).astype(jnp.bfloat16)


def expert_slots(inputs, weights, routes, expert, gate_rows, up_rows, down_rows, capacity):
    count = inputs.shape[0]
    match = routes == expert
    hits = jnp.any(match, axis=1)
    gate_of = jnp.sum(jnp.where(match, weights.astype(jnp.float32), 0.0), axis=1)
    slot_ids = jnp.cumsum(hits.astype(jnp.int32)) - 1
    target = jnp.where(hits, slot_ids, capacity)
    index = jnp.full((capacity,), count, jnp.int32).at[target].set(jnp.arange(count), mode="drop")
    valid = index < count
    safe = jnp.minimum(index, count - 1)
    picked = inputs[safe]
    gate_val = lax.dot_general(
        picked, gate_rows, (((1,), (1,)), ((), ())), preferred_element_type=jnp.float32
    )
    up_val = lax.dot_general(
        picked, up_rows, (((1,), (1,)), ((), ())), preferred_element_type=jnp.float32
    )
    active = (gate_val * jax.nn.sigmoid(SWIGLU_ALPHA * gate_val) * (up_val + 1.0)).astype(
        jnp.bfloat16
    )
    result = jnp.dot(active, down_rows, preferred_element_type=jnp.float32)
    scale_rows = jnp.where(valid, gate_of[safe], 0.0)
    return (result * scale_rows[:, None], index)


def local_general(
    hidden,
    attn_gain,
    w_query,
    w_keyval,
    w_out,
    cache_keys,
    cache_values,
    cache_lens,
    parents,
    accepted,
    moe_gain,
    w_router,
    routes,
    w_gate,
    w_up,
    w_down,
):
    devices = lax.axis_size("tp")
    index_me = lax.axis_index("tp")
    rows = hidden.shape[0]
    normed = rms_norm(hidden, attn_gain)
    local_query = w_query.shape[1]
    both_weights = jnp.concatenate([w_query, w_keyval], axis=1)
    projected = jnp.dot(
        lax.all_gather(normed, "tp", axis=0, tiled=True),
        both_weights,
        preferred_element_type=jnp.float32,
    ).astype(jnp.bfloat16)
    width = projected.shape[1]
    gathered_cols = lax.all_to_all(projected, "tp", split_axis=0, concat_axis=1, tiled=True)
    gathered_cols = gathered_cols.reshape(rows, devices, width)
    requests = cache_lens.shape[0]
    draft = parents.shape[1]
    query = gathered_cols[:, :, :local_query].reshape(requests, draft, HEADS, HEAD_DIM)
    keyval = gathered_cols[:, :, local_query:].reshape(
        requests, draft, devices * (width - local_query)
    )

    def per_request(items):
        return attend_padded(*items, DEPTH)

    attended, accepted_kv = lax.map(
        per_request, (query, keyval, cache_keys, cache_values, cache_lens, parents, accepted)
    )
    attended = attended.reshape(rows, HEADS * HEAD_DIM)
    head_cols = lax.all_to_all(attended, "tp", split_axis=1, concat_axis=0, tiled=True)
    attn_sum = lax.psum_scatter(
        jnp.dot(head_cols, w_out, preferred_element_type=jnp.float32),
        "tp",
        scatter_dimension=0,
        tiled=True,
    )
    middle = (hidden.astype(jnp.float32) + attn_sum).astype(jnp.bfloat16)
    moe_in = rms_norm(middle, moe_gain)
    all_inputs = lax.all_gather(moe_in, "tp", axis=0, tiled=True)
    all_weights = gate_weights(all_inputs, w_router, routes)
    units = w_down.shape[0]
    expert = index_me * units // EXPERT_HID
    count = all_inputs.shape[0]
    capacity = 2 * count * routes.shape[1] // w_router.shape[1]
    slot_rows, slot_index = expert_slots(
        all_inputs, all_weights, routes, expert, w_gate, w_up, w_down, capacity
    )
    term = (
        jnp.zeros((count, all_inputs.shape[1]), jnp.float32)
        .at[slot_index]
        .add(slot_rows, mode="drop")
    )
    mixed = lax.psum_scatter(
        term.astype(jnp.bfloat16), "tp", scatter_dimension=0, tiled=True
    ).astype(jnp.float32)
    layer_out = (middle.astype(jnp.float32) + mixed).astype(jnp.bfloat16)
    return (layer_out, accepted_kv)


NEGATIVE = -1e30
MIB = 1024 * 1024
VMEM_LIMIT = 24 * MIB
SCORE_STEP = 1024
VM = pl.BlockSpec(memory_space=pltpu.VMEM)
SM = pl.BlockSpec(memory_space=pltpu.SMEM)


def run(kernel, outs, args, scalars=1, scratch=(), flops=0, moved=0, limit=VMEM_LIMIT):
    return pl.pallas_call(
        kernel,
        out_shape=tuple(jax.ShapeDtypeStruct(s, t) for s, t in outs),
        in_specs=[SM] * scalars + [VM] * (len(args) - scalars),
        out_specs=tuple(VM for _ in outs),
        scratch_shapes=list(scratch),
        compiler_params=pltpu.CompilerParams(vmem_limit_bytes=limit),
        cost_estimate=pl.CostEstimate(flops=flops, bytes_accessed=moved, transcendentals=0),
    )(*args)


def near(values):
    return pltpu.with_memory_space_constraint(values, pltpu.VMEM)


def far(values):
    return pltpu.with_memory_space_constraint(values, pltpu.HBM)


def load(*arrays):
    def kernel(*refs):
        count = len(arrays)
        sources, targets, sems = refs[:count], refs[count : 2 * count], refs[2 * count]
        copies = [
            pltpu.make_async_copy(source, target, sems.at[i])
            for i, (source, target) in enumerate(zip(sources, targets))
        ]
        for copy in copies:
            copy.start()
        for copy in copies:
            copy.wait()

    moved = sum(a.size * a.dtype.itemsize for a in arrays)
    return pl.pallas_call(
        kernel,
        out_shape=tuple(pltpu.VMEM(a.shape, a.dtype) for a in arrays),
        in_specs=[pl.BlockSpec(memory_space=pl.ANY)] * len(arrays),
        out_specs=tuple(VM for _ in arrays),
        scratch_shapes=[pltpu.SemaphoreType.DMA((len(arrays),))],
        compiler_params=pltpu.CompilerParams(vmem_limit_bytes=MIB),
        cost_estimate=pl.CostEstimate(flops=0, bytes_accessed=2 * moved, transcendentals=0),
    )(*[far(a) for a in arrays])


def dot_nt(left, right):
    return lax.dot_general(
        left, right, (((1,), (1,)), ((), ())), preferred_element_type=jnp.float32
    )


def dot_tn(left, right):
    return lax.dot_general(
        left, right, (((0,), (0,)), ((), ())), preferred_element_type=jnp.float32
    )


def dot_nn(left, right):
    return jnp.dot(left, right, preferred_element_type=jnp.float32)


def iota(shape, dim):
    return lax.broadcasted_iota(jnp.int32, shape, dim)


def tree_kernel(lens, accepted, parents, cos_out, sin_out, bias_out, pick_out):
    wide = parents.shape[1]
    draft, lanes = cos_out.shape
    rows, cols = iota((wide, wide), 0), iota((wide, wide), 1)
    identity = (rows == cols).astype(jnp.bfloat16)
    step = jnp.maximum((parents[...] == rows).astype(jnp.bfloat16), identity)
    span = 1
    while span < DEPTH:
        step = (dot_nn(step, step) > 0.5).astype(jnp.bfloat16)
        span = span * 2
    ancestry = dot_tn(step, identity)
    depth_row = jnp.sum(step.astype(jnp.float32), axis=0, keepdims=True) - 1.0
    depth_col = jnp.sum(ancestry, axis=1, keepdims=True) - 1.0
    positions = depth_col[:draft] + lens[0].astype(jnp.float32)
    lane = iota((1, lanes), 1)
    powers = jnp.bitwise_and(lane, HEAD_DIM // 2 - 1).astype(jnp.float32)
    inverse = jnp.exp(powers * (-2.0 * math.log(THETA) / HEAD_DIM))
    angles = positions * inverse
    cos_out[...] = jnp.cos(angles)
    low = jnp.bitwise_and(lane, HEAD_DIM - 1) < HEAD_DIM // 2
    sine = jnp.sin(angles)
    sin_out[...] = jnp.where(low, -sine, sine)
    bias_out[...] = jnp.where(ancestry[:draft] > 0.5, 0.0, NEGATIVE)
    leaf_row = jnp.sum(jnp.where(rows == accepted[0], ancestry, 0.0), axis=0, keepdims=True)
    depths = iota(pick_out.shape, 0).astype(jnp.float32)
    pick_out[...] = jnp.where((depth_row == depths) & (leaf_row > 0.5), 1.0, 0.0)


def project_kernel(*refs):
    pieces, (gain, *weights), rest = refs[:4], refs[4:9], refs[9:]
    outs, normed = rest[:4], rest[4]
    count = pieces[0].shape[0]
    scale = gain[...].reshape(1, gain.shape[0])
    for k, piece in enumerate(pieces):
        floats = piece[...].astype(jnp.float32)
        mean_sq = jnp.mean(floats * floats, axis=-1, keepdims=True)
        normed[k * count : (k + 1) * count, :] = floats * lax.rsqrt(mean_sq + EPSILON) * scale
    rows = normed[...].astype(jnp.bfloat16)
    at = 0
    for weight in weights:
        result = dot_nn(rows, weight[...])
        width = weight.shape[1]
        for i, out in enumerate(outs):
            out[:, at : at + width] = result[count * i : count * (i + 1)].astype(jnp.bfloat16)
        at += width


def attend_kernel(ways, accept, *refs):
    me, lens = refs[0][0], refs[1][0]
    arrived = refs[2:6]
    cos, sin, bias, pick, keys, values = refs[6:12]
    outs, rest = refs[12 : 12 + len(ways)], list(refs[12 + len(ways) :])
    accepted_out = rest.pop(0) if accept else None
    blocks, queries, new_keys, new_values, held = rest
    draft = cos.shape[0]
    lanes = 2 * HEAD_DIM
    columns = blocks.shape[2]
    for i in range(4):
        blocks[me ^ (2 * i)] = arrived[i][:, :columns].astype(jnp.float32)
        blocks[me ^ (2 * i + 1)] = arrived[i][:, columns:].astype(jnp.float32)
    lane = iota((draft, lanes), 1)
    low = jnp.bitwise_and(lane, HEAD_DIM - 1) < HEAD_DIM // 2
    left = lane < HEAD_DIM
    cosine, sine, mask = cos[...], sin[...], bias[...]
    slots = keys.shape[0]
    step = SCORE_STEP
    live = jnp.where(iota((1, slots), 1) < lens, 0.0, NEGATIVE)

    def rope(tile):
        half = HEAD_DIM // 2
        partner = jnp.where(low, pltpu.roll(tile, lanes - half, 1), pltpu.roll(tile, half, 1))
        return (tile * cosine + partner * sine).astype(jnp.bfloat16).astype(jnp.float32)

    new_keys[...] = jnp.zeros_like(new_keys)
    new_values[...] = jnp.zeros_like(new_values)
    q_cols = columns - lanes
    heads = q_cols // HEAD_DIM
    count = heads * draft
    both = 2 * count
    pairs = [(me // 2) ^ way for way in ways]

    def columns_of(n):
        return pl.ds(pl.multiple_of(pairs[n] * lanes, lanes), lanes)

    def fill(n):
        new_keys[n, :draft, :] = rope(blocks[pairs[n], :, q_cols:])
        new_values[n, :draft, :] = blocks[4 + pairs[n], :, q_cols:]
        for p in range(2):
            for t in range(heads // 2):
                tile = rope(blocks[2 * pairs[n] + p, :, t * lanes : (t + 1) * lanes]) * 0.125
                turned = pltpu.roll(tile, HEAD_DIM, 1)
                first, second = (tile, turned) if p == 0 else (turned, tile)
                keep = left if p == 0 else ~left
                at = n * both + p * count + 2 * t * draft
                queries[at : at + draft, :] = jnp.where(keep, first, 0.0)
                queries[at + draft : at + 2 * draft, :] = jnp.where(keep, second, 0.0)

    def asked(n):
        return queries[n * both : (n + 1) * both, :].astype(jnp.bfloat16)

    def tiles(block):
        return [block[:, i : i + lanes] for i in range(0, block.shape[1], lanes)]

    def score(n, at):
        chunk = dot_nt(asked(n), keys[at : at + step, columns_of(n)])
        chunk = chunk + live[:, at : at + step]
        held[n % 2, :, at : at + step] = chunk
        return functools.reduce(jnp.maximum, tiles(chunk))

    def tree_score(n):
        fresh = dot_nt(asked(n), new_keys[n].astype(jnp.bfloat16))
        return (fresh.reshape(2 * heads, draft, lanes) + mask[None]).reshape(fresh.shape)

    chunks = range(0, slots, step)
    for n in range(len(ways)):
        fill(n)
    fresh = tree_score(0)
    peak = functools.reduce(jnp.maximum, [fresh] + [score(0, at) for at in chunks])
    for n, out in enumerate(outs):
        top = jnp.max(peak, axis=1, keepdims=True)
        weights = jnp.exp(fresh - top)
        total = weights
        mixed = dot_nn(weights.astype(jnp.bfloat16), new_values[n].astype(jnp.bfloat16))
        more = n + 1 < len(ways)
        if more:
            fresh = peak = tree_score(n + 1)
        for at in chunks:
            if more:
                peak = jnp.maximum(peak, score(n + 1, at))
            weights = jnp.exp(held[n % 2, :, at : at + step] - top)
            total = total + functools.reduce(jnp.add, tiles(weights))
            part = dot_nn(weights.astype(jnp.bfloat16), values[at : at + step, columns_of(n)])
            mixed = mixed + part
        mixed = mixed / jnp.sum(total, axis=1, keepdims=True)
        for p in range(2):
            for t in range(heads // 2):
                at = (p * heads + 2 * t) * draft
                first, second = mixed[at : at + draft], mixed[at + draft : at + 2 * draft]
                if p == 0:
                    tile = jnp.where(left, first, pltpu.roll(second, HEAD_DIM, 1))
                else:
                    tile = jnp.where(left, pltpu.roll(first, HEAD_DIM, 1), second)
                col = p * q_cols + t * lanes
                out[:, col : col + lanes] = tile.astype(jnp.bfloat16)
    if accept:
        picked = pick[...].astype(jnp.bfloat16)
        for pair in range(4):
            new_keys[0, :draft, :] = rope(blocks[pair, :, q_cols:])
            new_values[0, :draft, :] = blocks[4 + pair, :, q_cols:]
            for half, fresh in enumerate((new_keys, new_values)):
                at = (4 * half + pair) * lanes
                rows = dot_nn(picked, fresh[0].astype(jnp.bfloat16))
                accepted_out[:, at : at + lanes] = rows.astype(jnp.bfloat16)


def slot_order(routes, expert):
    tokens = routes.shape[1]
    hits = jnp.max((routes[...] == expert).astype(jnp.float32), axis=0, keepdims=True)
    upper = (iota((tokens, tokens), 0) <= iota((tokens, tokens), 1)).astype(jnp.bfloat16)
    wide = jnp.broadcast_to(hits, (16, tokens)).astype(jnp.bfloat16)
    return dot_nn(wide, upper)[:1] * hits


def slot_rows(order, first, count):
    place = iota((count, order.shape[1]), 0).astype(jnp.float32) + (first + 1).astype(jnp.float32)
    return jnp.where(order == place, 1.0, 0.0)


def slots_kernel(*refs):
    me, pieces, routes, rest = refs[0][0], refs[1:5], refs[5], refs[6:]
    kept, given, table, home, named_out, rows = rest
    core, expert = me % 2, me // 2
    count, half = pieces[0].shape[0], kept.shape[0]
    for i in range(4):
        order = slot_order(routes, expert ^ i)
        for side, first in enumerate((core * half, (1 - core) * half)):
            at = (4 * side + i) * half
            table[at : at + half, :] = slot_rows(order, first, half)
        if i == 0:
            chosen = slot_rows(order, expert * 0, 2 * half).astype(jnp.bfloat16)
    home[...] = chosen
    rows[...] = jnp.zeros_like(rows)
    for i, piece in enumerate(pieces):
        at = pl.multiple_of((me ^ (2 * i)) * count, 8)
        rows[pl.ds(at, count), :] = piece[...].astype(jnp.float32)
    found = rows[...].astype(jnp.bfloat16)
    kept[...] = dot_nn(table[:half, :].astype(jnp.bfloat16), found).astype(jnp.bfloat16)
    given[...] = dot_nn(table[4 * half : 5 * half, :].astype(jnp.bfloat16), found).astype(jnp.bfloat16)
    experts, tokens = named_out.shape[1], routes.shape[1]
    named = jnp.zeros((experts, tokens), jnp.float32)
    for i in range(routes.shape[0]):
        named = jnp.maximum(
            named, (iota((experts, tokens), 0) == routes[i : i + 1, :]).astype(jnp.float32)
        )
    named_out[...] = dot_nt(chosen, named.astype(jnp.bfloat16))


def pick_kernel(*refs):
    me, pieces, (table, kept, given, rows) = refs[0][0], refs[1:5], refs[5:]
    count = pieces[0].shape[0]
    rows[...] = jnp.zeros_like(rows)
    for i, piece in enumerate(pieces):
        at = pl.multiple_of((me ^ (2 * i)) * count, 8)
        rows[pl.ds(at, count), :] = piece[...].astype(jnp.float32)
    picked = dot_nn(table[...].astype(jnp.bfloat16), rows[...].astype(jnp.bfloat16))
    half = kept.shape[0]
    kept[...] = picked[:half].astype(jnp.bfloat16)
    given[...] = picked[half:].astype(jnp.bfloat16)


def outproj_kernel(me_ref, kept, taken, w_own, w_other, own, *sends):
    core = me_ref[0] % 2
    half, width = own.shape[0], w_own.shape[1]
    picked = kept[...].astype(jnp.float32) + taken[...].astype(jnp.float32)
    low, high = picked[:, :width], picked[:, width:]
    first = jnp.where(core == 0, low, high).astype(jnp.bfloat16)
    second = jnp.where(core == 0, high, low).astype(jnp.bfloat16)
    summed = dot_nt(first, w_own[...]) + dot_nt(second, w_other[...])
    own[...] = summed[:half]
    for i, out in enumerate(sends):
        out[...] = summed[(i + 1) * half : (i + 2) * half].astype(jnp.bfloat16)


def token_kernel(*refs):
    me, pieces, (w_own, w_other, out, rows) = refs[0][0], refs[1:5], refs[5:]
    count = pieces[0].shape[0]
    core = me % 2
    for i, piece in enumerate(pieces):
        rows[i * count : (i + 1) * count, :] = piece[...].astype(jnp.float32)
    width = w_own.shape[1]
    low, high = rows[:, :width], rows[:, width:]
    first = jnp.where(core == 0, low, high).astype(jnp.bfloat16)
    second = jnp.where(core == 0, high, low).astype(jnp.bfloat16)
    out[...] = dot_nt(first, w_own[...]) + dot_nt(second, w_other[...])


def expert_kernel(me_ref, mine, theirs, gain, *refs):
    router, named_ref, w_gate, w_up, w_down, out, rows, active = refs
    me = me_ref[0]
    core, expert = me % 2, me // 2
    half = mine.shape[0]
    rows[pl.ds(pl.multiple_of(core * half, 8), half), :] = mine[...].astype(jnp.float32)
    rows[pl.ds(pl.multiple_of((1 - core) * half, 8), half), :] = theirs[...].astype(jnp.float32)
    floats = rows[...]
    mean_sq = jnp.mean(floats * floats, axis=-1, keepdims=True)
    scale = gain[...].reshape(1, gain.shape[0])
    inputs = (floats * lax.rsqrt(mean_sq + EPSILON) * scale).astype(jnp.bfloat16)
    named = named_ref[...] > 0.5
    logits = jnp.where(named, dot_nt(inputs, router[...]), NEGATIVE)
    odds = jnp.exp(logits - jnp.max(logits, axis=1, keepdims=True))
    here = named & (iota(logits.shape, 1) == expert)
    share = jnp.sum(jnp.where(here, odds, 0.0), axis=1, keepdims=True)
    share = (share / jnp.sum(odds, axis=1, keepdims=True)).astype(jnp.bfloat16).astype(jnp.float32)
    gate_val = dot_nt(inputs, w_gate[...])
    up_val = dot_nt(inputs, w_up[...])
    act = gate_val * jax.nn.sigmoid(SWIGLU_ALPHA * gate_val) * (up_val + 1.0)
    active[...] = act.astype(jnp.bfloat16)
    out[...] = (dot_nn(active[...], w_down[...]) * share).astype(jnp.bfloat16)


def combine_kernel(me_ref, mine, theirs, home, sums, hidden, own, *refs):
    sends, rows = refs[:3], refs[3]
    me = me_ref[0]
    count = hidden.shape[0]
    total = (mine[...].astype(jnp.float32) + theirs[...].astype(jnp.float32)).astype(jnp.bfloat16)
    rows[...] = dot_tn(home[...], total)

    def of(i):
        start = pl.multiple_of((me ^ (2 * i)) * count, 8)
        return rows[pl.ds(start, count), :] + sums[i * count : (i + 1) * count, :]

    own[...] = of(0) + hidden[...].astype(jnp.float32)
    for i, out in enumerate(sends):
        out[...] = of(i + 1).astype(jnp.bfloat16)


def local_paired(
    hidden,
    attn_gain,
    w_query,
    w_keyval,
    w_out,
    cache_keys,
    cache_values,
    cache_lens,
    parents,
    accepted,
    moe_gain,
    w_router,
    routes,
    w_gate,
    w_up,
    w_down,
):
    devices = lax.axis_size("tp")
    me = lax.axis_index("tp").astype(jnp.int32).reshape(1)
    bf16, f32 = jnp.bfloat16, jnp.float32

    def spread(blocks, order):
        return [blocks[0], *(swap(blocks[i], 2 * i) for i in order)]

    def swap(values, offset):
        return lax.ppermute(values, "tp", [(i, i ^ offset) for i in range(devices)])

    rows, width = hidden.shape
    tokens = routes.shape[0]
    draft = parents.shape[1]
    capacity = 2 * tokens * routes.shape[1] // w_router.shape[1]
    half = capacity // 2
    routes_t = routes.T
    router_t = w_router.T

    line = [hidden, *(swap(hidden, s) for s in (2, 6, 4))]
    lanes = 128
    parents = jnp.pad(parents, ((0, 0), (0, lanes - draft)))
    other_query, other_keyval = swap(w_query, 1), swap(w_keyval, 1)
    early = (parents, load(w_query, w_keyval))
    line, early = lax.optimization_barrier((line, early))
    line = [line[i] for i in (0, 1, 3, 2)]
    parents, (near_query, near_keyval) = early
    queries, keyvals = w_query.shape[1], w_keyval.shape[1]
    columns = queries + keyvals
    projected = run(
        project_kernel,
        [((rows, 2 * columns), bf16)] * 4,
        [
            *line,
            attn_gain,
            near(near_query),
            near(near_keyval),
            near(other_query),
            near(other_keyval),
        ],
        scalars=0,
        scratch=[pltpu.VMEM((4 * rows, width), f32)],
        limit=10 * MIB,
        flops=2 * tokens * width * columns,
        moved=width * columns * 2,
    )
    later = (line, w_out, cache_keys[0], cache_values[0], cache_lens)
    later, projected = lax.optimization_barrier((later, projected))
    line, w_pair, keys, values, lens = later
    arrived = spread(projected, (2, 1, 3))
    tree = run(
        tree_kernel,
        [((draft, lanes), f32), ((draft, lanes), f32), ((draft, lanes), f32), ((DEPTH, lanes), f32)],
        [lens, accepted, parents],
        scalars=2,
        limit=4 * MIB,
    )
    w_other = swap(w_pair, 1)
    cached = load(keys, values)
    slotted = run(
        slots_kernel,
        [
            ((half, width), bf16),
            ((half, width), bf16),
            ((8 * half, tokens), f32),
            ((capacity, tokens), bf16),
            ((capacity, w_router.shape[1]), f32),
        ],
        [me, *line, routes_t],
        scratch=[pltpu.VMEM((tokens, width), f32)],
        limit=6 * MIB,
        flops=4 * half * tokens * width,
        moved=tokens * width * 4,
    )
    shadow = (tree, cached, slotted)
    arrived, shadow = lax.optimization_barrier((arrived, shadow))
    tree, cached, (kept, given, table, home, named) = shadow
    taken = swap(given, 1)
    arrived = [arrived[i] for i in (0, 2, 1, 3)]
    slots, kv_cols = cache_keys.shape[1:]
    def attend(inputs, ways, accept):
        outs = [((rows, 2 * queries), bf16)] * len(ways)
        per_way = rows * queries * 2 // HEAD_DIM
        return run(
            functools.partial(attend_kernel, ways, accept),
            outs + [((DEPTH, 2 * kv_cols), bf16)] * accept,
            inputs,
            scalars=2,
            scratch=[
                pltpu.VMEM((devices, rows, columns), f32),
                pltpu.VMEM((len(ways) * per_way, lanes), f32),
                pltpu.VMEM((len(ways), lanes, lanes), f32),
                pltpu.VMEM((len(ways), lanes, lanes), f32),
                pltpu.VMEM((min(len(ways), 2), per_way, slots), f32),
            ],
            limit=16 * MIB,
            flops=len(ways) * rows * HEADS * slots * HEAD_DIM,
            moved=len(ways) * slots * kv_cols,
        )

    lengths = cache_lens
    inputs = [me, lengths, *arrived, *tree, near(cached[0]), near(cached[1])]
    attended = attend(inputs, (1, 2, 3), False)
    later = (w_out, w_other, me, lengths)
    later, attended, taken = lax.optimization_barrier((later, attended, taken))
    w_own, w_other, me_now, lengths = later
    inputs[:2] = [me_now, lengths]
    own, accepted_kv = attend(inputs, (0,), True)
    straight = spread([own, *attended], (2, 3, 1))
    accepted_kv = accepted_kv[None]
    near_out = load(w_own.T, w_other.T)
    straight, near_out = lax.optimization_barrier((straight, near_out))
    straight = [straight[i] for i in (0, 3, 1, 2)]
    picked = run(
        pick_kernel,
        [((4 * half, 2 * queries), bf16)] * 2,
        [me, *straight, table],
        scratch=[pltpu.VMEM((tokens, 2 * queries), f32)],
        limit=6 * MIB,
        flops=16 * half * tokens * 2 * queries,
        moved=8 * half * 2 * queries * 2,
    )
    out_flops = 2 * 4 * half * 2 * queries * width
    dispatched = run(
        outproj_kernel,
        [((half, width), f32)] + [((half, width), bf16)] * 3,
        [me, picked[0], swap(picked[1], 1), *map(near, near_out)],
        limit=10 * MIB,
        flops=out_flops,
        moved=4 * queries * width,
    )
    arrived = spread(dispatched, (2, 3, 1))[1:]
    (me_then, experts), _ = lax.optimization_barrier(
        ((me, (w_gate, w_up, w_down)), dispatched[1])
    )
    sums = run(
        token_kernel,
        [((4 * rows, width), f32)],
        [me_then, *straight, *map(near, near_out)],
        scratch=[pltpu.VMEM((4 * rows, 2 * queries), f32)],
        limit=6 * MIB,
        flops=out_flops,
        moved=4 * queries * width,
    )[0]
    near_weights = load(*experts)
    middle, arrived, sums, taken, near_weights = lax.optimization_barrier(
        (dispatched[0], arrived, sums, taken, near_weights)
    )
    arrived = [kept, taken, *arrived]
    for block in arrived:
        middle = middle + block.astype(f32)
    middle = middle.astype(bf16)
    expert_rows = run(
        expert_kernel,
        [((capacity, width), bf16)],
        [
            me,
            middle,
            swap(middle, 1),
            moe_gain,
            router_t,
            named,
            *map(near, near_weights),
        ],
        scratch=[pltpu.VMEM((capacity, width), f32), pltpu.VMEM((capacity, w_down.shape[0]), bf16)],
        limit=6 * MIB,
        flops=6 * capacity * width * w_down.shape[0],
        moved=6 * width * w_down.shape[0],
    )[0]
    combined = run(
        combine_kernel,
        [((rows, width), f32)] + [((rows, width), bf16)] * 3,
        [me, expert_rows, swap(expert_rows, 1), home, sums, hidden],
        scratch=[pltpu.VMEM((tokens, width), f32)],
        flops=2 * capacity * tokens * width,
        moved=tokens * width * 4,
    )
    layer_out, *arrived = spread(combined, (2, 3, 1))
    for block in arrived:
        layer_out = layer_out + block.astype(f32)
    return (layer_out.astype(bf16), accepted_kv)


def local(hidden, attn_gain, w_query, w_keyval, *rest):
    devices = lax.axis_size("tp")
    parents, units = rest[4], rest[11].shape[0]
    paired = (
        devices == 8
        and parents.shape[0] == 1
        and units * 2 == EXPERT_HID
        and w_query.shape[1] * devices == HEADS * HEAD_DIM
        and w_keyval.shape[1] == 2 * HEAD_DIM
    )
    return (local_paired if paired else local_general)(hidden, attn_gain, w_query, w_keyval, *rest)


def solution(mesh):
    return jax.shard_map(
        local,
        mesh=mesh,
        in_specs=(
            P(("dp", "tp"), None),
            P(),
            P(None, "tp"),
            P(None, "tp"),
            P("tp", None),
            P(("dp", "tp"), None, None),
            P(("dp", "tp"), None, None),
            P(("dp", "tp")),
            P(("dp", "tp"), None),
            P(("dp", "tp")),
            P(),
            P(),
            P("dp", None),
            P("tp", None),
            P("tp", None),
            P("tp", None),
        ),
        out_specs=(P(("dp", "tp"), None), P(("dp", "tp"), None, None)),
        check_vma=False,
    )
```

```python
import functools
import math

import jax
import jax.numpy as jnp
from jax import lax
from jax.experimental import pallas as pl
from jax.experimental.pallas import tpu as pltpu
from jax.sharding import PartitionSpec as P

HEADS = 64
HEAD_DIM = 64
EXPERT_HID = 2880
DEPTH = 8


THETA = 150000.0
SWIGLU_ALPHA = 1.702
EPSILON = 1e-05


def rms_norm(values, gain):
    floats = values.astype(jnp.float32)
    mean_sq = jnp.mean(floats * floats, axis=-1, keepdims=True)
    return (floats * lax.rsqrt(mean_sq + EPSILON) * gain).astype(jnp.bfloat16)


def tree_paths(parent_row, depth_limit):
    count = parent_row.shape[0]
    identity = jnp.eye(count, dtype=jnp.bool_)
    ancestry = identity
    for level in range(depth_limit):
        ancestry = identity | jnp.take(ancestry, parent_row, axis=0)
    depths = jnp.sum(ancestry.astype(jnp.int32), axis=1) - 1
    return (ancestry, depths)


def rotate(values, positions):
    half = values.shape[-1] // 2
    steps_f = jnp.arange(half).astype(jnp.float32)
    inverse = jnp.exp(steps_f * (-2.0 * math.log(THETA) / values.shape[-1]))
    angles = positions[:, None] * inverse[None, :]
    cosine = jnp.cos(angles)[:, None, :]
    sine = jnp.sin(angles)[:, None, :]
    first = values[..., :half].astype(jnp.float32)
    second = values[..., half:].astype(jnp.float32)
    turned = jnp.concatenate(
        [first * cosine - second * sine, second * cosine + first * sine], axis=-1
    )
    return turned.astype(jnp.bfloat16)


def prepare(query, keyval, length, parent_row, depth_limit):
    draft, heads, head_dim = query.shape
    kv_width = keyval.shape[1] // 2
    kv_heads = kv_width // head_dim
    ancestry, depths = tree_paths(parent_row, depth_limit)
    positions = (length + depths).astype(jnp.float32)
    query_rot = rotate(query, positions)
    new_keys = rotate(keyval[:, :kv_width].reshape(draft, kv_heads, head_dim), positions)
    new_values = keyval[:, kv_width:].reshape(draft, kv_heads, head_dim)
    grouped = query_rot.reshape(draft, kv_heads, heads // kv_heads, head_dim)
    draft_scores = jnp.einsum(
        "jgqd,kgd->gqjk", grouped, new_keys, preferred_element_type=jnp.float32
    ) * (1.0 / math.sqrt(head_dim))
    draft_scores = jnp.where(ancestry[None, None], draft_scores, -jnp.inf)
    return (grouped, new_keys, new_values, ancestry, depths, draft_scores)


def accept_rows(new_keys, new_values, ancestry, depths, leaf, depth_limit):
    draft = depths.shape[0]
    selector = ancestry[leaf][None, :] & (depths[None, :] == jnp.arange(depth_limit)[:, None])
    new_rows = jnp.concatenate([new_keys.reshape(draft, -1), new_values.reshape(draft, -1)], axis=1)
    return jnp.dot(
        selector.astype(jnp.bfloat16), new_rows, preferred_element_type=jnp.float32
    ).astype(jnp.bfloat16)


def finish(weighted, total, draft):
    return (
        (weighted / jnp.transpose(total, (2, 0, 1))[..., None])
        .astype(jnp.bfloat16)
        .reshape(draft, -1)
    )


def attend_padded(query, keyval, keys_cache, values_cache, length, parent_row, leaf, depth_limit):
    draft, heads, head_dim = query.shape
    grouped, new_keys, new_values, ancestry, depths, draft_scores = prepare(
        query, keyval, length, parent_row, depth_limit
    )
    slots = keys_cache.shape[0]
    kv_heads = new_keys.shape[1]
    cache_k = keys_cache.reshape(slots, kv_heads, head_dim)
    cache_v = values_cache.reshape(slots, kv_heads, head_dim)
    cache_scores = jnp.einsum(
        "jgqd,pgd->gqjp", grouped, cache_k, preferred_element_type=jnp.float32
    ) * (1.0 / math.sqrt(head_dim))
    live = jnp.arange(slots) < length
    cache_scores = jnp.where(live[None, None, None], cache_scores, -jnp.inf)
    top = jnp.maximum(jnp.max(draft_scores, axis=-1), jnp.max(cache_scores, axis=-1))
    draft_exp = jnp.exp(draft_scores - top[..., None])
    cache_exp = jnp.exp(cache_scores - top[..., None])
    total = jnp.sum(draft_exp, axis=-1) + jnp.sum(cache_exp, axis=-1)
    weighted = jnp.einsum(
        "gqjk,kgd->jgqd",
        draft_exp.astype(jnp.bfloat16),
        new_values,
        preferred_element_type=jnp.float32,
    )
    weighted = weighted + jnp.einsum(
        "gqjp,pgd->jgqd",
        cache_exp.astype(jnp.bfloat16),
        cache_v,
        preferred_element_type=jnp.float32,
    )
    return (
        finish(weighted, total, draft),
        accept_rows(new_keys, new_values, ancestry, depths, leaf, depth_limit),
    )


def gate_weights(inputs, router, routes):
    logits = jnp.dot(inputs, router, preferred_element_type=jnp.float32)
    onehot = routes[:, :, None] == jnp.arange(router.shape[1])[None, None, :]
    picked = jnp.sum(jnp.where(onehot, logits[:, None, :], 0.0), axis=2)
    return jax.nn.softmax(picked, axis=1).astype(jnp.bfloat16)


def expert_slots(inputs, weights, routes, expert, gate_rows, up_rows, down_rows, capacity):
    count = inputs.shape[0]
    match = routes == expert
    hits = jnp.any(match, axis=1)
    gate_of = jnp.sum(jnp.where(match, weights.astype(jnp.float32), 0.0), axis=1)
    slot_ids = jnp.cumsum(hits.astype(jnp.int32)) - 1
    target = jnp.where(hits, slot_ids, capacity)
    index = jnp.full((capacity,), count, jnp.int32).at[target].set(jnp.arange(count), mode="drop")
    valid = index < count
    safe = jnp.minimum(index, count - 1)
    picked = inputs[safe]
    gate_val = lax.dot_general(
        picked, gate_rows, (((1,), (1,)), ((), ())), preferred_element_type=jnp.float32
    )
    up_val = lax.dot_general(
        picked, up_rows, (((1,), (1,)), ((), ())), preferred_element_type=jnp.float32
    )
    active = (gate_val * jax.nn.sigmoid(SWIGLU_ALPHA * gate_val) * (up_val + 1.0)).astype(
        jnp.bfloat16
    )
    result = jnp.dot(active, down_rows, preferred_element_type=jnp.float32)
    scale_rows = jnp.where(valid, gate_of[safe], 0.0)
    return (result * scale_rows[:, None], index)


def local_general(
    hidden,
    attn_gain,
    w_query,
    w_keyval,
    w_out,
    cache_keys,
    cache_values,
    cache_lens,
    parents,
    accepted,
    moe_gain,
    w_router,
    routes,
    w_gate,
    w_up,
    w_down,
):
    devices = lax.axis_size("tp")
    index_me = lax.axis_index("tp")
    rows = hidden.shape[0]
    normed = rms_norm(hidden, attn_gain)
    local_query = w_query.shape[1]
    both_weights = jnp.concatenate([w_query, w_keyval], axis=1)
    projected = jnp.dot(
        lax.all_gather(normed, "tp", axis=0, tiled=True),
        both_weights,
        preferred_element_type=jnp.float32,
    ).astype(jnp.bfloat16)
    width = projected.shape[1]
    gathered_cols = lax.all_to_all(projected, "tp", split_axis=0, concat_axis=1, tiled=True)
    gathered_cols = gathered_cols.reshape(rows, devices, width)
    requests = cache_lens.shape[0]
    draft = parents.shape[1]
    query = gathered_cols[:, :, :local_query].reshape(requests, draft, HEADS, HEAD_DIM)
    keyval = gathered_cols[:, :, local_query:].reshape(
        requests, draft, devices * (width - local_query)
    )

    def per_request(items):
        return attend_padded(*items, DEPTH)

    attended, accepted_kv = lax.map(
        per_request, (query, keyval, cache_keys, cache_values, cache_lens, parents, accepted)
    )
    attended = attended.reshape(rows, HEADS * HEAD_DIM)
    head_cols = lax.all_to_all(attended, "tp", split_axis=1, concat_axis=0, tiled=True)
    attn_sum = lax.psum_scatter(
        jnp.dot(head_cols, w_out, preferred_element_type=jnp.float32),
        "tp",
        scatter_dimension=0,
        tiled=True,
    )
    middle = (hidden.astype(jnp.float32) + attn_sum).astype(jnp.bfloat16)
    moe_in = rms_norm(middle, moe_gain)
    all_inputs = lax.all_gather(moe_in, "tp", axis=0, tiled=True)
    all_weights = gate_weights(all_inputs, w_router, routes)
    units = w_down.shape[0]
    expert = index_me * units // EXPERT_HID
    count = all_inputs.shape[0]
    capacity = 2 * count * routes.shape[1] // w_router.shape[1]
    slot_rows, slot_index = expert_slots(
        all_inputs, all_weights, routes, expert, w_gate, w_up, w_down, capacity
    )
    term = (
        jnp.zeros((count, all_inputs.shape[1]), jnp.float32)
        .at[slot_index]
        .add(slot_rows, mode="drop")
    )
    mixed = lax.psum_scatter(
        term.astype(jnp.bfloat16), "tp", scatter_dimension=0, tiled=True
    ).astype(jnp.float32)
    layer_out = (middle.astype(jnp.float32) + mixed).astype(jnp.bfloat16)
    return (layer_out, accepted_kv)


NEGATIVE = -1e30
MIB = 1024 * 1024
VMEM_LIMIT = 24 * MIB
SCORE_STEP = 1024
VM = pl.BlockSpec(memory_space=pltpu.VMEM)
SM = pl.BlockSpec(memory_space=pltpu.SMEM)


def run(kernel, outs, args, scalars=1, scratch=(), flops=0, moved=0, limit=VMEM_LIMIT):
    return pl.pallas_call(
        kernel,
        out_shape=tuple(jax.ShapeDtypeStruct(s, t) for s, t in outs),
        in_specs=[SM] * scalars + [VM] * (len(args) - scalars),
        out_specs=tuple(VM for _ in outs),
        scratch_shapes=list(scratch),
        compiler_params=pltpu.CompilerParams(vmem_limit_bytes=limit),
        cost_estimate=pl.CostEstimate(flops=flops, bytes_accessed=moved, transcendentals=0),
    )(*args)


def near(values):
    return pltpu.with_memory_space_constraint(values, pltpu.VMEM)


def far(values):
    return pltpu.with_memory_space_constraint(values, pltpu.HBM)


def load(*arrays):
    def kernel(*refs):
        count = len(arrays)
        sources, targets, sems = refs[:count], refs[count : 2 * count], refs[2 * count]
        copies = [
            pltpu.make_async_copy(source, target, sems.at[i])
            for i, (source, target) in enumerate(zip(sources, targets))
        ]
        for copy in copies:
            copy.start()
        for copy in copies:
            copy.wait()

    moved = sum(a.size * a.dtype.itemsize for a in arrays)
    return pl.pallas_call(
        kernel,
        out_shape=tuple(pltpu.VMEM(a.shape, a.dtype) for a in arrays),
        in_specs=[pl.BlockSpec(memory_space=pl.ANY)] * len(arrays),
        out_specs=tuple(VM for _ in arrays),
        scratch_shapes=[pltpu.SemaphoreType.DMA((len(arrays),))],
        compiler_params=pltpu.CompilerParams(vmem_limit_bytes=MIB),
        cost_estimate=pl.CostEstimate(flops=0, bytes_accessed=2 * moved, transcendentals=0),
    )(*[far(a) for a in arrays])


def dot_nt(left, right):
    return lax.dot_general(
        left, right, (((1,), (1,)), ((), ())), preferred_element_type=jnp.float32
    )


def dot_tn(left, right):
    return lax.dot_general(
        left, right, (((0,), (0,)), ((), ())), preferred_element_type=jnp.float32
    )


def dot_nn(left, right):
    return jnp.dot(left, right, preferred_element_type=jnp.float32)


def iota(shape, dim):
    return lax.broadcasted_iota(jnp.int32, shape, dim)


def tree_kernel(lens, accepted, parents, cos_out, sin_out, bias_out, pick_out):
    wide = parents.shape[1]
    draft, lanes = cos_out.shape
    rows, cols = iota((wide, wide), 0), iota((wide, wide), 1)
    identity = (rows == cols).astype(jnp.bfloat16)
    step = jnp.maximum((parents[...] == rows).astype(jnp.bfloat16), identity)
    span = 1
    while span < DEPTH:
        step = (dot_nn(step, step) > 0.5).astype(jnp.bfloat16)
        span = span * 2
    ancestry = dot_tn(step, identity)
    depth_row = jnp.sum(step.astype(jnp.float32), axis=0, keepdims=True) - 1.0
    depth_col = jnp.sum(ancestry, axis=1, keepdims=True) - 1.0
    positions = depth_col[:draft] + lens[0].astype(jnp.float32)
    lane = iota((1, lanes), 1)
    powers = jnp.bitwise_and(lane, HEAD_DIM // 2 - 1).astype(jnp.float32)
    inverse = jnp.exp(powers * (-2.0 * math.log(THETA) / HEAD_DIM))
    angles = positions * inverse
    cos_out[...] = jnp.cos(angles)
    low = jnp.bitwise_and(lane, HEAD_DIM - 1) < HEAD_DIM // 2
    sine = jnp.sin(angles)
    sin_out[...] = jnp.where(low, -sine, sine)
    bias_out[...] = jnp.where(ancestry[:draft] > 0.5, 0.0, NEGATIVE)
    leaf_row = jnp.sum(jnp.where(rows == accepted[0], ancestry, 0.0), axis=0, keepdims=True)
    depths = iota(pick_out.shape, 0).astype(jnp.float32)
    pick_out[...] = jnp.where((depth_row == depths) & (leaf_row > 0.5), 1.0, 0.0)


def project_kernel(*refs):
    pieces, (gain, *weights), rest = refs[:4], refs[4:9], refs[9:]
    outs, normed = rest[:4], rest[4]
    count = pieces[0].shape[0]
    scale = gain[...].reshape(1, gain.shape[0])
    for k, piece in enumerate(pieces):
        floats = piece[...].astype(jnp.float32)
        mean_sq = jnp.mean(floats * floats, axis=-1, keepdims=True)
        normed[k * count : (k + 1) * count, :] = floats * lax.rsqrt(mean_sq + EPSILON) * scale
    rows = normed[...].astype(jnp.bfloat16)
    at = 0
    for weight in weights:
        result = dot_nn(rows, weight[...])
        width = weight.shape[1]
        for i, out in enumerate(outs):
            out[:, at : at + width] = result[count * i : count * (i + 1)].astype(jnp.bfloat16)
        at += width


def attend_kernel(ways, accept, *refs):
    me, lens = refs[0][0], refs[1][0]
    arrived = refs[2:6]
    cos, sin, bias, pick, keys, values = refs[6:12]
    outs, rest = refs[12 : 12 + len(ways)], list(refs[12 + len(ways) :])
    accepted_out, fresh_rows = (rest.pop(0), rest.pop()) if accept else (None, None)
    blocks, queries, new_keys, new_values, held = rest
    draft = cos.shape[0]
    lanes = 2 * HEAD_DIM
    columns = blocks.shape[2]
    for i in range(4):
        blocks[me ^ (2 * i)] = arrived[i][:, :columns].astype(jnp.float32)
        blocks[me ^ (2 * i + 1)] = arrived[i][:, columns:].astype(jnp.float32)
    lane = iota((draft, lanes), 1)
    low = jnp.bitwise_and(lane, HEAD_DIM - 1) < HEAD_DIM // 2
    left = lane < HEAD_DIM
    cosine, sine, mask = cos[...], sin[...], bias[...]
    slots = keys.shape[0]
    step = SCORE_STEP
    live = jnp.where(iota((1, slots), 1) < lens, 0.0, NEGATIVE)

    def rope(tile):
        half = HEAD_DIM // 2
        partner = jnp.where(low, pltpu.roll(tile, lanes - half, 1), pltpu.roll(tile, half, 1))
        return (tile * cosine + partner * sine).astype(jnp.bfloat16).astype(jnp.float32)

    new_keys[...] = jnp.zeros_like(new_keys)
    new_values[...] = jnp.zeros_like(new_values)
    q_cols = columns - lanes
    heads = q_cols // HEAD_DIM
    count = heads * draft
    both = 2 * count
    pairs = [(me // 2) ^ way for way in ways]

    def columns_of(n):
        return pl.ds(pl.multiple_of(pairs[n] * lanes, lanes), lanes)

    def fill(n):
        new_keys[n, :draft, :] = rope(blocks[pairs[n], :, q_cols:])
        new_values[n, :draft, :] = blocks[4 + pairs[n], :, q_cols:]
        for p in range(2):
            for t in range(heads // 2):
                tile = rope(blocks[2 * pairs[n] + p, :, t * lanes : (t + 1) * lanes]) * 0.125
                turned = pltpu.roll(tile, HEAD_DIM, 1)
                first, second = (tile, turned) if p == 0 else (turned, tile)
                keep = left if p == 0 else ~left
                at = n * both + p * count + 2 * t * draft
                queries[at : at + draft, :] = jnp.where(keep, first, 0.0)
                queries[at + draft : at + 2 * draft, :] = jnp.where(keep, second, 0.0)

    def asked(n):
        return queries[n * both : (n + 1) * both, :].astype(jnp.bfloat16)

    def tiles(block):
        return [block[:, i : i + lanes] for i in range(0, block.shape[1], lanes)]

    def score(n, at):
        chunk = dot_nt(asked(n), keys[at : at + step, columns_of(n)])
        chunk = chunk + live[:, at : at + step]
        held[n % 2, :, at : at + step] = chunk
        return functools.reduce(jnp.maximum, tiles(chunk))

    def tree_score(n):
        fresh = dot_nt(asked(n), new_keys[n].astype(jnp.bfloat16))
        return (fresh.reshape(2 * heads, draft, lanes) + mask[None]).reshape(fresh.shape)

    chunks = range(0, slots, step)
    for n in range(len(ways)):
        fill(n)
    fresh = tree_score(0)
    peak = functools.reduce(jnp.maximum, [fresh] + [score(0, at) for at in chunks])
    for n, out in enumerate(outs):
        top = jnp.max(peak, axis=1, keepdims=True)
        weights = jnp.exp(fresh - top)
        total = weights
        mixed = dot_nn(weights.astype(jnp.bfloat16), new_values[n].astype(jnp.bfloat16))
        more = n + 1 < len(ways)
        if more:
            fresh = peak = tree_score(n + 1)
        for at in chunks:
            if more:
                peak = jnp.maximum(peak, score(n + 1, at))
            weights = jnp.exp(held[n % 2, :, at : at + step] - top)
            total = total + functools.reduce(jnp.add, tiles(weights))
            part = dot_nn(weights.astype(jnp.bfloat16), values[at : at + step, columns_of(n)])
            mixed = mixed + part
        mixed = mixed / jnp.sum(total, axis=1, keepdims=True)
        for p in range(2):
            for t in range(heads // 2):
                at = (p * heads + 2 * t) * draft
                first, second = mixed[at : at + draft], mixed[at + draft : at + 2 * draft]
                if p == 0:
                    tile = jnp.where(left, first, pltpu.roll(second, HEAD_DIM, 1))
                else:
                    tile = jnp.where(left, pltpu.roll(first, HEAD_DIM, 1), second)
                col = p * q_cols + t * lanes
                out[:, col : col + lanes] = tile.astype(jnp.bfloat16)
    if accept:
        fresh_rows[...] = jnp.zeros_like(fresh_rows)
        for pair in range(4):
            at = pair * lanes
            fresh_rows[:draft, at : at + lanes] = rope(blocks[pair, :, q_cols:])
            fresh_rows[:draft, 4 * lanes + at : 5 * lanes + at] = blocks[4 + pair, :, q_cols:]
        rows = dot_nn(pick[...].astype(jnp.bfloat16), fresh_rows[...].astype(jnp.bfloat16))
        accepted_out[...] = rows.astype(jnp.bfloat16)


def slot_order(routes, expert):
    tokens = routes.shape[1]
    hits = jnp.max((routes[...] == expert).astype(jnp.float32), axis=0, keepdims=True)
    upper = (iota((tokens, tokens), 0) <= iota((tokens, tokens), 1)).astype(jnp.bfloat16)
    wide = jnp.broadcast_to(hits, (16, tokens)).astype(jnp.bfloat16)
    return dot_nn(wide, upper)[:1] * hits


def slot_rows(order, first, count):
    place = iota((count, order.shape[1]), 0).astype(jnp.float32) + (first + 1).astype(jnp.float32)
    return jnp.where(order == place, 1.0, 0.0)


def slots_kernel(*refs):
    me, pieces, routes, rest = refs[0][0], refs[1:5], refs[5], refs[6:]
    kept, given, table, home, named_out, rows = rest
    core, expert = me % 2, me // 2
    count, half = pieces[0].shape[0], kept.shape[0]
    for i in range(4):
        order = slot_order(routes, expert ^ i)
        for side, first in enumerate((core * half, (1 - core) * half)):
            at = (4 * side + i) * half
            table[at : at + half, :] = slot_rows(order, first, half)
        if i == 0:
            chosen = slot_rows(order, expert * 0, 2 * half).astype(jnp.bfloat16)
    home[...] = chosen
    rows[...] = jnp.zeros_like(rows)
    for i, piece in enumerate(pieces):
        at = pl.multiple_of((me ^ (2 * i)) * count, 8)
        rows[pl.ds(at, count), :] = piece[...].astype(jnp.float32)
    found = rows[...].astype(jnp.bfloat16)
    kept[...] = dot_nn(table[:half, :].astype(jnp.bfloat16), found).astype(jnp.bfloat16)
    given[...] = dot_nn(table[4 * half : 5 * half, :].astype(jnp.bfloat16), found).astype(jnp.bfloat16)
    experts, tokens = named_out.shape[1], routes.shape[1]
    named = jnp.zeros((experts, tokens), jnp.float32)
    for i in range(routes.shape[0]):
        named = jnp.maximum(
            named, (iota((experts, tokens), 0) == routes[i : i + 1, :]).astype(jnp.float32)
        )
    named_out[...] = dot_nt(chosen, named.astype(jnp.bfloat16))


def pick_kernel(*refs):
    me, pieces, (table, kept, given, rows) = refs[0][0], refs[1:5], refs[5:]
    count = pieces[0].shape[0]
    rows[...] = jnp.zeros_like(rows)
    for i, piece in enumerate(pieces):
        at = pl.multiple_of((me ^ (2 * i)) * count, 8)
        rows[pl.ds(at, count), :] = piece[...].astype(jnp.float32)
    picked = dot_nn(table[...].astype(jnp.bfloat16), rows[...].astype(jnp.bfloat16))
    half = kept.shape[0]
    kept[...] = picked[:half].astype(jnp.bfloat16)
    given[...] = picked[half:].astype(jnp.bfloat16)


def outproj_kernel(me_ref, kept, taken, w_own, w_other, own, *sends):
    core = me_ref[0] % 2
    half, width = own.shape[0], w_own.shape[1]
    picked = kept[...].astype(jnp.float32) + taken[...].astype(jnp.float32)
    low, high = picked[:, :width], picked[:, width:]
    first = jnp.where(core == 0, low, high).astype(jnp.bfloat16)
    second = jnp.where(core == 0, high, low).astype(jnp.bfloat16)
    summed = dot_nt(first, w_own[...]) + dot_nt(second, w_other[...])
    own[...] = summed[:half]
    for i, out in enumerate(sends):
        out[...] = summed[(i + 1) * half : (i + 2) * half].astype(jnp.bfloat16)


def token_kernel(*refs):
    me, pieces, (w_own, w_other, out, rows) = refs[0][0], refs[1:5], refs[5:]
    count = pieces[0].shape[0]
    core = me % 2
    for i, piece in enumerate(pieces):
        rows[i * count : (i + 1) * count, :] = piece[...].astype(jnp.float32)
    width = w_own.shape[1]
    low, high = rows[:, :width], rows[:, width:]
    first = jnp.where(core == 0, low, high).astype(jnp.bfloat16)
    second = jnp.where(core == 0, high, low).astype(jnp.bfloat16)
    out[...] = dot_nt(first, w_own[...]) + dot_nt(second, w_other[...])


def expert_kernel(me_ref, mine, theirs, gain, *refs):
    router, named_ref, w_gate, w_up, w_down, out, rows, active = refs
    me = me_ref[0]
    core, expert = me % 2, me // 2
    half = mine.shape[0]
    rows[pl.ds(pl.multiple_of(core * half, 8), half), :] = mine[...].astype(jnp.float32)
    rows[pl.ds(pl.multiple_of((1 - core) * half, 8), half), :] = theirs[...].astype(jnp.float32)
    floats = rows[...]
    mean_sq = jnp.mean(floats * floats, axis=-1, keepdims=True)
    scale = gain[...].reshape(1, gain.shape[0])
    inputs = (floats * lax.rsqrt(mean_sq + EPSILON) * scale).astype(jnp.bfloat16)
    named = named_ref[...] > 0.5
    logits = jnp.where(named, dot_nt(inputs, router[...]), NEGATIVE)
    odds = jnp.exp(logits - jnp.max(logits, axis=1, keepdims=True))
    here = named & (iota(logits.shape, 1) == expert)
    share = jnp.sum(jnp.where(here, odds, 0.0), axis=1, keepdims=True)
    share = (share / jnp.sum(odds, axis=1, keepdims=True)).astype(jnp.bfloat16).astype(jnp.float32)
    gate_val = dot_nt(inputs, w_gate[...])
    up_val = dot_nt(inputs, w_up[...])
    act = gate_val * jax.nn.sigmoid(SWIGLU_ALPHA * gate_val) * (up_val + 1.0)
    active[...] = act.astype(jnp.bfloat16)
    out[...] = (dot_nn(active[...], w_down[...]) * share).astype(jnp.bfloat16)


def combine_kernel(me_ref, mine, theirs, home, sums, hidden, own, *refs):
    sends, rows = refs[:3], refs[3]
    me = me_ref[0]
    count = hidden.shape[0]
    total = (mine[...].astype(jnp.float32) + theirs[...].astype(jnp.float32)).astype(jnp.bfloat16)
    rows[...] = dot_tn(home[...], total)

    def of(i):
        start = pl.multiple_of((me ^ (2 * i)) * count, 8)
        return rows[pl.ds(start, count), :] + sums[i * count : (i + 1) * count, :]

    own[...] = of(0) + hidden[...].astype(jnp.float32)
    for i, out in enumerate(sends):
        out[...] = of(i + 1).astype(jnp.bfloat16)


def local_paired(
    hidden,
    attn_gain,
    w_query,
    w_keyval,
    w_out,
    cache_keys,
    cache_values,
    cache_lens,
    parents,
    accepted,
    moe_gain,
    w_router,
    routes,
    w_gate,
    w_up,
    w_down,
):
    devices = lax.axis_size("tp")
    me = lax.axis_index("tp").astype(jnp.int32).reshape(1)
    bf16, f32 = jnp.bfloat16, jnp.float32

    def spread(blocks, order):
        return [blocks[0], *(swap(blocks[i], 2 * i) for i in order)]

    def swap(values, offset):
        return lax.ppermute(values, "tp", [(i, i ^ offset) for i in range(devices)])

    rows, width = hidden.shape
    tokens = routes.shape[0]
    draft = parents.shape[1]
    capacity = 2 * tokens * routes.shape[1] // w_router.shape[1]
    half = capacity // 2
    routes_t = routes.T
    router_t = w_router.T

    line = [hidden, *(swap(hidden, s) for s in (2, 6, 4))]
    lanes = 128
    parents = jnp.pad(parents, ((0, 0), (0, lanes - draft)))
    other_query, other_keyval = swap(w_query, 1), swap(w_keyval, 1)
    early = (parents, load(w_query, w_keyval))
    line, early = lax.optimization_barrier((line, early))
    line = [line[i] for i in (0, 1, 3, 2)]
    parents, (near_query, near_keyval) = early
    queries, keyvals = w_query.shape[1], w_keyval.shape[1]
    columns = queries + keyvals
    projected = run(
        project_kernel,
        [((rows, 2 * columns), bf16)] * 4,
        [
            *line,
            attn_gain,
            near(near_query),
            near(near_keyval),
            near(other_query),
            near(other_keyval),
        ],
        scalars=0,
        scratch=[pltpu.VMEM((4 * rows, width), f32)],
        limit=10 * MIB,
        flops=2 * tokens * width * columns,
        moved=width * columns * 2,
    )
    later = (line, w_out, cache_keys[0], cache_values[0], cache_lens)
    later, projected = lax.optimization_barrier((later, projected))
    line, w_pair, keys, values, lens = later
    arrived = spread(projected, (2, 1, 3))
    tree = run(
        tree_kernel,
        [((draft, lanes), f32), ((draft, lanes), f32), ((draft, lanes), f32), ((DEPTH, lanes), f32)],
        [lens, accepted, parents],
        scalars=2,
        limit=4 * MIB,
    )
    w_other = swap(w_pair, 1)
    cached = load(keys, values)
    slotted = run(
        slots_kernel,
        [
            ((half, width), bf16),
            ((half, width), bf16),
            ((8 * half, tokens), f32),
            ((capacity, tokens), bf16),
            ((capacity, w_router.shape[1]), f32),
        ],
        [me, *line, routes_t],
        scratch=[pltpu.VMEM((tokens, width), f32)],
        limit=6 * MIB,
        flops=4 * half * tokens * width,
        moved=tokens * width * 4,
    )
    shadow = (tree, cached, slotted)
    arrived, shadow = lax.optimization_barrier((arrived, shadow))
    tree, cached, (kept, given, table, home, named) = shadow
    taken = swap(given, 1)
    arrived = [arrived[i] for i in (0, 2, 1, 3)]
    slots, kv_cols = cache_keys.shape[1:]
    def attend(inputs, ways, accept):
        outs = [((rows, 2 * queries), bf16)] * len(ways)
        per_way = rows * queries * 2 // HEAD_DIM
        return run(
            functools.partial(attend_kernel, ways, accept),
            outs + [((DEPTH, 2 * kv_cols), bf16)] * accept,
            inputs,
            scalars=2,
            scratch=[
                pltpu.VMEM((devices, rows, columns), f32),
                pltpu.VMEM((len(ways) * per_way, lanes), f32),
                pltpu.VMEM((len(ways), lanes, lanes), f32),
                pltpu.VMEM((len(ways), lanes, lanes), f32),
                pltpu.VMEM((min(len(ways), 2), per_way, slots), f32),
                *([pltpu.VMEM((lanes, 2 * kv_cols), f32)] * accept),
            ],
            limit=16 * MIB,
            flops=len(ways) * rows * HEADS * slots * HEAD_DIM,
            moved=len(ways) * slots * kv_cols,
        )

    lengths = cache_lens
    inputs = [me, lengths, *arrived, *tree, near(cached[0]), near(cached[1])]
    attended = attend(inputs, (1, 2, 3), False)
    later = (w_out, w_other, me, lengths)
    later, attended, taken = lax.optimization_barrier((later, attended, taken))
    w_own, w_other, me_now, lengths = later
    inputs[:2] = [me_now, lengths]
    own, accepted_kv = attend(inputs, (0,), True)
    straight = spread([own, *attended], (2, 3, 1))
    accepted_kv = accepted_kv[None]
    near_out = load(w_own.T, w_other.T)
    straight, near_out = lax.optimization_barrier((straight, near_out))
    straight = [straight[i] for i in (0, 3, 1, 2)]
    picked = run(
        pick_kernel,
        [((4 * half, 2 * queries), bf16)] * 2,
        [me, *straight, table],
        scratch=[pltpu.VMEM((tokens, 2 * queries), f32)],
        limit=6 * MIB,
        flops=16 * half * tokens * 2 * queries,
        moved=8 * half * 2 * queries * 2,
    )
    out_flops = 2 * 4 * half * 2 * queries * width
    dispatched = run(
        outproj_kernel,
        [((half, width), f32)] + [((half, width), bf16)] * 3,
        [me, picked[0], swap(picked[1], 1), *map(near, near_out)],
        limit=10 * MIB,
        flops=out_flops,
        moved=4 * queries * width,
    )
    arrived = spread(dispatched, (2, 3, 1))[1:]
    (me_then, experts), _ = lax.optimization_barrier(
        ((me, (w_gate, w_up, w_down)), dispatched[1])
    )
    sums = run(
        token_kernel,
        [((4 * rows, width), f32)],
        [me_then, *straight, *map(near, near_out)],
        scratch=[pltpu.VMEM((4 * rows, 2 * queries), f32)],
        limit=6 * MIB,
        flops=out_flops,
        moved=4 * queries * width,
    )[0]
    near_weights = load(*experts)
    middle, arrived, sums, taken, near_weights = lax.optimization_barrier(
        (dispatched[0], arrived, sums, taken, near_weights)
    )
    arrived = [kept, taken, *arrived]
    for block in arrived:
        middle = middle + block.astype(f32)
    middle = middle.astype(bf16)
    expert_rows = run(
        expert_kernel,
        [((capacity, width), bf16)],
        [
            me,
            middle,
            swap(middle, 1),
            moe_gain,
            router_t,
            named,
            *map(near, near_weights),
        ],
        scratch=[pltpu.VMEM((capacity, width), f32), pltpu.VMEM((capacity, w_down.shape[0]), bf16)],
        limit=6 * MIB,
        flops=6 * capacity * width * w_down.shape[0],
        moved=6 * width * w_down.shape[0],
    )[0]
    combined = run(
        combine_kernel,
        [((rows, width), f32)] + [((rows, width), bf16)] * 3,
        [me, expert_rows, swap(expert_rows, 1), home, sums, hidden],
        scratch=[pltpu.VMEM((tokens, width), f32)],
        flops=2 * capacity * tokens * width,
        moved=tokens * width * 4,
    )
    layer_out, *arrived = spread(combined, (2, 3, 1))
    for block in arrived:
        layer_out = layer_out + block.astype(f32)
    return (layer_out.astype(bf16), accepted_kv)


def local(hidden, attn_gain, w_query, w_keyval, *rest):
    devices = lax.axis_size("tp")
    parents, units = rest[4], rest[11].shape[0]
    paired = (
        devices == 8
        and parents.shape[0] == 1
        and units * 2 == EXPERT_HID
        and w_query.shape[1] * devices == HEADS * HEAD_DIM
        and w_keyval.shape[1] == 2 * HEAD_DIM
    )
    return (local_paired if paired else local_general)(hidden, attn_gain, w_query, w_keyval, *rest)


def solution(mesh):
    return jax.shard_map(
        local,
        mesh=mesh,
        in_specs=(
            P(("dp", "tp"), None),
            P(),
            P(None, "tp"),
            P(None, "tp"),
            P("tp", None),
            P(("dp", "tp"), None, None),
            P(("dp", "tp"), None, None),
            P(("dp", "tp")),
            P(("dp", "tp"), None),
            P(("dp", "tp")),
            P(),
            P(),
            P("dp", None),
            P("tp", None),
            P("tp", None),
            P("tp", None),
        ),
        out_specs=(P(("dp", "tp"), None), P(("dp", "tp"), None, None)),
        check_vma=False,
    )
```
